32 devices in a mesh: dp: 4 (over y, core), tensor: 8 (over z, x).
Axes of the slice: x: 2, y: 2, z: 4, core: 2. Of those that a mesh axis runs over, the one named last changes fastest.
Arguments:
- tokens: bfloat16 [8192, 1024], P(('dp', 'tensor')), may hold values from -6 to 6
- segment_ids: int32 [4, 2048], P('dp'), may hold values from 0 to 3, never falling along the last dimension, each value on 1 to 1024 neighbouring positions
- cotangent: bfloat16 [8192, 1024], P(('dp', 'tensor')), may hold values from -6 to 6
- attn_gain: float32 [1024], replicated, may hold values from 0.5 to 1.5
- query_weight: bfloat16 [1024, 1024], P('dp', 'tensor'), may hold values from -0.1875 to 0.1875
- key_weight: bfloat16 [1024, 512], P('dp', 'tensor'), may hold values from -0.1875 to 0.1875
- value_weight: bfloat16 [1024, 512], P('dp', 'tensor'), may hold values from -0.1875 to 0.1875
- output_weight: bfloat16 [1024, 1024], P('tensor', 'dp'), may hold values from -0.75 to 0.75
- query_gain: float32 [64], replicated, may hold values from 0.5 to 1.5
- key_gain: float32 [64], replicated, may hold values from 0.5 to 1.5
- ffn_gain: float32 [1024], replicated, may hold values from 0.5 to 1.5
- gate_weight: bfloat16 [1024, 4608], P('dp', 'tensor'), may hold values from -0.1875 to 0.1875
- up_weight: bfloat16 [1024, 4608], P('dp', 'tensor'), may hold values from -0.1875 to 0.1875
- down_weight: bfloat16 [4608, 1024], P('tensor', 'dp'), may hold values from -0.09375 to 0.09375
Outputs:
- block_out: bfloat16 [8192, 1024], P(('dp', 'tensor'))
- input_grad: bfloat16 [8192, 1024], P(('dp', 'tensor'))
- attn_gain_grad: float32 [1024], replicated
- query_grad: float32 [1024, 1024], P('dp', 'tensor')
- key_grad: float32 [1024, 512], P('dp', 'tensor')
- value_grad: float32 [1024, 512], P('dp', 'tensor')
- output_grad: float32 [1024, 1024], P('tensor', 'dp')
- query_gain_grad: float32 [64], replicated
- key_gain_grad: float32 [64], replicated
- ffn_gain_grad: float32 [1024], replicated
- gate_grad: float32 [1024, 4608], P('dp', 'tensor')
- up_grad: float32 [1024, 4608], P('dp', 'tensor')
- down_grad: float32 [4608, 1024], P('tensor', 'dp')
The draws below stay inside these ranges and needn't reach their ends.
Inputs may be any that keep to these rules, and one draw needn't show every extreme that they name: `segment_ids`: in each row the numbers never fall; every run of one number covers 1 to 1024 positions, and some run covers exactly 1024.
All inputs are finite; a program needn't handle non-finite values.
Results may differ from the reference program's by a relative error of at most 0.022.
Values may be sent and summed in bfloat16 or wider, within the bound.
No kernel may reach another device: no remote copies, remote signals or barrier semaphores. Data moves between devices by JAX's collectives and lax.ppermute only.
A program may use at most 128 MiB of HBM per device.

```python
import math
import jax
import jax.numpy as jnp
import numpy as np
from jax import lax

D = 1024
HEADS = 16
KV_HEADS = 8
HEAD_DIM = 64
FF = 4608
TOKG = 2048
MAXLEN = 1024
SEGS = 4
GROUPS = 4
TOKENS = 8192


def levels(own_key, dims, shards, low, high):
    factor_of = 1.0
    for dim, parts in shards:
        heights = jax.random.uniform(jax.random.fold_in(jax.random.fold_in(own_key, 6), dim), (parts,), jnp.float32, low / len(shards), high / len(shards))
        factor_of = factor_of * jnp.repeat(jnp.exp(heights), dims[dim] // parts).reshape((-1,) + (1,) * (len(dims) - 1 - dim))
    return factor_of


def split_up(number_of, total, bound, skew):
    weights = [(1 << 20) // math.isqrt(rank ** skew) + 1 for rank in range(2, number_of + 1)]
    rest, holding = total - bound - (number_of - 1), [1] * (number_of - 1)
    while rest > 0:
        free = [i for i in range(number_of - 1) if holding[i] < bound]
        mass, left = sum([weights[i] for i in free]), rest
        for i in free:
            more = min(bound - holding[i], max(1, left * weights[i] // mass), rest)
            holding[i] = holding[i] + more
            rest = rest - more
    return np.array([bound] + holding)


def uneven_parts(key, count, total, limit, lean):
    if count == 2:
        one = jax.random.randint(key, (), max(1, total - limit), min(limit, total - 1) + 1)
        return jnp.stack([one, total - one])
    lengths = jnp.asarray(split_up(count, total, limit, lean), jnp.int32)
    couples = (count - 1) // 2
    source_of, taker = lengths[1:1 + 2 * couples:2], lengths[2:2 + 2 * couples:2]
    slack = jnp.minimum(source_of - 1, limit - taker)
    shifted = jax.random.randint(jax.random.fold_in(key, 1), (couples,), 0, 1 << 20) % (slack + 1)
    lengths = lengths.at[1:1 + 2 * couples:2].set(source_of - shifted).at[2:2 + 2 * couples:2].set(taker + shifted)
    return lengths[jax.random.permutation(jax.random.fold_in(key, 2), count)]


def normal_values(own_key, shape, scale, bound, split=(), held_as=jnp.bfloat16):
    entries = jax.random.normal(own_key, shape, jnp.float32) * scale
    if len(split) > 0:
        entries = levels(own_key, shape, split, -0.22, 0.18) * entries
    return jnp.clip(entries, min=-bound, max=bound).astype(held_as)


def setup_inputs(seed: int = 0) -> dict:
    key_list = jax.random.split(jax.random.key(seed), 15)
    return {
        "tokens": normal_values(key_list[0], (TOKENS, D), 1.0, 6.0, ((0, 32),)),
        "segment_ids": jax.vmap(lambda own: jnp.searchsorted(jnp.cumsum(uneven_parts(own, SEGS, TOKG, MAXLEN, 2)), jnp.arange(TOKG), side="right"))(jax.random.split(key_list[1], GROUPS)).reshape((GROUPS, TOKG)).astype(jnp.int32),
        "cotangent": normal_values(key_list[2], (TOKENS, D), 1.0, 6.0, ((0, 32),)),
        "attn_gain": jnp.clip(1.0 + 0.1 * jax.random.normal(key_list[3], (D,), jnp.float32), 0.5, 1.5),
        "query_weight": normal_values(key_list[4], (D, HEADS * HEAD_DIM), D ** -0.5, 0.1875, ((0, 4), (1, 8))),
        "key_weight": normal_values(key_list[5], (D, KV_HEADS * HEAD_DIM), D ** -0.5, 0.1875, ((0, 4), (1, 8))),
        "value_weight": normal_values(key_list[6], (D, KV_HEADS * HEAD_DIM), D ** -0.5, 0.1875, ((0, 4), (1, 8))),
        "output_weight": normal_values(key_list[7], (HEADS * HEAD_DIM, D), (HEADS * HEAD_DIM // 16) ** -0.5, 0.75, ((0, 8), (1, 4))),
        "query_gain": jnp.clip(1.0 + 0.1 * jax.random.normal(key_list[8], (HEAD_DIM,), jnp.float32), 0.5, 1.5),
        "key_gain": jnp.clip(1.0 + 0.1 * jax.random.normal(key_list[9], (HEAD_DIM,), jnp.float32), 0.5, 1.5),
        "ffn_gain": jnp.clip(1.0 + 0.1 * jax.random.normal(key_list[10], (D,), jnp.float32), 0.5, 1.5),
        "gate_weight": normal_values(key_list[11], (D, FF), D ** -0.5, 0.1875, ((0, 4), (1, 8))),
        "up_weight": normal_values(key_list[12], (D, FF), D ** -0.5, 0.1875, ((0, 4), (1, 8))),
        "down_weight": normal_values(key_list[13], (FF, D), FF ** -0.5, 0.09375, ((0, 8), (1, 4))),
    }


EPSILON = 1e-05
ROPE_BASE = 1000000.0
NEGATIVE = -1e+30

@jax.custom_vjp
def low(v):
    return lax.optimization_barrier(v.astype(jnp.bfloat16)).astype(jnp.float32)

@jax.custom_vjp
def low_back(v):
    return v

def low_keep(v):
    return (low(v), None)

def low_pass(kept, grad):
    return (grad,)

def back_keep(v):
    return (v, None)

def back_low(kept, grad):
    return (low(grad),)
low.defvjp(low_keep, low_pass)
low_back.defvjp(back_keep, back_low)

def product(a, b):
    return jnp.dot(a, b, precision=lax.Precision.HIGHEST, preferred_element_type=jnp.float32)

def norm_rows(v, scales):
    factor = lax.rsqrt(lax.optimization_barrier(jnp.mean(v * v, axis=-1, keepdims=True)) + EPSILON)
    return v * factor * scales

def rotate(v, cosine, sine):
    half_dim = v.shape[-1] // 2
    first = v[..., :half_dim]
    second = v[..., half_dim:]
    return jnp.concatenate([first * cosine - second * sine, second * cosine + first * sine], axis=-1)

def positions(segment):
    index = jnp.arange(segment.shape[0], dtype=jnp.int32)
    first = jnp.concatenate([jnp.ones((1,), dtype=jnp.bool_), segment[1:] != segment[:-1]])
    start = lax.cummax(jnp.where(first, index, jnp.zeros_like(index)), axis=0)
    return index - start

def rope_tables(segment, head_dim):
    half_dim = head_dim // 2
    inverse = ROPE_BASE ** (-(jnp.arange(half_dim, dtype=jnp.float32) * 2.0) / head_dim)
    angles = positions(segment).astype(jnp.float32)[:, None] * inverse[None, :]
    return (jnp.cos(angles)[:, None, :], jnp.sin(angles)[:, None, :])

def attend(q_rot, k_rot, v_low, segment):
    total_rows = segment.shape[0]
    block_rows = min(512, total_rows)
    key_index = jnp.arange(total_rows, dtype=jnp.int32)
    score_scale = 1.0 / math.sqrt(q_rot.shape[-1])

    def one_block(start):
        q_block = lax.dynamic_slice_in_dim(q_rot, start, block_rows, 0)
        s_block = lax.dynamic_slice_in_dim(segment, start, block_rows, 0)
        row_index = start + jnp.arange(block_rows, dtype=jnp.int32)
        raw_scores = low_back(jnp.einsum('qcgd,kcd->cgqk', q_block, k_rot, precision=lax.Precision.HIGHEST) * score_scale)
        allowed = (s_block[:, None] == segment[None, :]) & (key_index[None, :] <= row_index[:, None])
        masked = jnp.where(allowed, raw_scores, NEGATIVE)
        row_max = lax.optimization_barrier(jnp.max(masked, axis=-1, keepdims=True))
        exponent = jnp.exp(masked - row_max)
        attn_probs = exponent / lax.optimization_barrier(jnp.sum(exponent, axis=-1, keepdims=True))
        return jnp.einsum('cgqk,kcd->qcgd', low(attn_probs), v_low, precision=lax.Precision.HIGHEST)
    starts = jnp.arange(0, total_rows, block_rows, dtype=jnp.int32)
    context = lax.map(jax.checkpoint(one_block), starts)
    return context.reshape(total_rows, -1)

def forward(x, attn_gain, query_weight, key_weight, value_weight, output_weight, query_gain, key_gain, ffn_gain, gate_weight, up_weight, down_weight, segment, cosine, sine):
    total_rows = x.shape[0]
    head_dim = query_gain.shape[0]
    xn_attn = low(norm_rows(x, attn_gain))
    query_proj = low_back(product(xn_attn, query_weight)).reshape(total_rows, -1, head_dim)
    key_proj = low_back(product(xn_attn, key_weight)).reshape(total_rows, -1, head_dim)
    value_proj = low_back(product(xn_attn, value_weight)).reshape(total_rows, -1, head_dim)
    kv_count = key_proj.shape[1]
    q_rot = low(rotate(norm_rows(query_proj, query_gain), cosine, sine)).reshape(total_rows, kv_count, -1, head_dim)
    k_rot = low(rotate(norm_rows(key_proj, key_gain), cosine, sine))
    context = low(low_back(attend(q_rot, k_rot, low(value_proj), segment)))
    hidden_state = x + low_back(product(context, output_weight))
    xn_ffn = low(norm_rows(hidden_state, ffn_gain))
    gate_pre = low_back(product(xn_ffn, gate_weight))
    up_pre = low_back(product(xn_ffn, up_weight))
    activation = low(low_back(jax.nn.silu(gate_pre) * up_pre))
    return hidden_state + low_back(product(activation, down_weight))

def reference(tokens, segment_ids, cotangent, attn_gain, query_weight, key_weight, value_weight, output_weight, query_gain, key_gain, ffn_gain, gate_weight, up_weight, down_weight):
    params = tuple((p.astype(jnp.float32) for p in (attn_gain, query_weight, key_weight, value_weight, output_weight, query_gain, key_gain, ffn_gain, gate_weight, up_weight, down_weight)))
    groups = segment_ids.shape[0]
    total_rows = segment_ids.shape[1]
    head_dim = query_gain.shape[0]
    inputs = tokens.astype(jnp.float32).reshape(groups, total_rows, -1)
    grads_in = cotangent.astype(jnp.float32).reshape(groups, total_rows, -1)

    def group_step(totals, operands):
        x_group, dy_group, segment = operands
        cosine, sine = rope_tables(segment, head_dim)

        def closure(x, *weights):
            return forward(x, *weights, segment, cosine, sine)
        result, pull_back = jax.vjp(closure, x_group, *params)
        grads = pull_back(dy_group)
        totals = tuple((a + b for a, b in zip(totals, grads[1:])))
        return (totals, (result.astype(jnp.bfloat16), grads[0].astype(jnp.bfloat16)))
    zero_grads = tuple((jnp.zeros_like(p) for p in params))
    totals, (outputs, input_grads) = lax.scan(group_step, zero_grads, (inputs, grads_in, segment_ids))
    all_rows = groups * total_rows
    return (outputs.reshape(all_rows, -1), input_grads.reshape(all_rows, -1), totals[0], totals[1], totals[2], totals[3], totals[4], totals[5], totals[6], totals[7], totals[8], totals[9], totals[10])
```

```python
import functools

import jax
import jax.numpy as jnp
from jax import lax
from jax.experimental import pallas as pl
from jax.experimental.pallas import tpu as pltpu
from jax.sharding import Mesh
from jax.sharding import PartitionSpec as P

EPSILON = 1e-05
ROPE_BASE = 1000000.0
BLOCK = 256
F32 = jnp.float32
BF16 = jnp.bfloat16
VMEM_LIMIT = 40 * 1024 * 1024


def nn(a, b):
    return lax.dot_general(a, b, (((1,), (0,)), ((), ())), preferred_element_type=F32)


def nt(a, b):
    return lax.dot_general(a, b, (((1,), (1,)), ((), ())), preferred_element_type=F32)


def tn(a, b):
    return lax.dot_general(a, b, (((0,), (0,)), ((), ())), preferred_element_type=F32)


def exact_nn(a, b):
    return lax.dot_general(
        a, b, (((1,), (0,)), ((), ())), preferred_element_type=F32, precision=lax.Precision.HIGHEST
    )


def params(**more):
    return pltpu.CompilerParams(vmem_limit_bytes=VMEM_LIMIT, **more)


def swap(v, axes, bit):
    size = lax.axis_size(axes)
    return lax.ppermute(v, axes, [(i, i ^ bit) for i in range(size)])


def line_gather(v, axis):
    size = lax.axis_size(axis)
    me = lax.axis_index(axis)
    from_left, from_right = [], []
    left = right = v
    for step in range(1, size):
        left = lax.ppermute(left, axis, [(i, i + 1) for i in range(step - 1, size - 1)])
        right = lax.ppermute(right, axis, [(i, i - 1) for i in range(1, size - step + 1)])
        from_left.append(left)
        from_right.append(right)
    slots = [v]
    for d in range(1, size):
        slots.append(jnp.where(me + d < size, from_right[d - 1], from_left[size - d - 1]))
    return slots


def line_scatter(parts, axis):
    size = lax.axis_size(axis)
    left = right = None
    for m in range(size - 1, 0, -1):
        up, down = parts[m].astype(F32), parts[size - m].astype(F32)
        if left is not None:
            up, down = up + left.astype(F32), down + right.astype(F32)
        left = lax.ppermute(up.astype(BF16), axis, [(i, i + 1) for i in range(size - m)])
        right = lax.ppermute(down.astype(BF16), axis, [(i, i - 1) for i in range(m, size)])
    return parts[0].astype(F32) + left.astype(F32) + right.astype(F32)


def quads(v):
    return jnp.split(v, 4, axis=-1)


def flip_y(v):
    a, b = jnp.split(v, 2, axis=-1)
    return jnp.concatenate([b, a], axis=-1)


def own_order(v, y, c):
    runs = lax.axis_size("r")
    if runs > 1:
        lead = v.shape[:-1]
        v = jnp.moveaxis(v.reshape(lead + (runs, 4, -1)), -3, -2).reshape(lead + (-1,))
    return exchange(v, y, c)


def exchange(v, y, c):
    a = quads(v)
    a = [jnp.where(c == 0, a[e], a[e ^ 1]) for e in range(4)]
    return jnp.concatenate([jnp.where(y == 0, a[e], a[e ^ 2]) for e in range(4)], axis=-1)


def arrays_order(v, y, c):
    v = exchange(v, y, c)
    runs = lax.axis_size("r")
    if runs > 1:
        lead = v.shape[:-1]
        v = jnp.moveaxis(v.reshape(lead + (4, runs, -1)), -2, -3).reshape(lead + (-1,))
    return v


def gather_runs(v):
    return lax.all_gather(v, "r", axis=v.ndim - 1, tiled=True) if lax.axis_size("r") > 1 else v


def scatter_runs(v):
    if lax.axis_size("r") == 1:
        return v
    return lax.psum_scatter(
        v.astype(BF16), "r", scatter_dimension=v.ndim - 1, tiled=True
    ).astype(F32)


def total_of(v):
    if lax.axis_size("r") > 1:
        v = lax.psum(v, "r")
    for axis in ("c", "x", "y", "z"):
        bit = 1
        while bit < lax.axis_size(axis):
            v = v + swap(v, axis, bit)
            bit *= 2
    return v


def gather_heads(w):
    slots = jnp.stack(line_gather(w, "z"))
    near = [slots] + [swap(slots, ("y", "x"), bit) for bit in (1, 2, 3)]
    far = [swap(v, "c", 1) for v in near]
    rows = [
        jnp.concatenate([near[ex], far[ex], near[ex + 2], far[ex + 2]], axis=-1) for ex in (0, 1)
    ]
    return jnp.concatenate(rows, axis=0)


def scatter_heads(g):
    e0, e1, e2, e3 = quads(g)
    from_core = swap(jnp.concatenate([e1, e3], axis=-1), "c", 1)
    both = (jnp.concatenate([e0, e2], axis=-1).astype(F32) + from_core.astype(F32)).astype(BF16)
    half, cols = g.shape[0] // 2, both.shape[-1] // 2
    mine = both[:half, :, :cols].astype(F32)
    mine = mine + swap(both[half:, :, :cols], ("y", "x"), 1).astype(F32)
    mine = mine + swap(both[:half, :, cols:], ("y", "x"), 2).astype(F32)
    mine = mine + swap(both[half:, :, cols:], ("y", "x"), 3).astype(F32)
    return line_scatter([mine[d] for d in range(half)], "z")


def gather_tokens(v):
    around = [swap(v, ("y", "x"), bit) for bit in (1, 2, 3)]
    return jnp.concatenate([v, around[0], flip_y(around[1]), flip_y(around[2])], axis=0)


def scatter_tokens(parts):
    near = swap(parts[1], ("y", "x"), 1).astype(F32) + parts[0]
    far = swap(parts[2], ("y", "x"), 2).astype(F32) + swap(parts[3], ("y", "x"), 3).astype(F32)
    return near + flip_y(far)


def lanes_of(shape):
    return lax.broadcasted_iota(jnp.int32, shape, len(shape) - 1)


def head_sums(v, head):
    width = v.shape[-1]
    row = lax.broadcasted_iota(jnp.int32, (width, width), 0) // head
    col = lax.broadcasted_iota(jnp.int32, (width, width), 1) // head
    return exact_nn(v, jnp.where(row == col, 1.0, 0.0).astype(F32))


def swap_halves(v, head):
    width, half = v.shape[-1], head // 2
    low = (lanes_of(v.shape) % head) < half
    return jnp.where(low, pltpu.roll(v, width - half, 1), pltpu.roll(v, half, 1))


def qkv_kernel(head, order, xa, w, cosine, sine, q_gain, k_gain, low, kept):
    del order
    proj = nt(xa[...], w[0])
    width = 2 * head
    kept[0] = proj

    def prep(v, gain):
        factor = lax.rsqrt(head_sums(v * v, head) * (1.0 / head) + EPSILON)
        n = v * factor * gain
        return n * cosine[...] + swap_halves(n, head) * sine[...]

    q = prep(proj[:, :width], q_gain[...])
    kv = proj[:, width:]
    k = prep(kv, k_gain[...])
    low[0, :, :width] = q.astype(BF16)
    low[0, :, width:] = jnp.where(lanes_of(kv.shape) < head, k, kv).astype(BF16)


def qkv_call(order, xa, w, cosine, sine, q_gain, k_gain, head):
    blocks, n, d = w.shape
    rows = xa.shape[0]
    whole = lambda shape: pl.BlockSpec(shape, lambda j, order: (0,) * len(shape))
    return pl.pallas_call(
        functools.partial(qkv_kernel, head),
        grid_spec=pltpu.PrefetchScalarGridSpec(
            num_scalar_prefetch=1,
            grid=(blocks,),
            in_specs=[
                whole((rows, d)),
                pl.BlockSpec((1, n, d), lambda j, order: (order[j], 0, 0)),
                whole((rows, 2 * head)),
                whole((rows, 2 * head)),
                whole((1, 2 * head)),
                whole((1, 2 * head)),
            ],
            out_specs=[
                pl.BlockSpec((1, rows, n), lambda j, order: (j, 0, 0)),
                pl.BlockSpec((1, rows, n), lambda j, order: (j, 0, 0)),
            ],
        ),
        out_shape=[
            jax.ShapeDtypeStruct((blocks, rows, n), BF16),
            jax.ShapeDtypeStruct((blocks, rows, n), F32),
        ],
        compiler_params=params(),
        cost_estimate=pl.CostEstimate(
            flops=2 * blocks * rows * n * d, bytes_accessed=2 * blocks * n * d, transcendentals=0
        ),
        name="qkv",
    )(order, xa, w, cosine, sine, q_gain, k_gain)


def stack_heads(v, head, scale=None):
    out = jnp.concatenate([v[:, :head], v[:, head : 2 * head]], axis=0)
    return out if scale is None else (out.astype(F32) * scale).astype(BF16)


def unstack(v_t):
    rows = v_t.shape[1] // 2
    return jnp.concatenate([v_t[:, :rows], v_t[:, rows:]], axis=0).T


def attend_kernel(head, first, qkv, start, context, log_total, turned):
    b = pl.program_id(0)
    width = 2 * head

    @pl.when(b == 0)
    def _():
        kv_t = qkv[:, width:].astype(F32).T
        row = lax.broadcasted_iota(jnp.int32, kv_t.shape, 0)
        turned[...] = jnp.where(row < head, 1.0, kv_t).astype(BF16)

    q2 = stack_heads(qkv[pl.ds(b * BLOCK, BLOCK), :width], head, head**-0.5)
    begin = start[0]
    key = lax.broadcasted_iota(jnp.int32, (BLOCK, 2 * BLOCK), 0)

    def block(j, acc, diagonal):
        s = nt(qkv[pl.ds(j * BLOCK, BLOCK), width : width + head], q2)
        allowed = key >= begin - j * BLOCK
        if diagonal:
            row = lanes_of((BLOCK, 2 * BLOCK)) % BLOCK
            allowed = allowed & (key <= row)
        p = jnp.where(allowed, jnp.exp(s), 0.0)
        return acc + nn(turned[:, pl.ds(j * BLOCK, BLOCK)], p.astype(BF16))

    acc = jnp.zeros((width, 2 * BLOCK), F32)
    acc = lax.fori_loop(first[b], b, lambda j, acc: block(j, acc, False), acc)
    acc = block(b, acc, True)
    total = acc[:1]
    context[...] = unstack(acc[head:] / total).astype(BF16)
    log_total[0] = jnp.log(total)


def attend_call(first, qkv, start, head):
    rows, n = qkv.shape
    blocks = rows // BLOCK
    return pl.pallas_call(
        functools.partial(attend_kernel, head),
        grid_spec=pltpu.PrefetchScalarGridSpec(
            num_scalar_prefetch=1,
            grid=(blocks,),
            in_specs=[
                pl.BlockSpec((rows, n), lambda b, first: (0, 0)),
                pl.BlockSpec((1, 1, 2 * BLOCK), lambda b, first: (b, 0, 0)),
            ],
            out_specs=[
                pl.BlockSpec((BLOCK, 2 * head), lambda b, first: (b, 0)),
                pl.BlockSpec((1, 1, 2 * BLOCK), lambda b, first: (b, 0, 0)),
            ],
            scratch_shapes=[pltpu.VMEM((2 * head, rows), BF16)],
        ),
        out_shape=[
            jax.ShapeDtypeStruct((rows, 2 * head), BF16),
            jax.ShapeDtypeStruct((blocks, 1, 2 * BLOCK), F32),
        ],
        compiler_params=params(),
        cost_estimate=pl.CostEstimate(
            flops=8 * rows * rows * head, bytes_accessed=3 * rows * n, transcendentals=rows * rows
        ),
        name="attend",
    )(first, qkv, start)


def attend_back_kernel(
    head, first, qkv, context, d_context, start, log_total, out, turned, d_key, d_value
):
    b = pl.program_id(0)
    width = 2 * head

    @pl.when(b == 0)
    def _():
        turned[...] = qkv[:, width:].astype(F32).T.astype(BF16)
        d_key[...] = jnp.zeros_like(d_key)
        d_value[...] = jnp.zeros_like(d_value)

    scale = head**-0.5
    q2 = stack_heads(qkv[pl.ds(b * BLOCK, BLOCK), :width], head, scale)
    g = d_context[...]
    g2 = stack_heads(g, head)
    begin = start[0]
    log_sum = log_total[0]
    picks = jnp.where(
        lanes_of((8, width)) // head == lax.broadcasted_iota(jnp.int32, (8, width), 0), 1.0, 0.0
    ).astype(F32)
    delta = lax.dot_general(
        picks,
        g.astype(F32) * context[...].astype(F32),
        (((1,), (1,)), ((), ())),
        preferred_element_type=F32,
        precision=lax.Precision.HIGHEST,
    )
    delta = jnp.concatenate([delta[0:1], delta[1:2]], axis=1)
    key = lax.broadcasted_iota(jnp.int32, (BLOCK, 2 * BLOCK), 0)

    def block(j, acc, diagonal):
        at = pl.ds(j * BLOCK, BLOCK)
        s = nt(qkv[at, width : width + head], q2)
        allowed = key >= begin - j * BLOCK
        if diagonal:
            row = lanes_of((BLOCK, 2 * BLOCK)) % BLOCK
            allowed = allowed & (key <= row)
        p = jnp.where(allowed, jnp.exp(s - log_sum), 0.0)
        d_p = nt(qkv[at, width + head :], g2)
        d_s = (p * (d_p - delta)).astype(BF16)
        d_value[at, :] += nn(p.astype(BF16), g2)
        d_key[at, :] += nn(d_s, q2)
        return acc + nn(turned[:, at], d_s)

    acc = jnp.zeros((width, 2 * BLOCK), F32)
    acc = lax.fori_loop(first[b], b, lambda j, acc: block(j, acc, False), acc)
    acc = block(b, acc, True)
    out[pl.ds(b * BLOCK, BLOCK), :width] = (unstack(acc[:head]) * scale).astype(BF16)

    @pl.when(b == pl.num_programs(0) - 1)
    def _():
        out[:, width:] = jnp.concatenate([d_key[...], d_value[...]], axis=1).astype(BF16)


def attend_back_call(first, qkv, context, d_context, start, log_total, head):
    rows, n = qkv.shape
    blocks = rows // BLOCK
    per_block = pl.BlockSpec((BLOCK, 2 * head), lambda b, first: (b, 0))
    per_row = pl.BlockSpec((1, 1, 2 * BLOCK), lambda b, first: (b, 0, 0))
    return pl.pallas_call(
        functools.partial(attend_back_kernel, head),
        grid_spec=pltpu.PrefetchScalarGridSpec(
            num_scalar_prefetch=1,
            grid=(blocks,),
            in_specs=[
                pl.BlockSpec((rows, n), lambda b, first: (0, 0)),
                per_block,
                per_block,
                per_row,
                per_row,
            ],
            out_specs=pl.BlockSpec((rows, n), lambda b, first: (0, 0)),
            scratch_shapes=[
                pltpu.VMEM((2 * head, rows), BF16),
                pltpu.VMEM((rows, head), F32),
                pltpu.VMEM((rows, head), F32),
            ],
        ),
        out_shape=jax.ShapeDtypeStruct((rows, n), BF16),
        compiler_params=params(),
        cost_estimate=pl.CostEstimate(
            flops=20 * rows * rows * head, bytes_accessed=6 * rows * n, transcendentals=rows * rows
        ),
        name="attend_back",
    )(first, qkv, context, d_context, start, log_total)


def project_kernel(order, context, w, x, gain, hidden, normed):
    del order
    j = pl.program_id(0)

    @pl.when(j == 0)
    def _():
        hidden[...] = x[...]

    hidden[...] += nn(context[0], w[0])

    @pl.when(j == pl.num_programs(0) - 1)
    def _():
        h = hidden[...]
        factor = lax.rsqrt(jnp.mean(h * h, axis=-1, keepdims=True) + EPSILON)
        normed[...] = (h * factor * gain[...]).astype(BF16)


def project_call(order, context, w, x, gain):
    blocks, n, d = w.shape
    rows = x.shape[0]
    whole = lambda shape: pl.BlockSpec(shape, lambda j, order: (0,) * len(shape))
    return pl.pallas_call(
        project_kernel,
        grid_spec=pltpu.PrefetchScalarGridSpec(
            num_scalar_prefetch=1,
            grid=(blocks,),
            in_specs=[
                pl.BlockSpec((1, rows, n), lambda j, order: (j, 0, 0)),
                pl.BlockSpec((1, n, d), lambda j, order: (order[j], 0, 0)),
                whole((rows, d)),
                whole((1, d)),
            ],
            out_specs=[whole((rows, d)), whole((rows, d))],
        ),
        out_shape=[jax.ShapeDtypeStruct((rows, d), F32), jax.ShapeDtypeStruct((rows, d), BF16)],
        compiler_params=params(),
        cost_estimate=pl.CostEstimate(
            flops=2 * blocks * rows * n * d, bytes_accessed=2 * blocks * n * d, transcendentals=0
        ),
        name="project",
    )(order, context, w, x, gain)


def project_back_kernel(order, context, w, d_hidden, d_context, grad):
    del order
    low = d_hidden[...]
    d_context[0] = nt(low, w[0]).astype(BF16)
    grad[0] = tn(context[0], low).astype(BF16)


def project_back_call(order, context, w, d_hidden):
    blocks, n, d = w.shape
    rows = d_hidden.shape[0]
    by_block = pl.BlockSpec((1, rows, n), lambda j, order: (j, 0, 0))
    by_order = pl.BlockSpec((1, n, d), lambda j, order: (order[j], 0, 0))
    return pl.pallas_call(
        project_back_kernel,
        grid_spec=pltpu.PrefetchScalarGridSpec(
            num_scalar_prefetch=1,
            grid=(blocks,),
            in_specs=[by_block, by_order, pl.BlockSpec((rows, d), lambda j, order: (0, 0))],
            out_specs=[by_block, by_order],
        ),
        out_shape=[
            jax.ShapeDtypeStruct((blocks, rows, n), BF16),
            jax.ShapeDtypeStruct((blocks, n, d), BF16),
        ],
        compiler_params=params(),
        cost_estimate=pl.CostEstimate(
            flops=4 * blocks * rows * n * d, bytes_accessed=4 * blocks * n * d, transcendentals=0
        ),
        name="project_back",
    )(order, context, w, d_hidden)


def qkv_back_kernel(
    head, order, grads, kept, xa, w, cosine, sine, q_gain, k_gain, d_xa, d_w, q_part, k_part
):
    del order
    j = pl.program_id(0)
    width = 2 * head

    @pl.when(j == 0)
    def _():
        d_xa[...] = jnp.zeros_like(d_xa)
        q_part[...] = jnp.zeros_like(q_part)
        k_part[...] = jnp.zeros_like(k_part)

    def back(g, v, gain):
        e = g * cosine[...] - swap_halves(g, head) * sine[...]
        m = lax.rsqrt(head_sums(v * v, head) * (1.0 / head) + EPSILON)
        u = gain * e
        mean = head_sums(u * v, head) * (1.0 / head)
        return m * u - v * (m * m * m * mean), jnp.sum(e * v * m, axis=0, keepdims=True)

    g, v = grads[0].astype(F32), kept[0]
    d_q, part = back(g[:, :width], v[:, :width], q_gain[...])
    q_part[...] += part
    d_k, part = back(g[:, width:], v[:, width:], k_gain[...])
    k_part[...] += part
    d_kv = jnp.where(lanes_of(d_k.shape) < head, d_k, g[:, width:])
    low = jnp.concatenate([d_q, d_kv], axis=1).astype(BF16)
    d_xa[...] += nn(low, w[0])
    d_w[0] = tn(low, xa[...]).astype(BF16)


def qkv_back_call(order, grads, kept, xa, w, cosine, sine, q_gain, k_gain, head):
    blocks, n, d = w.shape
    rows = xa.shape[0]
    whole = lambda shape: pl.BlockSpec(shape, lambda j, order: (0,) * len(shape))
    by_block = pl.BlockSpec((1, rows, n), lambda j, order: (j, 0, 0))
    by_order = pl.BlockSpec((1, n, d), lambda j, order: (order[j], 0, 0))
    lane = (1, 2 * head)
    return pl.pallas_call(
        functools.partial(qkv_back_kernel, head),
        grid_spec=pltpu.PrefetchScalarGridSpec(
            num_scalar_prefetch=1,
            grid=(blocks,),
            in_specs=[
                by_block,
                by_block,
                whole((rows, d)),
                by_order,
                whole((rows, 2 * head)),
                whole((rows, 2 * head)),
                whole(lane),
                whole(lane),
            ],
            out_specs=[whole((rows, d)), by_order, whole(lane), whole(lane)],
        ),
        out_shape=[
            jax.ShapeDtypeStruct((rows, d), F32),
            jax.ShapeDtypeStruct((blocks, n, d), BF16),
            jax.ShapeDtypeStruct(lane, F32),
            jax.ShapeDtypeStruct(lane, F32),
        ],
        compiler_params=params(),
        cost_estimate=pl.CostEstimate(
            flops=4 * blocks * rows * n * d, bytes_accessed=4 * blocks * n * d, transcendentals=0
        ),
        name="qkv_back",
    )(order, grads, kept, xa, w, cosine, sine, q_gain, k_gain)


def norm_factor(v):
    return lax.rsqrt(jnp.mean(v * v, axis=-1, keepdims=True) + EPSILON)


def norm_back(v, factor, gain, grad):
    u = gain * grad
    part = jnp.sum(grad * v * factor, axis=0)
    mean = jnp.mean(u * v, axis=-1, keepdims=True)
    return factor * u - v * (factor * factor * factor * mean), part


def per_device(
    tokens,
    segment_ids,
    cotangent,
    attn_gain,
    query_weight,
    key_weight,
    value_weight,
    output_weight,
    query_gain,
    key_gain,
    ffn_gain,
    gate_weight,
    up_weight,
    down_weight,
):
    y, c = lax.axis_index("y"), lax.axis_index("c")
    z, x_at = lax.axis_index("z"), lax.axis_index("x")
    z_size = lax.axis_size("z")
    head = query_gain.shape[0]
    rows = tokens.shape[0]
    nq, nk = query_weight.shape[1], key_weight.shape[1]

    qkv_w = gather_heads(
        gather_runs(jnp.concatenate([query_weight.T, key_weight.T, value_weight.T], axis=0))
    )
    out_w = gather_heads(gather_runs(output_weight))
    ffn = gather_runs(jnp.stack([gate_weight.T, up_weight.T, down_weight]))
    units = ffn.shape[1] // 2
    keep = jnp.where(y == 0, ffn[:, :units], ffn[:, units:])
    give = jnp.where(y == 0, ffn[:, units:], ffn[:, :units])
    ffn = jnp.concatenate([keep, swap(give, "y", 1)], axis=-1)
    near = jnp.concatenate(line_gather(ffn, "z"), axis=1)
    far = swap(near, "c", 1)
    a, b = jnp.split(near, 2, axis=-1)
    a_far, b_far = jnp.split(far, 2, axis=-1)
    ffn_w = jnp.concatenate([a, a_far, b, b_far], axis=-1)
    gate_w, up_w, down_w = ffn_w[0], ffn_w[1], ffn_w[2]

    segment = segment_ids[0]
    total_rows = segment.shape[0]
    index = jnp.arange(total_rows, dtype=jnp.int32)
    opens = jnp.concatenate([jnp.ones((1,), dtype=jnp.bool_), segment[1:] != segment[:-1]])
    begin = lax.cummax(jnp.where(opens, index, 0), axis=0)
    blocks = total_rows // BLOCK
    first = begin[::BLOCK] // BLOCK
    by_block = begin.reshape(blocks, 1, BLOCK)
    start = jnp.concatenate([by_block, by_block], axis=2)
    here = lax.axis_index(("z", "x")) * rows
    position = lax.dynamic_slice_in_dim(index - begin, here, rows).astype(F32)
    inverse = ROPE_BASE ** (-(jnp.arange(head // 2, dtype=F32) * 2.0) / head)
    angle = position[:, None] * inverse[None, :]
    cos_half, sin_half = jnp.cos(angle), jnp.sin(angle)
    cosine = jnp.concatenate([cos_half] * 4, axis=1)
    sine = jnp.concatenate([-sin_half, sin_half] * 2, axis=1)
    slots = jnp.arange(z_size, dtype=jnp.int32)
    order = jnp.stack([(slots - z) % z_size + z_size * x_at, (slots - z) % z_size + z_size * (1 - x_at)], axis=1)
    order = order.reshape(-1).astype(jnp.int32)

    x = own_order(tokens, y, c).astype(F32)
    grad_low = own_order(cotangent, y, c)
    grad_out = grad_low.astype(F32)
    gain_a = own_order(attn_gain[None], y, c)
    gain_f = own_order(ffn_gain[None], y, c)
    gain_q = jnp.concatenate([query_gain, query_gain])[None]
    gain_k = jnp.concatenate([key_gain, key_gain])[None]

    x_factor = norm_factor(x)
    xa = (x * x_factor * gain_a).astype(BF16)
    low, kept = qkv_call(order, xa, qkv_w, cosine, sine, gain_q, gain_k, head)

    def to_heads(v):
        return lax.all_to_all(v, ("z", "x"), 0, 0, tiled=True)

    qkv = to_heads(low).reshape(total_rows, nq + 2 * nk)
    context, log_total = attend_call(first, qkv, start, head)
    context_rows = to_heads(context.reshape(-1, rows, nq))
    hidden, xf = project_call(order, context_rows, out_w, x, gain_f)

    xf_all = gather_tokens(xf)
    dy_all = gather_tokens(grad_low)
    gate_pre = nt(xf_all, gate_w)
    up_pre = nt(xf_all, up_w)
    gate_sig = jax.nn.sigmoid(gate_pre)
    silu = gate_pre * gate_sig
    activation = (silu * up_pre).astype(BF16)
    d_act = nt(dy_all, down_w).astype(BF16).astype(F32)
    d_gate = (d_act * up_pre * (gate_sig * (1.0 + gate_pre * (1.0 - gate_sig)))).astype(BF16)
    d_up = (d_act * silu).astype(BF16)

    def rows_of(v, e):
        return v[e * rows : (e + 1) * rows]

    d_xf_parts = [
        nn(rows_of(d_gate, e), gate_w) + nn(rows_of(d_up, e), up_w) for e in range(4)
    ]
    d_xf = scatter_tokens([d_xf_parts[0]] + [v.astype(BF16) for v in d_xf_parts[1:]])
    ffn_parts = [nn(rows_of(activation, e), down_w) for e in range(4)]
    ffn_out = scatter_tokens([ffn_parts[0]] + [v.astype(BF16) for v in ffn_parts[1:]])
    block_out = arrays_order((hidden + ffn_out).astype(BF16), y, c)

    h_back, ffn_gain_part = norm_back(hidden, norm_factor(hidden), gain_f, d_xf)
    d_hidden = grad_out + h_back
    d_context_rows, out_grad = project_back_call(
        order, context_rows, out_w, d_hidden.astype(BF16)
    )
    d_context = to_heads(d_context_rows).reshape(total_rows, nq)
    d_qkv = attend_back_call(first, qkv, context, d_context, start, log_total, head)
    d_qkv_rows = to_heads(d_qkv.reshape(-1, rows, nq + 2 * nk))
    d_xa, qkv_grad, q_part, k_part = qkv_back_call(
        order, d_qkv_rows, kept, xa, qkv_w, cosine, sine, gain_q, gain_k, head
    )
    x_back, attn_gain_part = norm_back(x, x_factor, gain_a, d_xa)
    input_grad = arrays_order((d_hidden + x_back).astype(BF16), y, c)

    ffn_grad = jnp.stack([tn(d_gate, xf_all), tn(d_up, xf_all), tn(activation, dy_all)])
    e0, e1, e2, e3 = quads(ffn_grad.astype(BF16))
    from_core = swap(jnp.concatenate([e1, e3], axis=-1), "c", 1)
    both = jnp.concatenate([e0, e2], axis=-1).astype(F32) + from_core.astype(F32)
    both = both.astype(BF16)
    mine = line_scatter(
        [both[:, d * units : (d + 1) * units] for d in range(z_size)], "z"
    )
    own, other = jnp.split(mine, 2, axis=-1)
    other = swap(other.astype(BF16), "y", 1).astype(F32)
    ffn_grad = jnp.concatenate(
        [jnp.where(y == 0, own, other), jnp.where(y == 0, other, own)], axis=1
    )
    ffn_grad = scatter_runs(ffn_grad)
    out_grad = scatter_runs(scatter_heads(out_grad))
    qkv_grad = scatter_runs(scatter_heads(qkv_grad))

    d = x.shape[1]
    gains = total_of(
        jnp.concatenate(
            [
                arrays_order(attn_gain_part[None], y, c)[0],
                arrays_order(ffn_gain_part[None], y, c)[0],
                q_part[0, :head] + q_part[0, head:],
                k_part[0, :head],
            ]
        ).reshape(-1, 128)
    ).reshape(-1)
    return (
        block_out,
        input_grad,
        gains[:d],
        qkv_grad[:nq].T,
        qkv_grad[nq : nq + nk].T,
        qkv_grad[nq + nk :].T,
        out_grad,
        gains[2 * d : 2 * d + head],
        gains[2 * d + head :],
        gains[d : 2 * d],
        ffn_grad[0].T,
        ffn_grad[1].T,
        ffn_grad[2],
    )


def solution(mesh):
    dp, tensor = mesh.shape["dp"], mesh.shape["tensor"]
    cut = Mesh(
        mesh.devices.reshape(dp // 4, 2, 2, tensor // 2, 2), ("r", "y", "c", "z", "x")
    )
    data, model = ("r", "y", "c"), ("z", "x")
    both = data + model
    rows, wide, tall = P(both, None), P(data, model), P(model, data)
    in_specs = (
        rows, P(data, None), rows, P(), wide, wide, wide, tall, P(), P(), P(), wide, wide, tall
    )
    out_specs = (
        rows, rows, P(), wide, wide, wide, tall, P(), P(), P(), wide, wide, tall
    )
    return jax.shard_map(
        per_device, mesh=cut, in_specs=in_specs, out_specs=out_specs, check_vma=False
    )
```

```python
import functools

import jax
import jax.numpy as jnp
from jax import lax
from jax.experimental import pallas as pl
from jax.experimental.pallas import tpu as pltpu
from jax.sharding import Mesh
from jax.sharding import PartitionSpec as P

EPSILON = 1e-05
ROPE_BASE = 1000000.0
BLOCK = 256
F32 = jnp.float32
BF16 = jnp.bfloat16
VMEM_LIMIT = 40 * 1024 * 1024

NEAR = ("zl", "x")
TENSOR = ("zh", "zl", "x")


def nn(a, b):
    return lax.dot_general(a, b, (((1,), (0,)), ((), ())), preferred_element_type=F32)


def nt(a, b):
    return lax.dot_general(a, b, (((1,), (1,)), ((), ())), preferred_element_type=F32)


def tn(a, b):
    return lax.dot_general(a, b, (((0,), (0,)), ((), ())), preferred_element_type=F32)


def params(**more):
    return pltpu.CompilerParams(vmem_limit_bytes=VMEM_LIMIT, **more)


def swap(v, axes, bit):
    size = lax.axis_size(axes)
    return lax.ppermute(v, axes, [(i, i ^ bit) for i in range(size)])


def quads(v):
    return jnp.split(v, 4, axis=-1)


def own_order(v, y, c):
    runs = lax.axis_size("r")
    if runs > 1:
        lead = v.shape[:-1]
        v = jnp.moveaxis(v.reshape(lead + (runs, 4, -1)), -3, -2).reshape(lead + (-1,))
    return exchange(v, y, c)


def exchange(v, y, c):
    a = quads(v)
    a = [jnp.where(c == 0, a[e], a[e ^ 1]) for e in range(4)]
    return jnp.concatenate([jnp.where(y == 0, a[e], a[e ^ 2]) for e in range(4)], axis=-1)


def arrays_order(v, y, c):
    v = exchange(v, y, c)
    runs = lax.axis_size("r")
    if runs > 1:
        lead = v.shape[:-1]
        v = jnp.moveaxis(v.reshape(lead + (4, runs, -1)), -2, -3).reshape(lead + (-1,))
    return v


def gather_runs(v):
    return lax.all_gather(v, "r", axis=v.ndim - 1, tiled=True) if lax.axis_size("r") > 1 else v


def scatter_runs(v):
    if lax.axis_size("r") == 1:
        return v
    return lax.psum_scatter(
        v.astype(BF16), "r", scatter_dimension=v.ndim - 1, tiled=True
    ).astype(F32)


def total_of(v):
    if lax.axis_size("r") > 1:
        v = lax.psum(v, "r")
    for axis in ("c", "x", "y", "zl", "zh"):
        bit = 1
        while bit < lax.axis_size(axis):
            v = v + swap(v, axis, bit)
            bit *= 2
    return v


def gather_pair(w):
    pair = []
    for v in (w, swap(w, "zh", 1)):
        both = jnp.concatenate([v, swap(v, "y", 1)], axis=-1)
        pair.append((both, swap(both, "c", 1)))
    return [weave(a, b) for a, b in pair]


def weave(near, far):
    (a, b), (a_far, b_far) = jnp.split(near, 2, axis=-1), jnp.split(far, 2, axis=-1)
    return jnp.concatenate([a, a_far, b, b_far], axis=-1)


def fold_core(g):
    e0, e1, e2, e3 = quads(g)
    from_core = swap(jnp.concatenate([e1, e3], axis=-1), "c", 1)
    return (jnp.concatenate([e0, e2], axis=-1).astype(F32) + from_core.astype(F32)).astype(BF16)


def fold_y(g):
    a, b = jnp.split(g, 2, axis=-1)
    return a.astype(F32) + swap(b, "y", 1).astype(F32)


def scatter_pair(own, other):
    other = fold_y(fold_core(other)).astype(BF16)
    return fold_y(fold_core(own)) + swap(other, "zh", 1).astype(F32)


def gather_near(v):
    return [v] + [swap(v, NEAR, bit) for bit in (1, 2, 3)]


def scatter_near(parts):
    return [parts[0]] + [swap(parts[bit], NEAR, bit) for bit in (1, 2, 3)]


def gather_out(w):
    pair = jnp.stack([w, swap(w, "zh", 1)])
    both = jnp.concatenate([pair, swap(pair, "y", 1)], axis=-1)
    every = jnp.stack(gather_near(both))
    return weave(every, swap(every, "c", 1))


def scatter_out(g):
    parts = scatter_near([v for v in fold_core(g)])
    total = sum(v.astype(F32) for v in parts).astype(BF16)
    pair = fold_y(total)
    return pair[0] + swap(pair[1].astype(BF16), "zh", 1).astype(F32)


def lanes_of(shape):
    return lax.broadcasted_iota(jnp.int32, shape, len(shape) - 1)


def head_sums(v, head):
    width = v.shape[-1]
    row = lax.broadcasted_iota(jnp.int32, (width, width), 0) // head
    col = lax.broadcasted_iota(jnp.int32, (width, width), 1) // head
    ones = jnp.where(row == col, 1.0, 0.0).astype(BF16)
    high = v.astype(BF16)
    return nn(high, ones) + nn((v - high.astype(F32)).astype(BF16), ones)


def swap_halves(v, head):
    width, half = v.shape[-1], head // 2
    low = (lanes_of(v.shape) % head) < half
    return jnp.where(low, pltpu.roll(v, width - half, 1), pltpu.roll(v, half, 1))


def qkv_kernel(head, order, xa, w, cosine, sine, q_gain, k_gain, low, kept):
    del order
    proj = nt(xa[0], w[...])
    width = 2 * head
    kept[0] = proj

    def prep(v, gain):
        factor = lax.rsqrt(head_sums(v * v, head) * (1.0 / head) + EPSILON)
        n = v * factor * gain
        return n * cosine[0] + swap_halves(n, head) * sine[0]

    q = prep(proj[:, :width], q_gain[...])
    kv = proj[:, width:]
    k = prep(kv, k_gain[...])
    low[0, :, :width] = q.astype(BF16)
    low[0, :, width:] = jnp.where(lanes_of(kv.shape) < head, k, kv).astype(BF16)


def qkv_call(order, xa, w, cosine, sine, q_gain, k_gain, head):
    blocks, rows, d = xa.shape
    n = w.shape[0]
    whole = lambda shape: pl.BlockSpec(shape, lambda j, order: (0,) * len(shape))
    by_block = lambda *shape: pl.BlockSpec((1,) + shape, lambda j, order: (j, 0, 0))
    return pl.pallas_call(
        functools.partial(qkv_kernel, head),
        grid_spec=pltpu.PrefetchScalarGridSpec(
            num_scalar_prefetch=1,
            grid=(blocks,),
            in_specs=[
                by_block(rows, d),
                whole((n, d)),
                by_block(rows, 2 * head),
                by_block(rows, 2 * head),
                whole((1, 2 * head)),
                whole((1, 2 * head)),
            ],
            out_specs=[
                pl.BlockSpec((1, rows, n), lambda j, order: (order[j], 0, 0)),
                by_block(rows, n),
            ],
        ),
        out_shape=[
            jax.ShapeDtypeStruct((blocks, rows, n), BF16),
            jax.ShapeDtypeStruct((blocks, rows, n), F32),
        ],
        compiler_params=params(),
        cost_estimate=pl.CostEstimate(
            flops=2 * blocks * rows * n * d, bytes_accessed=4 * blocks * rows * d, transcendentals=0
        ),
        name="qkv",
    )(order, xa, w, cosine, sine, q_gain, k_gain)


def stack_heads(v, head, scale=None):
    out = jnp.concatenate([v[:, :head], v[:, head : 2 * head]], axis=0)
    return out if scale is None else (out.astype(F32) * scale).astype(BF16)


def unstack(v_t):
    rows = v_t.shape[1] // 2
    return jnp.concatenate([v_t[:, :rows], v_t[:, rows:]], axis=0).T


def attend_kernel(head, first, qkv, start, context, log_total, turned):
    b = pl.program_id(0)
    width = 2 * head

    @pl.when(b == 0)
    def _():
        kv_t = qkv[:, width:].astype(F32).T
        row = lax.broadcasted_iota(jnp.int32, kv_t.shape, 0)
        turned[...] = jnp.where(row < head, 1.0, kv_t).astype(BF16)

    q2 = stack_heads(qkv[pl.ds(b * BLOCK, BLOCK), :width], head, head**-0.5)
    begin = start[0]
    key = lax.broadcasted_iota(jnp.int32, (BLOCK, 2 * BLOCK), 0)

    def block(j, acc, diagonal):
        s = nt(qkv[pl.ds(j * BLOCK, BLOCK), width : width + head], q2)
        allowed = key >= begin - j * BLOCK
        if diagonal:
            row = lanes_of((BLOCK, 2 * BLOCK)) % BLOCK
            allowed = allowed & (key <= row)
        p = jnp.where(allowed, jnp.exp(s), 0.0)
        return acc + nn(turned[:, pl.ds(j * BLOCK, BLOCK)], p.astype(BF16))

    acc = jnp.zeros((width, 2 * BLOCK), F32)
    acc = lax.fori_loop(first[b], b, lambda j, acc: block(j, acc, False), acc)
    acc = block(b, acc, True)
    total = acc[:1]
    context[...] = unstack(acc[head:] / total).astype(BF16)
    log_total[0] = jnp.log(total)


def attend_call(first, qkv, start, head):
    rows, n = qkv.shape
    blocks = rows // BLOCK
    return pl.pallas_call(
        functools.partial(attend_kernel, head),
        grid_spec=pltpu.PrefetchScalarGridSpec(
            num_scalar_prefetch=1,
            grid=(blocks,),
            in_specs=[
                pl.BlockSpec((rows, n), lambda b, first: (0, 0)),
                pl.BlockSpec((1, 1, 2 * BLOCK), lambda b, first: (b, 0, 0)),
            ],
            out_specs=[
                pl.BlockSpec((BLOCK, 2 * head), lambda b, first: (b, 0)),
                pl.BlockSpec((1, 1, 2 * BLOCK), lambda b, first: (b, 0, 0)),
            ],
            scratch_shapes=[pltpu.VMEM((2 * head, rows), BF16)],
        ),
        out_shape=[
            jax.ShapeDtypeStruct((rows, 2 * head), BF16),
            jax.ShapeDtypeStruct((blocks, 1, 2 * BLOCK), F32),
        ],
        compiler_params=params(),
        cost_estimate=pl.CostEstimate(
            flops=8 * rows * rows * head, bytes_accessed=3 * rows * n, transcendentals=rows * rows
        ),
        name="attend",
    )(first, qkv, start)


def attend_back_kernel(
    head, first, qkv, context, d_context, start, log_total, out, turned, d_key, d_value
):
    b = pl.program_id(0)
    width = 2 * head

    @pl.when(b == 0)
    def _():
        turned[...] = qkv[:, width:].astype(F32).T.astype(BF16)
        d_key[...] = jnp.zeros_like(d_key)
        d_value[...] = jnp.zeros_like(d_value)

    scale = head**-0.5
    q2 = stack_heads(qkv[pl.ds(b * BLOCK, BLOCK), :width], head, scale)
    g = d_context[...]
    g2 = stack_heads(g, head)
    begin = start[0]
    log_sum = log_total[0]
    picks = jnp.where(
        lanes_of((8, width)) // head == lax.broadcasted_iota(jnp.int32, (8, width), 0), 1.0, 0.0
    ).astype(F32)
    delta = lax.dot_general(
        picks,
        g.astype(F32) * context[...].astype(F32),
        (((1,), (1,)), ((), ())),
        preferred_element_type=F32,
        precision=lax.Precision.HIGHEST,
    )
    delta = jnp.concatenate([delta[0:1], delta[1:2]], axis=1)
    key = lax.broadcasted_iota(jnp.int32, (BLOCK, 2 * BLOCK), 0)

    def block(j, acc, diagonal):
        at = pl.ds(j * BLOCK, BLOCK)
        s = nt(qkv[at, width : width + head], q2)
        allowed = key >= begin - j * BLOCK
        if diagonal:
            row = lanes_of((BLOCK, 2 * BLOCK)) % BLOCK
            allowed = allowed & (key <= row)
        p = jnp.where(allowed, jnp.exp(s - log_sum), 0.0)
        d_p = nt(qkv[at, width + head :], g2)
        d_s = (p * (d_p - delta)).astype(BF16)
        d_value[at, :] += nn(p.astype(BF16), g2)
        d_key[at, :] += nn(d_s, q2)
        return acc + nn(turned[:, at], d_s)

    acc = jnp.zeros((width, 2 * BLOCK), F32)
    acc = lax.fori_loop(first[b], b, lambda j, acc: block(j, acc, False), acc)
    acc = block(b, acc, True)
    out[pl.ds(b * BLOCK, BLOCK), :width] = (unstack(acc[:head]) * scale).astype(BF16)

    @pl.when(b == pl.num_programs(0) - 1)
    def _():
        out[:, width:] = jnp.concatenate([d_key[...], d_value[...]], axis=1).astype(BF16)


def attend_back_call(first, qkv, context, d_context, start, log_total, head):
    rows, n = qkv.shape
    blocks = rows // BLOCK
    per_block = pl.BlockSpec((BLOCK, 2 * head), lambda b, first: (b, 0))
    per_row = pl.BlockSpec((1, 1, 2 * BLOCK), lambda b, first: (b, 0, 0))
    return pl.pallas_call(
        functools.partial(attend_back_kernel, head),
        grid_spec=pltpu.PrefetchScalarGridSpec(
            num_scalar_prefetch=1,
            grid=(blocks,),
            in_specs=[
                pl.BlockSpec((rows, n), lambda b, first: (0, 0)),
                per_block,
                per_block,
                per_row,
                per_row,
            ],
            out_specs=pl.BlockSpec((rows, n), lambda b, first: (0, 0)),
            scratch_shapes=[
                pltpu.VMEM((2 * head, rows), BF16),
                pltpu.VMEM((rows, head), F32),
                pltpu.VMEM((rows, head), F32),
            ],
        ),
        out_shape=jax.ShapeDtypeStruct((rows, n), BF16),
        compiler_params=params(),
        cost_estimate=pl.CostEstimate(
            flops=20 * rows * rows * head, bytes_accessed=6 * rows * n, transcendentals=rows * rows
        ),
        name="attend_back",
    )(first, qkv, context, d_context, start, log_total)


def project_kernel(order, context, w, x, gain, hidden, normed):
    del order
    j = pl.program_id(0)

    @pl.when(j == 0)
    def _():
        hidden[...] = x[...]

    hidden[...] += nn(context[0], w[0])

    @pl.when(j == pl.num_programs(0) - 1)
    def _():
        h = hidden[...]
        factor = lax.rsqrt(jnp.mean(h * h, axis=-1, keepdims=True) + EPSILON)
        normed[...] = (h * factor * gain[...]).astype(BF16)


def project_call(order, context, w, x, gain):
    blocks, n, d = w.shape
    rows = x.shape[0]
    whole = lambda shape: pl.BlockSpec(shape, lambda j, order: (0,) * len(shape))
    return pl.pallas_call(
        project_kernel,
        grid_spec=pltpu.PrefetchScalarGridSpec(
            num_scalar_prefetch=1,
            grid=(blocks,),
            in_specs=[
                pl.BlockSpec((1, rows, n), lambda j, order: (j, 0, 0)),
                pl.BlockSpec((1, n, d), lambda j, order: (order[j], 0, 0)),
                whole((rows, d)),
                whole((1, d)),
            ],
            out_specs=[whole((rows, d)), whole((rows, d))],
        ),
        out_shape=[jax.ShapeDtypeStruct((rows, d), F32), jax.ShapeDtypeStruct((rows, d), BF16)],
        compiler_params=params(),
        cost_estimate=pl.CostEstimate(
            flops=2 * blocks * rows * n * d, bytes_accessed=2 * blocks * n * d, transcendentals=0
        ),
        name="project",
    )(order, context, w, x, gain)


def project_back_kernel(
    order, context, w, hidden, gain, dy, p0, p1, p2, p3, d_context, grad, d_hidden, part, low
):
    del order

    @pl.when(pl.program_id(0) == 0)
    def _():
        h = hidden[...]
        g = (p0[...].astype(F32) + p1[...].astype(F32)) + (p2[...].astype(F32) + p3[...].astype(F32))
        n = lax.rsqrt(jnp.mean(h * h, axis=-1, keepdims=True) + EPSILON)
        part[...] = jnp.sum(g * h * n, axis=0, keepdims=True)
        u = gain[...] * g
        mean = jnp.mean(u * h, axis=-1, keepdims=True)
        out = dy[...].astype(F32) + (n * u - h * (n * n * n * mean))
        d_hidden[...] = out
        low[...] = out.astype(BF16)

    d_context[0] = nt(low[...], w[0]).astype(BF16)
    grad[0] = tn(context[0], low[...]).astype(BF16)


def project_back_call(order, context, w, hidden, gain, dy, parts):
    blocks, n, d = w.shape
    rows = hidden.shape[0]
    whole = lambda shape: pl.BlockSpec(shape, lambda j, order: (0,) * len(shape))
    by_block = pl.BlockSpec((1, rows, n), lambda j, order: (j, 0, 0))
    by_order = pl.BlockSpec((1, n, d), lambda j, order: (order[j], 0, 0))
    return pl.pallas_call(
        project_back_kernel,
        grid_spec=pltpu.PrefetchScalarGridSpec(
            num_scalar_prefetch=1,
            grid=(blocks,),
            in_specs=[by_block, by_order, whole((rows, d)), whole((1, d))]
            + [whole((rows, d))] * 5,
            out_specs=[by_block, by_order, whole((rows, d)), whole((1, d))],
            scratch_shapes=[pltpu.VMEM((rows, d), BF16)],
        ),
        out_shape=[
            jax.ShapeDtypeStruct((blocks, rows, n), BF16),
            jax.ShapeDtypeStruct((blocks, n, d), BF16),
            jax.ShapeDtypeStruct((rows, d), F32),
            jax.ShapeDtypeStruct((1, d), F32),
        ],
        compiler_params=params(),
        cost_estimate=pl.CostEstimate(
            flops=4 * blocks * rows * n * d, bytes_accessed=4 * blocks * n * d, transcendentals=0
        ),
        name="project_back",
    )(order, context, w, hidden, gain, dy, *parts)


def qkv_back_kernel(
    head,
    where,
    d_own,
    d_other,
    kept_own,
    kept_other,
    xa,
    w_own,
    w_other,
    cosine,
    sine,
    q_gain,
    k_gain,
    d_xa,
    dw_own,
    dw_other,
    q_part,
    k_part,
    sums,
):
    del where
    j = pl.program_id(0)
    last = pl.num_programs(0) - 1
    width = 2 * head

    @pl.when(j == 0)
    def _():
        q_part[...] = jnp.zeros_like(q_part)
        k_part[...] = jnp.zeros_like(k_part)
        sums[...] = jnp.zeros_like(sums)

    def back(g, v, gain):
        e = g * cosine[0] - swap_halves(g, head) * sine[0]
        m = lax.rsqrt(head_sums(v * v, head) * (1.0 / head) + EPSILON)
        u = gain * e
        mean = head_sums(u * v, head) * (1.0 / head)
        return m * u - v * (m * m * m * mean), jnp.sum(e * v * m, axis=0, keepdims=True)

    total = None
    for s, (grads, kept, w) in enumerate(
        ((d_own, kept_own, w_own), (d_other, kept_other, w_other))
    ):
        g, v = grads[0].astype(F32), kept[0]
        d_q, part = back(g[:, :width], v[:, :width], q_gain[...])
        q_part[...] += part
        d_k, part = back(g[:, width:], v[:, width:], k_gain[...])
        k_part[...] += part
        d_kv = jnp.where(lanes_of(d_k.shape) < head, d_k, g[:, width:])
        low = jnp.concatenate([d_q, d_kv], axis=1).astype(BF16)
        here = nn(low, w[...])
        total = here if total is None else total + here
        sums[s] += tn(low, xa[0])
    d_xa[0] = total.astype(BF16)

    @pl.when(j == last)
    def _():
        dw_own[...] = sums[0].astype(BF16)
        dw_other[...] = sums[1].astype(BF16)


def qkv_back_call(
    where, d_own, d_other, kept, xa, w, cosine, sine, q_gain, k_gain, head
):
    blocks, rows, d = xa.shape
    n = w[0].shape[0]
    whole = lambda shape: pl.BlockSpec(shape, lambda j, where: (0,) * len(shape))
    by_block = lambda *shape: pl.BlockSpec((1,) + shape, lambda j, where: (j, 0, 0))
    lane = (1, 2 * head)
    return pl.pallas_call(
        functools.partial(qkv_back_kernel, head),
        grid_spec=pltpu.PrefetchScalarGridSpec(
            num_scalar_prefetch=1,
            grid=(blocks,),
            in_specs=[
                pl.BlockSpec((1, rows, n), lambda j, where: (where[4] * 4 + where[j], 0, 0)),
                pl.BlockSpec((1, rows, n), lambda j, where: (where[j], 0, 0)),
                by_block(rows, n),
                by_block(rows, n),
                by_block(rows, d),
                whole((n, d)),
                whole((n, d)),
                by_block(rows, 2 * head),
                by_block(rows, 2 * head),
                whole(lane),
                whole(lane),
            ],
            out_specs=[by_block(rows, d), whole((n, d)), whole((n, d)), whole(lane), whole(lane)],
            scratch_shapes=[pltpu.VMEM((2, n, d), F32)],
        ),
        out_shape=[
            jax.ShapeDtypeStruct((blocks, rows, d), BF16),
            jax.ShapeDtypeStruct((n, d), BF16),
            jax.ShapeDtypeStruct((n, d), BF16),
            jax.ShapeDtypeStruct(lane, F32),
            jax.ShapeDtypeStruct(lane, F32),
        ],
        compiler_params=params(),
        cost_estimate=pl.CostEstimate(
            flops=8 * blocks * rows * n * d, bytes_accessed=8 * blocks * rows * d, transcendentals=0
        ),
        name="qkv_back",
    )(where, d_own, d_other, kept[0], kept[1], xa, w[0], w[1], cosine, sine, q_gain, k_gain)


def ffn_kernel(xf, dy, w, acts, out, d_xf):
    gate, up = nt(xf[...], w[0]), nt(xf[...], w[1])
    d_act = nt(dy[...], w[2]).astype(BF16).astype(F32)
    sig = 1.0 / (1.0 + jnp.exp(-gate))
    silu = gate * sig
    act = (silu * up).astype(BF16)
    d_gate = (d_act * up * (sig * (1.0 + gate * (1.0 - sig)))).astype(BF16)
    d_up = (d_act * silu).astype(BF16)
    d_xf[...] = (nn(d_gate, w[0]) + nn(d_up, w[1])).astype(BF16)
    out[...] = nn(act, w[2]).astype(BF16)
    acts[0] = d_gate
    acts[1] = d_up
    acts[2] = act


def ffn_call(xf, dy, w):
    rows, d = xf.shape
    units = w.shape[1]
    tokens = pl.BlockSpec((BLOCK, d), lambda j: (j, 0))
    return pl.pallas_call(
        ffn_kernel,
        grid=(rows // BLOCK,),
        in_specs=[tokens, tokens, pl.BlockSpec((3, units, d), lambda j: (0, 0, 0))],
        out_specs=[pl.BlockSpec((3, BLOCK, units), lambda j: (0, j, 0)), tokens, tokens],
        out_shape=[
            jax.ShapeDtypeStruct((3, rows, units), BF16),
            jax.ShapeDtypeStruct((rows, d), BF16),
            jax.ShapeDtypeStruct((rows, d), BF16),
        ],
        compiler_params=params(),
        cost_estimate=pl.CostEstimate(
            flops=12 * rows * units * d,
            bytes_accessed=6 * units * d + 8 * rows * d,
            transcendentals=rows * units,
        ),
        name="ffn",
    )(xf, dy, w)


def ffn_grad_kernel(a_own, a_rest, x_own, x_rest, y_own, y_rest, grad):
    which = pl.program_id(0)

    @pl.when(which < 2)
    def _():
        grad[0] = (tn(a_own[0], x_own[...]) + tn(a_rest[0], x_rest[...])).astype(BF16)

    @pl.when(which == 2)
    def _():
        grad[0] = (tn(a_own[0], y_own[...]) + tn(a_rest[0], y_rest[...])).astype(BF16)


def ffn_grad_call(a_own, a_rest, x_own, x_rest, y_own, y_rest):
    three, own, units = a_own.shape
    rest, d = x_rest.shape
    tile = units // 3
    whole = lambda shape: pl.BlockSpec(shape, lambda k, j: (0,) * len(shape))
    return pl.pallas_call(
        ffn_grad_kernel,
        grid=(three, 3),
        in_specs=[
            pl.BlockSpec((1, own, tile), lambda k, j: (k, 0, j)),
            pl.BlockSpec((1, rest, tile), lambda k, j: (k, 0, j)),
            whole((own, d)),
            whole((rest, d)),
            whole((own, d)),
            whole((rest, d)),
        ],
        out_specs=pl.BlockSpec((1, tile, d), lambda k, j: (k, j, 0)),
        out_shape=jax.ShapeDtypeStruct((three, units, d), BF16),
        compiler_params=params(),
        cost_estimate=pl.CostEstimate(
            flops=6 * units * d * (own + rest),
            bytes_accessed=2 * units * (4 * d + 3 * (own + rest)),
            transcendentals=0,
        ),
        name="ffn_grad",
    )(a_own, a_rest, x_own, x_rest, y_own, y_rest)


def norm_factor(v):
    return lax.rsqrt(jnp.mean(v * v, axis=-1, keepdims=True) + EPSILON)


def norm_back(v, factor, gain, grad):
    u = gain * grad
    part = jnp.sum(grad * v * factor, axis=0)
    mean = jnp.mean(u * v, axis=-1, keepdims=True)
    return factor * u - v * (factor * factor * factor * mean), part


def per_device(
    tokens,
    segment_ids,
    cotangent,
    attn_gain,
    query_weight,
    key_weight,
    value_weight,
    output_weight,
    query_gain,
    key_gain,
    ffn_gain,
    gate_weight,
    up_weight,
    down_weight,
):
    y, c, zh = lax.axis_index("y"), lax.axis_index("c"), lax.axis_index("zh")
    near = lax.axis_index(NEAR)
    head = query_gain.shape[0]
    rows = tokens.shape[0]
    nq, nk = query_weight.shape[1], key_weight.shape[1]
    n = nq + 2 * nk

    x = own_order(tokens, y, c).astype(F32)
    gain_a = own_order(attn_gain[None], y, c)
    gain_f = own_order(ffn_gain[None], y, c)
    gain_q = jnp.concatenate([query_gain, query_gain])[None]
    gain_k = jnp.concatenate([key_gain, key_gain])[None]
    x_factor = norm_factor(x)
    xa = (x * x_factor * gain_a).astype(BF16)
    xa_all = jnp.stack(gather_near(xa))
    qkv_w = gather_pair(
        gather_runs(jnp.concatenate([query_weight.T, key_weight.T, value_weight.T], axis=0))
    )

    xa_all, qkv_w, later = lax.optimization_barrier(
        (xa_all, qkv_w, (cotangent, output_weight, gate_weight, up_weight, down_weight))
    )
    cotangent, output_weight, gate_weight, up_weight, down_weight = later
    dy = own_order(cotangent, y, c)
    ffn_w = gather_pair(gather_runs(jnp.stack([gate_weight.T, up_weight.T, down_weight])))
    units = ffn_w[0].shape[1]
    ffn_w = jnp.concatenate(ffn_w, axis=1)
    out_w = gather_out(gather_runs(output_weight))
    out_w = out_w.reshape((8,) + out_w.shape[2:])
    dy_all = gather_near(dy)
    dy_rest = jnp.concatenate(dy_all[1:], axis=0)

    segment = segment_ids[0]
    total_rows = segment.shape[0]
    index = jnp.arange(total_rows, dtype=jnp.int32)
    opens = jnp.concatenate([jnp.ones((1,), dtype=jnp.bool_), segment[1:] != segment[:-1]])
    begin = lax.cummax(jnp.where(opens, index, 0), axis=0)
    blocks = total_rows // BLOCK
    first = begin[::BLOCK] // BLOCK
    by_block = begin.reshape(blocks, 1, BLOCK)
    start = jnp.concatenate([by_block, by_block], axis=2)
    four = jnp.arange(4, dtype=jnp.int32) ^ near
    position = lax.dynamic_slice_in_dim(index - begin, zh * 4 * rows, 4 * rows).astype(F32)
    inverse = ROPE_BASE ** (-(jnp.arange(head // 2, dtype=F32) * 2.0) / head)
    angle = (position[:, None] * inverse[None, :]).reshape(4, rows, head // 2)[four]
    cos_half, sin_half = jnp.cos(angle), jnp.sin(angle)
    cosine = jnp.concatenate([cos_half] * 4, axis=2)
    sine = jnp.concatenate([-sin_half, sin_half] * 2, axis=2)
    where = jnp.concatenate([four, zh[None]]).astype(jnp.int32)
    eight = jnp.arange(8, dtype=jnp.int32)
    order = (((eight % 4) ^ near) * 2 + ((eight // 4) ^ zh)).astype(jnp.int32)

    low, kept = zip(
        *[qkv_call(where, xa_all, w, cosine, sine, gain_q, gain_k, head) for w in qkv_w]
    )
    here, there = low[0], swap(low[1], "zh", 1)
    qkv = jnp.concatenate(
        [jnp.where(zh == 0, here, there), jnp.where(zh == 0, there, here)], axis=0
    ).reshape(total_rows, n)
    context, log_total = attend_call(first, qkv, start, head)

    def to_heads(v):
        return lax.all_to_all(v, TENSOR, 0, 0, tiled=True)

    context_rows = to_heads(context.reshape(-1, rows, nq))
    hidden, xf = project_call(order, context_rows, out_w, x, gain_f)

    xf_all = gather_near(xf)
    acts_own, out_own, d_xf_own = ffn_call(xf, dy, ffn_w)
    xf_rest = jnp.concatenate(xf_all[1:], axis=0)
    acts_rest, out_rest, d_xf_rest = ffn_call(xf_rest, dy_rest, ffn_w)
    d_xf = scatter_near([d_xf_own] + jnp.split(d_xf_rest, 3, axis=0))
    ffn_grad = ffn_grad_call(acts_own, acts_rest, xf, xf_rest, dy, dy_rest)

    d_context_rows, out_grad, d_hidden, ffn_gain_part = project_back_call(
        order, context_rows, out_w, hidden, gain_f, dy, d_xf
    )
    d_context = to_heads(d_context_rows).reshape(total_rows, nq)
    d_qkv = attend_back_call(first, qkv, context, d_context, start, log_total, head)
    d_qkv = d_qkv.reshape(-1, rows, n)
    d_other = swap(jnp.where(zh == 0, d_qkv[4:], d_qkv[:4]), "zh", 1)
    d_xa, dw_own, dw_other, q_part, k_part = qkv_back_call(
        where, d_qkv, d_other, kept, xa_all, qkv_w, cosine, sine, gain_q, gain_k, head
    )
    d_xa = sum(v.astype(F32) for v in scatter_near([v for v in d_xa]))
    x_back, attn_gain_part = norm_back(x, x_factor, gain_a, d_xa)
    input_grad = arrays_order((d_hidden + x_back).astype(BF16), y, c)

    ffn_out = scatter_near([out_own] + jnp.split(out_rest, 3, axis=0))
    ffn_out = sum(v.astype(F32) for v in ffn_out)
    block_out = arrays_order((hidden + ffn_out).astype(BF16), y, c)

    qkv_grad = scatter_runs(scatter_pair(dw_own, dw_other))
    ffn_grad = scatter_runs(scatter_pair(ffn_grad[:, :units], ffn_grad[:, units:]))
    out_grad = scatter_runs(scatter_out(out_grad.reshape((4, 2) + out_grad.shape[1:])))

    d = x.shape[1]
    gains = total_of(
        jnp.concatenate(
            [
                arrays_order(attn_gain_part[None], y, c)[0],
                arrays_order(ffn_gain_part, y, c)[0],
                q_part[0, :head] + q_part[0, head:],
                k_part[0, :head],
            ]
        ).reshape(-1, 128)
    ).reshape(-1)
    return (
        block_out,
        input_grad,
        gains[:d],
        qkv_grad[:nq].T,
        qkv_grad[nq : nq + nk].T,
        qkv_grad[nq + nk :].T,
        out_grad,
        gains[2 * d : 2 * d + head],
        gains[2 * d + head :],
        gains[d : 2 * d],
        ffn_grad[0].T,
        ffn_grad[1].T,
        ffn_grad[2],
    )


def solution(mesh):
    dp, tensor = mesh.shape["dp"], mesh.shape["tensor"]
    cut = Mesh(
        mesh.devices.reshape(dp // 4, 2, 2, tensor // 4, 2, 2), ("r", "y", "c", "zh", "zl", "x")
    )
    data, model = ("r", "y", "c"), TENSOR
    both = data + model
    rows, wide, tall = P(both, None), P(data, model), P(model, data)
    in_specs = (
        rows, P(data, None), rows, P(), wide, wide, wide, tall, P(), P(), P(), wide, wide, tall
    )
    out_specs = (
        rows, rows, P(), wide, wide, wide, tall, P(), P(), P(), wide, wide, tall
    )
    return jax.shard_map(
        per_device, mesh=cut, in_specs=in_specs, out_specs=out_specs, check_vma=False
    )
```

```python
import functools

import jax
import jax.numpy as jnp
from jax import lax
from jax.experimental import pallas as pl
from jax.experimental.pallas import tpu as pltpu
from jax.sharding import Mesh
from jax.sharding import PartitionSpec as P

EPSILON = 1e-05
ROPE_BASE = 1000000.0
BLOCK = 256
F32 = jnp.float32
BF16 = jnp.bfloat16
VMEM_LIMIT = 40 * 1024 * 1024

NEAR = ("zl", "x")
TENSOR = ("zh", "zl", "x")


def nn(a, b):
    return lax.dot_general(a, b, (((1,), (0,)), ((), ())), preferred_element_type=F32)


def nt(a, b):
    return lax.dot_general(a, b, (((1,), (1,)), ((), ())), preferred_element_type=F32)


def tn(a, b):
    return lax.dot_general(a, b, (((0,), (0,)), ((), ())), preferred_element_type=F32)


def params(**more):
    return pltpu.CompilerParams(vmem_limit_bytes=VMEM_LIMIT, **more)


def swap(v, axes, bit):
    size = lax.axis_size(axes)
    return lax.ppermute(v, axes, [(i, i ^ bit) for i in range(size)])


def quads(v):
    return jnp.split(v, 4, axis=-1)


def own_order(v, y, c):
    runs = lax.axis_size("r")
    if runs > 1:
        lead = v.shape[:-1]
        v = jnp.moveaxis(v.reshape(lead + (runs, 4, -1)), -3, -2).reshape(lead + (-1,))
    return exchange(v, y, c)


def exchange(v, y, c):
    a = quads(v)
    a = [jnp.where(c == 0, a[e], a[e ^ 1]) for e in range(4)]
    return jnp.concatenate([jnp.where(y == 0, a[e], a[e ^ 2]) for e in range(4)], axis=-1)


def arrays_order(v, y, c):
    v = exchange(v, y, c)
    runs = lax.axis_size("r")
    if runs > 1:
        lead = v.shape[:-1]
        v = jnp.moveaxis(v.reshape(lead + (4, runs, -1)), -2, -3).reshape(lead + (-1,))
    return v


def gather_runs(v):
    return lax.all_gather(v, "r", axis=v.ndim - 1, tiled=True) if lax.axis_size("r") > 1 else v


def scatter_runs(v):
    if lax.axis_size("r") == 1:
        return v
    return lax.psum_scatter(
        v.astype(BF16), "r", scatter_dimension=v.ndim - 1, tiled=True
    ).astype(F32)


def total_of(v):
    if lax.axis_size("r") > 1:
        v = lax.psum(v, "r")
    for axis in ("c", "x", "y", "zl", "zh"):
        bit = 1
        while bit < lax.axis_size(axis):
            v = v + swap(v, axis, bit)
            bit *= 2
    return v


def gather_pair(w):
    pieces = []
    for v in (w, swap(w, "zh", 1)):
        v_y = swap(v, "y", 1)
        pieces.append([v, swap(v, "c", 1), v_y, swap(v_y, "c", 1)])
    return pieces


def gather_stacked(w):
    pair = jnp.stack([w, swap(w, "zh", 1)])
    pair_y = swap(pair, "y", 1)
    return [pair, swap(pair, "c", 1), pair_y, swap(pair_y, "c", 1)]


def gather_out(w):
    pair = jnp.stack([w, swap(w, "zh", 1)])
    both = jnp.concatenate([pair, swap(pair, "y", 1)], axis=-1)
    every = jnp.stack([both] + [swap(both, NEAR, bit) for bit in (1, 2, 3)])
    return every, swap(every, "c", 1)


def add_swapped(keep, send, axes, bit):
    return keep.astype(F32) + swap(send, axes, bit).astype(F32)


def halves(v):
    return jnp.split(v, 2, axis=-1)


def after(later, *done):
    later, done = lax.optimization_barrier((later, done))
    return (later,) + tuple(done)


def lanes_of(shape):
    return lax.broadcasted_iota(jnp.int32, shape, len(shape) - 1)


def head_sums(v, head):
    width = v.shape[-1]
    row = lax.broadcasted_iota(jnp.int32, (width, width), 0) // head
    col = lax.broadcasted_iota(jnp.int32, (width, width), 1) // head
    ones = jnp.where(row == col, 1.0, 0.0).astype(BF16)
    high = v.astype(BF16)
    return nn(high, ones) + nn((v - high.astype(F32)).astype(BF16), ones)


def swap_halves(v, head):
    width, half = v.shape[-1], head // 2
    low = (lanes_of(v.shape) % head) < half
    return jnp.where(low, pltpu.roll(v, width - half, 1), pltpu.roll(v, half, 1))


def rope_prep(v, gain, cosine, sine, head):
    factor = lax.rsqrt(head_sums(v * v, head) * (1.0 / head) + EPSILON)
    n = v * factor * gain
    return n * cosine + swap_halves(n, head) * sine


def project_qkv(xa, w, slot):
    cols = w[0].shape[-1]
    return sum(nt(xa[:, e * cols : (e + 1) * cols], w[e][slot]) for e in range(4))


def qkv_kernel(head, count, *refs):
    xa, w = refs[:count], refs[count : count + 4]
    cosine, sine, q_gain, k_gain, own, other = refs[count + 4 :]
    width = 2 * head
    for slot, low in ((1, other), (0, own)):
        for i in range(count):
            proj = project_qkv(xa[i], w, slot)
            q = rope_prep(proj[:, :width], q_gain[...], cosine[i], sine[i], head)
            kv = proj[:, width:]
            k = rope_prep(kv, k_gain[...], cosine[i], sine[i], head)
            low[i, :, :width] = q.astype(BF16)
            low[i, :, width:] = jnp.where(lanes_of(kv.shape) < head, k, kv).astype(BF16)


def qkv_call(xa, w, cosine, sine, q_gain, k_gain, head):
    count, (rows, d), n = len(xa), xa[0].shape, w[0].shape[1]
    low = jax.ShapeDtypeStruct((count, rows, n), BF16)
    return pl.pallas_call(
        functools.partial(qkv_kernel, head, count),
        out_shape=[low, low],
        compiler_params=params(),
        cost_estimate=pl.CostEstimate(
            flops=4 * count * rows * n * d, bytes_accessed=4 * count * rows * d, transcendentals=0
        ),
        name="qkv",
    )(*xa, *w, cosine, sine, q_gain, k_gain)


def stack_heads(v, head, scale=None):
    out = jnp.concatenate([v[:, :head], v[:, head : 2 * head]], axis=0)
    return out if scale is None else (out.astype(F32) * scale).astype(BF16)


def unstack(v_t):
    rows = v_t.shape[1] // 2
    return jnp.concatenate([v_t[:, :rows], v_t[:, rows:]], axis=0).T


def attend_kernel(head, first, at, *refs):
    parts = refs[:4]
    start, context, log_total, qkv, turned = refs[4:]
    b = pl.program_id(0)
    width = 2 * head

    @pl.when(b == 0)
    def _():
        done = 0
        for part in parts:
            for i in range(part.shape[0]):
                place = pl.multiple_of(at[done] * BLOCK, BLOCK)
                qkv[pl.ds(place, BLOCK), :] = part[i]
                done += 1
        kv_t = qkv[:, width:].astype(F32).T
        row = lax.broadcasted_iota(jnp.int32, kv_t.shape, 0)
        turned[...] = jnp.where(row < head, 1.0, kv_t).astype(BF16)

    q2 = stack_heads(qkv[pl.ds(b * BLOCK, BLOCK), :width], head, head**-0.5)
    begin = start[0]
    key = lax.broadcasted_iota(jnp.int32, (BLOCK, 2 * BLOCK), 0)

    def block(j, acc, diagonal):
        s = nt(qkv[pl.ds(j * BLOCK, BLOCK), width : width + head], q2)
        allowed = key >= begin - j * BLOCK
        if diagonal:
            row = lanes_of((BLOCK, 2 * BLOCK)) % BLOCK
            allowed = allowed & (key <= row)
        p = jnp.where(allowed, jnp.exp(s), 0.0)
        return acc + nn(turned[:, pl.ds(j * BLOCK, BLOCK)], p.astype(BF16))

    acc = jnp.zeros((width, 2 * BLOCK), F32)
    acc = lax.fori_loop(first[b], b, lambda j, acc: block(j, acc, False), acc)
    acc = block(b, acc, True)
    total = acc[:1]
    context[...] = unstack(acc[head:] / total).astype(BF16)
    log_total[0] = jnp.log(total)


def attend_call(first, at, parts, start, head):
    n = parts[0].shape[-1]
    rows = sum(v.shape[0] for v in parts) * BLOCK
    blocks = rows // BLOCK
    whole = lambda shape: pl.BlockSpec(shape, lambda b, first, at: (0,) * len(shape))
    return pl.pallas_call(
        functools.partial(attend_kernel, head),
        grid_spec=pltpu.PrefetchScalarGridSpec(
            num_scalar_prefetch=2,
            grid=(blocks,),
            in_specs=[whole(v.shape) for v in parts]
            + [pl.BlockSpec((1, 1, 2 * BLOCK), lambda b, first, at: (b, 0, 0))],
            out_specs=[
                pl.BlockSpec((BLOCK, 2 * head), lambda b, first, at: (b, 0)),
                pl.BlockSpec((1, 1, 2 * BLOCK), lambda b, first, at: (b, 0, 0)),
                whole((rows, n)),
            ],
            scratch_shapes=[pltpu.VMEM((2 * head, rows), BF16)],
        ),
        out_shape=[
            jax.ShapeDtypeStruct((rows, 2 * head), BF16),
            jax.ShapeDtypeStruct((blocks, 1, 2 * BLOCK), F32),
            jax.ShapeDtypeStruct((rows, n), BF16),
        ],
        compiler_params=params(),
        cost_estimate=pl.CostEstimate(
            flops=8 * rows * rows * head, bytes_accessed=3 * rows * n, transcendentals=rows * rows
        ),
        name="attend",
    )(first, at, *parts, start)


def attend_back_kernel(
    head, first, to, qkv, context, d_context, start, log_total, out, turned, d_key, d_value
):
    b = pl.program_id(0)
    width = 2 * head

    @pl.when(b == 0)
    def _():
        turned[...] = qkv[:, width:].astype(F32).T.astype(BF16)
        d_key[...] = jnp.zeros_like(d_key)
        d_value[...] = jnp.zeros_like(d_value)

    scale = head**-0.5
    q2 = stack_heads(qkv[pl.ds(b * BLOCK, BLOCK), :width], head, scale)
    g = d_context[...]
    g2 = stack_heads(g, head)
    begin = start[0]
    log_sum = log_total[0]
    picks = jnp.where(
        lanes_of((8, width)) // head == lax.broadcasted_iota(jnp.int32, (8, width), 0), 1.0, 0.0
    ).astype(F32)
    delta = lax.dot_general(
        picks,
        g.astype(F32) * context[...].astype(F32),
        (((1,), (1,)), ((), ())),
        preferred_element_type=F32,
        precision=lax.Precision.HIGHEST,
    )
    delta = jnp.concatenate([delta[0:1], delta[1:2]], axis=1)
    key = lax.broadcasted_iota(jnp.int32, (BLOCK, 2 * BLOCK), 0)

    def block(j, acc, diagonal):
        at = pl.ds(j * BLOCK, BLOCK)
        s = nt(qkv[at, width : width + head], q2)
        allowed = key >= begin - j * BLOCK
        if diagonal:
            row = lanes_of((BLOCK, 2 * BLOCK)) % BLOCK
            allowed = allowed & (key <= row)
        p = jnp.where(allowed, jnp.exp(s - log_sum), 0.0)
        d_p = nt(qkv[at, width + head :], g2)
        d_s = (p * (d_p - delta)).astype(BF16)
        d_value[at, :] += nn(p.astype(BF16), g2)
        d_key[at, :] += nn(d_s, q2)
        return acc + nn(turned[:, at], d_s)

    acc = jnp.zeros((width, 2 * BLOCK), F32)
    acc = lax.fori_loop(first[b], b, lambda j, acc: block(j, acc, False), acc)
    acc = block(b, acc, True)
    out[to[b], :, :width] = (unstack(acc[:head]) * scale).astype(BF16)

    @pl.when(b == pl.num_programs(0) - 1)
    def _():
        for j in range(out.shape[0]):
            at = pl.ds(j * BLOCK, BLOCK)
            out[to[j], :, width:] = jnp.concatenate([d_key[at, :], d_value[at, :]], axis=1).astype(
                BF16
            )


def attend_back_call(first, to, qkv, context, d_context, start, log_total, head):
    rows, n = qkv.shape
    blocks = rows // BLOCK
    per_block = pl.BlockSpec((BLOCK, 2 * head), lambda b, first, to: (b, 0))
    per_row = pl.BlockSpec((1, 1, 2 * BLOCK), lambda b, first, to: (b, 0, 0))
    return pl.pallas_call(
        functools.partial(attend_back_kernel, head),
        grid_spec=pltpu.PrefetchScalarGridSpec(
            num_scalar_prefetch=2,
            grid=(blocks,),
            in_specs=[
                pl.BlockSpec((rows, n), lambda b, first, to: (0, 0)),
                per_block,
                per_block,
                per_row,
                per_row,
            ],
            out_specs=pl.BlockSpec((blocks, BLOCK, n), lambda b, first, to: (0, 0, 0)),
            scratch_shapes=[
                pltpu.VMEM((2 * head, rows), BF16),
                pltpu.VMEM((rows, head), F32),
                pltpu.VMEM((rows, head), F32),
            ],
        ),
        out_shape=jax.ShapeDtypeStruct((blocks, BLOCK, n), BF16),
        compiler_params=params(),
        cost_estimate=pl.CostEstimate(
            flops=20 * rows * rows * head, bytes_accessed=6 * rows * n, transcendentals=rows * rows
        ),
        name="attend_back",
    )(first, to, qkv, context, d_context, start, log_total)


def project_kernel(order, context, w_near, w_far, x, gain, hidden, normed):
    del order
    j = pl.program_id(0)
    cols = w_near.shape[-1] // 2

    @pl.when(j == 0)
    def _():
        hidden[...] = x[...]

    for e in range(4):
        w = (w_near, w_far)[e % 2]
        at = slice(e * cols, (e + 1) * cols)
        hidden[:, at] += nn(context[0], w[0, :, (e // 2) * cols : (e // 2 + 1) * cols])

    @pl.when(j == pl.num_programs(0) - 1)
    def _():
        h = hidden[...]
        factor = lax.rsqrt(jnp.mean(h * h, axis=-1, keepdims=True) + EPSILON)
        normed[...] = (h * factor * gain[...]).astype(BF16)


def project_call(order, context, w, x, gain):
    blocks, n, half = w[0].shape
    rows, d = x.shape
    whole = lambda shape: pl.BlockSpec(shape, lambda j, order: (0,) * len(shape))
    by_order = pl.BlockSpec((1, n, half), lambda j, order: (order[j], 0, 0))
    return pl.pallas_call(
        project_kernel,
        grid_spec=pltpu.PrefetchScalarGridSpec(
            num_scalar_prefetch=1,
            grid=(blocks,),
            in_specs=[
                pl.BlockSpec((1, rows, n), lambda j, order: (j, 0, 0)),
                by_order,
                by_order,
                whole((rows, d)),
                whole((1, d)),
            ],
            out_specs=[whole((rows, d)), whole((rows, d))],
        ),
        out_shape=[jax.ShapeDtypeStruct((rows, d), F32), jax.ShapeDtypeStruct((rows, d), BF16)],
        compiler_params=params(),
        cost_estimate=pl.CostEstimate(
            flops=2 * blocks * rows * n * d, bytes_accessed=2 * blocks * n * d, transcendentals=0
        ),
        name="project",
    )(order, context, w[0], w[1], x, gain)


def project_back_kernel(
    order,
    context,
    w_near,
    w_far,
    hidden,
    gain,
    dy,
    p0,
    p1,
    p2,
    p3,
    d_context,
    keep,
    send,
    d_hidden,
    part,
    low,
):
    del order
    cols = w_near.shape[-1] // 2

    @pl.when(pl.program_id(0) == 0)
    def _():
        h = hidden[...]
        g = (p0[...].astype(F32) + p1[...].astype(F32)) + (p2[...].astype(F32) + p3[...].astype(F32))
        n = lax.rsqrt(jnp.mean(h * h, axis=-1, keepdims=True) + EPSILON)
        part[...] = jnp.sum(g * h * n, axis=0, keepdims=True)
        u = gain[...] * g
        mean = jnp.mean(u * h, axis=-1, keepdims=True)
        out = dy[...].astype(F32) + (n * u - h * (n * n * n * mean))
        d_hidden[...] = out
        low[...] = out.astype(BF16)

    d_low = None
    for e in range(4):
        w = (w_near, w_far)[e % 2]
        here = nt(low[:, e * cols : (e + 1) * cols], w[0, :, (e // 2) * cols : (e // 2 + 1) * cols])
        d_low = here if d_low is None else d_low + here
    d_context[0] = d_low.astype(BF16)
    grad = tn(context[0], low[...]).astype(BF16)
    keep[0, :, :cols] = grad[:, :cols]
    send[0, :, :cols] = grad[:, cols : 2 * cols]
    keep[0, :, cols:] = grad[:, 2 * cols : 3 * cols]
    send[0, :, cols:] = grad[:, 3 * cols :]


def project_back_call(order, context, w, hidden, gain, dy, parts):
    blocks, n, half = w[0].shape
    rows, d = hidden.shape
    whole = lambda shape: pl.BlockSpec(shape, lambda j, order: (0,) * len(shape))
    by_block = pl.BlockSpec((1, rows, n), lambda j, order: (j, 0, 0))
    by_order = pl.BlockSpec((1, n, half), lambda j, order: (order[j], 0, 0))
    grad = jax.ShapeDtypeStruct((blocks, n, half), BF16)
    return pl.pallas_call(
        project_back_kernel,
        grid_spec=pltpu.PrefetchScalarGridSpec(
            num_scalar_prefetch=1,
            grid=(blocks,),
            in_specs=[by_block, by_order, by_order, whole((rows, d)), whole((1, d))]
            + [whole((rows, d))] * 5,
            out_specs=[by_block, by_order, by_order, whole((rows, d)), whole((1, d))],
            scratch_shapes=[pltpu.VMEM((rows, d), BF16)],
        ),
        out_shape=[
            jax.ShapeDtypeStruct((blocks, rows, n), BF16),
            grad,
            grad,
            jax.ShapeDtypeStruct((rows, d), F32),
            jax.ShapeDtypeStruct((1, d), F32),
        ],
        compiler_params=params(),
        cost_estimate=pl.CostEstimate(
            flops=4 * blocks * rows * n * d, bytes_accessed=4 * blocks * n * d, transcendentals=0
        ),
        name="project_back",
    )(order, context, w[0], w[1], hidden, gain, dy, *parts)


def qkv_back_kernel(head, blocks, with_sums, *refs):
    count = len(blocks)
    grads = refs[:2]
    xa, w = refs[2 : 2 + count], refs[2 + count : 6 + count]
    cosine, sine, q_gain, k_gain, a_gain = refs[6 + count : 11 + count]
    refs = refs[11 + count :]
    if with_sums:
        sums_in, parts_in, a_part_in, *d_xa, keep, send, parts, a_part = refs
    else:
        *d_xa, sums, parts, a_part = refs
    width = 2 * head
    cols = w[0].shape[-1]

    def back(g, v, gain, i):
        b = blocks[i]
        e = g * cosine[b] - swap_halves(g, head) * sine[b]
        m = lax.rsqrt(head_sums(v * v, head) * (1.0 / head) + EPSILON)
        u = gain * e
        mean = head_sums(u * v, head) * (1.0 / head)
        return m * u - v * (m * m * m * mean), jnp.sum(e * v * m, axis=0, keepdims=True)

    lows = []
    q_sum = k_sum = 0.0
    for slot in (0, 1):
        for i in range(count):
            v, g = project_qkv(xa[i], w, slot), grads[slot][i].astype(F32)
            d_q, part = back(g[:, :width], v[:, :width], q_gain[...], i)
            q_sum += part
            d_k, part = back(g[:, width:], v[:, width:], k_gain[...], i)
            k_sum += part
            d_kv = jnp.where(lanes_of(d_k.shape) < head, d_k, g[:, width:])
            lows.append(jnp.concatenate([d_q, d_kv], axis=1).astype(BF16))
    a_sum = []
    for e in range(4):
        at = slice(e * cols, (e + 1) * cols)
        total = 0.0
        for i in range(count):
            here = nn(lows[i], w[e][0]) + nn(lows[count + i], w[e][1])
            d_xa[i][:, at] = here.astype(BF16)
            total += jnp.sum(here * xa[i][:, at].astype(F32), axis=0, keepdims=True)
        a_sum.append(total)
        for slot in (0, 1):
            here = sum(tn(lows[slot * count + i], xa[i][:, at]) for i in range(count))
            if with_sums:
                here = (here + sums_in[slot, :, at]).astype(BF16)
                to = slice((e // 2) * cols, (e // 2 + 1) * cols)
                (keep, send)[e % 2][slot, :, to] = here
            else:
                sums[slot, :, at] = here
    a_sum = jnp.concatenate(a_sum, axis=1) / a_gain[...]
    if with_sums:
        q_sum, k_sum = q_sum + parts_in[0:1], k_sum + parts_in[1:2]
        a_sum = a_sum + a_part_in[...]
    parts[0:1] = q_sum
    parts[1:2] = k_sum
    a_part[...] = a_sum


def qkv_back_call(grads, xa, w, cosine, sine, gains, head, blocks, sums=None):
    rows, d = xa[0].shape
    n = w[0].shape[1]
    out = [jax.ShapeDtypeStruct((rows, d), BF16)] * len(blocks)
    if sums is None:
        out += [jax.ShapeDtypeStruct((2, n, d), F32)]
    else:
        out += [jax.ShapeDtypeStruct((2, n, d // 2), BF16)] * 2
    out += [jax.ShapeDtypeStruct((2, 2 * head), F32), jax.ShapeDtypeStruct((1, d), F32)]
    return pl.pallas_call(
        functools.partial(qkv_back_kernel, head, blocks, sums is not None),
        out_shape=out,
        compiler_params=params(),
        cost_estimate=pl.CostEstimate(
            flops=12 * len(blocks) * rows * n * d,
            bytes_accessed=8 * len(blocks) * rows * d,
            transcendentals=0,
        ),
        name="qkv_back",
    )(*grads, *xa, *w, cosine, sine, *gains, *(sums or ()))


def ffn_kernel(count, *refs):
    xf, dy, w = refs[:count], refs[count : 2 * count], refs[2 * count : 2 * count + 8]
    refs = refs[2 * count + 8 :]
    cols = w[0].shape[-1]

    def piece(slot, e, which):
        return w[slot * 4 + e][which]

    def wide(v, slot, which):
        return sum(nt(v[:, e * cols : (e + 1) * cols], piece(slot, e, which)) for e in range(4))

    for i in range(count):
        acts, out, d_xf = refs[3 * i : 3 * i + 3]
        for slot in (0, 1):
            gate, up = wide(xf[i], slot, 0), wide(xf[i], slot, 1)
            d_act = wide(dy[i], slot, 2).astype(BF16).astype(F32)
            sig = 1.0 / (1.0 + jnp.exp(-gate))
            silu = gate * sig
            acts[2, slot] = (silu * up).astype(BF16)
            acts[0, slot] = (d_act * up * (sig * (1.0 + gate * (1.0 - sig)))).astype(BF16)
            acts[1, slot] = (d_act * silu).astype(BF16)
        for e in range(4):
            at = slice(e * cols, (e + 1) * cols)
            d_xf[:, at] = sum(
                nn(acts[k, slot], piece(slot, e, k)) for slot in (0, 1) for k in (0, 1)
            ).astype(BF16)
        for e in range(4):
            at = slice(e * cols, (e + 1) * cols)
            out[:, at] = sum(nn(acts[2, slot], piece(slot, e, 2)) for slot in (0, 1)).astype(BF16)


def ffn_call(xf, dy, w):
    count, (rows, d) = len(xf), xf[0].shape
    units = w[0].shape[1]
    tokens = jax.ShapeDtypeStruct((rows, d), BF16)
    return pl.pallas_call(
        functools.partial(ffn_kernel, count),
        out_shape=[jax.ShapeDtypeStruct((3, 2, rows, units), BF16), tokens, tokens] * count,
        compiler_params=params(),
        cost_estimate=pl.CostEstimate(
            flops=24 * count * rows * units * d,
            bytes_accessed=12 * units * d + 8 * count * rows * d,
            transcendentals=2 * count * rows * units,
        ),
        name="ffn",
    )(*xf, *dy, *w)


def ffn_grad_kernel(*refs):
    acts, xf, dy = refs[:4], refs[4:8], refs[8:12]
    keep, send = refs[12:]
    cols = keep.shape[-1] // 2

    def write(right):
        for e in range(4):
            at = slice(e * cols, (e + 1) * cols)
            here = sum(tn(acts[b][0, 0], right[b][:, at]) for b in range(4)).astype(BF16)
            to = slice((e // 2) * cols, (e // 2 + 1) * cols)
            (keep, send)[e % 2][0, :, to] = here

    pl.when(pl.program_id(0) < 2)(lambda: write(xf))
    pl.when(pl.program_id(0) == 2)(lambda: write(dy))


def ffn_grad_call(acts, xf, dy, slot):
    three, _, rows, units = acts[0].shape
    d = xf[0].shape[1]
    by_kind = pl.BlockSpec((1, 1, rows, units), lambda k: (k, slot, 0, 0))
    half = pl.BlockSpec((1, units, d // 2), lambda k: (k, 0, 0))
    out = jax.ShapeDtypeStruct((three, units, d // 2), BF16)
    return pl.pallas_call(
        ffn_grad_kernel,
        grid=(three,),
        in_specs=[by_kind] * 4 + [pl.BlockSpec((rows, d), lambda k: (0, 0))] * 8,
        out_specs=[half, half],
        out_shape=[out, out],
        compiler_params=params(),
        cost_estimate=pl.CostEstimate(
            flops=24 * units * d * rows,
            bytes_accessed=6 * units * d + 16 * rows * d,
            transcendentals=0,
        ),
        name="ffn_grad",
    )(*acts, *xf, *dy)


def norm_factor(v):
    return lax.rsqrt(jnp.mean(v * v, axis=-1, keepdims=True) + EPSILON)


def norm_back(v, factor, gain, grad):
    u = gain * grad
    part = jnp.sum(grad * v * factor, axis=0)
    mean = jnp.mean(u * v, axis=-1, keepdims=True)
    return factor * u - v * (factor * factor * factor * mean), part


def per_device(
    tokens,
    segment_ids,
    cotangent,
    attn_gain,
    query_weight,
    key_weight,
    value_weight,
    output_weight,
    query_gain,
    key_gain,
    ffn_gain,
    gate_weight,
    up_weight,
    down_weight,
):
    y, c, zh = lax.axis_index("y"), lax.axis_index("c"), lax.axis_index("zh")
    near = lax.axis_index(NEAR)
    head = query_gain.shape[0]
    rows = tokens.shape[0]
    nq, nk = query_weight.shape[1], key_weight.shape[1]
    n = nq + 2 * nk

    x = own_order(tokens, y, c).astype(F32)
    gain_a = own_order(attn_gain[None], y, c)
    gain_f = own_order(ffn_gain[None], y, c)
    gain_q = jnp.concatenate([query_gain, query_gain])[None]
    gain_k = jnp.concatenate([key_gain, key_gain])[None]
    x_factor = norm_factor(x)
    xa = (x * x_factor * gain_a).astype(BF16)
    qkv_shard = jnp.concatenate([query_weight.T, key_weight.T, value_weight.T], axis=0)
    qkv_w = gather_stacked(gather_runs(qkv_shard))
    xa_near = [xa, swap(xa, NEAR, 1), swap(xa, NEAR, 2)]
    ffn_shard = gather_runs(jnp.stack([gate_weight.T, up_weight.T, down_weight]))
    ffn_w = gather_pair(ffn_shard)
    ffn_w = ffn_w[0] + ffn_w[1]
    xa_near.append(swap(xa_near[2], NEAR, 1))

    segment = segment_ids[0]
    total_rows = segment.shape[0]
    index = jnp.arange(total_rows, dtype=jnp.int32)
    opens = jnp.concatenate([jnp.ones((1,), dtype=jnp.bool_), segment[1:] != segment[:-1]])
    begin = lax.cummax(jnp.where(opens, index, 0), axis=0)
    blocks = total_rows // BLOCK
    first = begin[::BLOCK] // BLOCK
    by_block = begin.reshape(blocks, 1, BLOCK)
    start = jnp.concatenate([by_block, by_block], axis=2)
    four = jnp.arange(4, dtype=jnp.int32) ^ near
    position = lax.dynamic_slice_in_dim(index - begin, zh * 4 * rows, 4 * rows).astype(F32)
    inverse = ROPE_BASE ** (-(jnp.arange(head // 2, dtype=F32) * 2.0) / head)
    angle = (position[:, None] * inverse[None, :]).reshape(4, rows, head // 2)[four]
    cos_half, sin_half = jnp.cos(angle), jnp.sin(angle)
    cosine = jnp.concatenate([cos_half] * 4, axis=2)
    sine = jnp.concatenate([-sin_half, sin_half] * 2, axis=2)
    eight = jnp.arange(8, dtype=jnp.int32)
    order = (((eight % 4) ^ near) * 2 + ((eight // 4) ^ zh)).astype(jnp.int32)

    own_a, other_a = qkv_call(xa_near[:3], qkv_w, cosine[:3], sine[:3], gain_q, gain_k, head)
    got_a = swap(other_a, "zh", 1)
    own_b, other_b = qkv_call(xa_near[3:], qkv_w, cosine[3:], sine[3:], gain_q, gain_k, head)
    got_b = swap(other_b, "zh", 1)
    at = jnp.concatenate(
        [zh * 4 + four[:3], zh * 4 + four[3:], (1 - zh) * 4 + four[:3], (1 - zh) * 4 + four[3:]]
    ).astype(jnp.int32)

    (cotangent, output_weight), xa_3 = after((cotangent, output_weight), xa_near[3])
    xa_near[3] = xa_3
    dy = own_order(cotangent, y, c)
    dy_near = [dy, swap(dy, NEAR, 1), swap(dy, NEAR, 2)]
    dy_near.append(swap(dy_near[2], NEAR, 1))
    out_w = [v.reshape((8,) + v.shape[2:]) for v in gather_out(gather_runs(output_weight))]
    parts, dy_near, ffn_w = after((own_a, own_b, got_a, got_b), dy_near, ffn_w)
    context, log_total, qkv = attend_call(first, at, parts, start, head)

    def to_heads(v):
        return lax.all_to_all(v, TENSOR, 0, 0, tiled=True)

    context_rows = to_heads(context.reshape(-1, rows, nq))
    hidden, xf = project_call(order, context_rows, out_w, x, gain_f)

    xf_near = [xf] + [swap(xf, NEAR, bit) for bit in (1, 2, 3)]
    acts_0, out_0, d_xf_0 = ffn_call(xf_near[:1], dy_near[:1], ffn_w)
    acts_1, out_1, d_xf_1, acts_2, out_2, d_xf_2 = ffn_call(xf_near[1:3], dy_near[1:3], ffn_w)
    acts_3, out_3, d_xf_3 = ffn_call(xf_near[3:], dy_near[3:], ffn_w)
    d_xf = [d_xf_0, swap(d_xf_1, NEAR, 1), swap(d_xf_2, NEAR, 2), swap(d_xf_3, NEAR, 3)]
    acts = [acts_0, acts_1, acts_2, acts_3]
    keep_1, send_1 = ffn_grad_call(acts, xf_near, dy_near, 1)
    keep_0, send_0 = ffn_grad_call(acts, xf_near, dy_near, 0)
    ffn_1 = add_swapped(keep_1, send_1, "c", 1).astype(BF16)
    ffn_0 = add_swapped(keep_0, send_0, "c", 1).astype(BF16)
    d_xf, ffn_1, ffn_0 = after(d_xf, ffn_1, ffn_0)
    (out_1, out_2, out_3), *d_xf = after((out_1, out_2, out_3), *d_xf)
    ffn_out = [out_0, swap(out_1, NEAR, 1), swap(out_2, NEAR, 2), swap(out_3, NEAR, 3)]

    d_context_rows, out_keep, out_send, d_hidden, ffn_gain_part = project_back_call(
        order, context_rows, out_w, hidden, gain_f, dy, d_xf
    )
    d_context = to_heads(d_context_rows).reshape(total_rows, nq)
    ffn_1 = add_swapped(*halves(ffn_1), "y", 1).astype(BF16)
    d_context, ffn_1 = after(d_context, ffn_1)
    rank = jnp.array([3, 1, 2, 0], dtype=jnp.int32)[(eight % 4) ^ near]
    to = (rank + 4 * (1 - ((eight // 4) ^ zh))).astype(jnp.int32)
    d_qkv = attend_back_call(first, to, qkv, context, d_context, start, log_total, head)
    ffn_0 = add_swapped(*halves(ffn_0), "y", 1)
    ffn_1_far = swap(ffn_1, "zh", 1)
    got_a, got_b = swap(d_qkv[0:2], "zh", 1), swap(d_qkv[2:4], "zh", 1)
    gains = (gain_q, gain_k, gain_a)
    xa = [xa_near[b] for b in (3, 1)]
    d_xa_3, d_xa_1, *sums = qkv_back_call(
        (d_qkv[4:6], got_a), xa, qkv_w, cosine, sine, gains, head, (3, 1)
    )
    d_xa = [swap(d_xa_3, NEAR, 3), swap(d_xa_1, NEAR, 1)]
    xa = [xa_near[b] for b in (2, 0)]
    d_xa_2, d_xa_0, qkv_keep, qkv_send, head_parts, attn_gain_part = qkv_back_call(
        (d_qkv[6:8], got_b), xa, qkv_w, cosine, sine, gains, head, (2, 0), tuple(sums)
    )
    d_xa += [swap(d_xa_2, NEAR, 2), d_xa_0]
    d_xa = sum(v.astype(F32) for v in d_xa)
    x_back, _ = norm_back(x, x_factor, gain_a, d_xa)
    input_grad = arrays_order((d_hidden + x_back).astype(BF16), y, c)
    block_out = arrays_order((hidden + sum(v.astype(F32) for v in ffn_out)).astype(BF16), y, c)

    own, far = halves(add_swapped(qkv_keep, qkv_send, "c", 1).astype(BF16))
    qkv_grad = own[0].astype(F32) + swap(far[0], "y", 1).astype(F32)
    qkv_grad = qkv_grad + swap(own[1], "zh", 1).astype(F32)
    qkv_grad = qkv_grad + swap(far[1], ("y", "zh"), 3).astype(F32)
    qkv_grad = scatter_runs(qkv_grad)
    ffn_grad = scatter_runs(ffn_0 + ffn_1_far.astype(F32))
    out_grad = add_swapped(out_keep, out_send, "c", 1).astype(BF16)
    out_grad = out_grad.reshape((4, 2) + out_grad.shape[1:])
    out_grad = out_grad[0].astype(F32) + sum(
        swap(out_grad[bit], NEAR, bit).astype(F32) for bit in (1, 2, 3)
    )
    out_grad = add_swapped(*halves(out_grad.astype(BF16)), "y", 1)
    out_grad = scatter_runs(add_swapped(out_grad[0], out_grad[1].astype(BF16), "zh", 1))

    d = x.shape[1]
    gains = total_of(
        jnp.concatenate(
            [
                arrays_order(attn_gain_part, y, c)[0],
                arrays_order(ffn_gain_part, y, c)[0],
                head_parts[0, :head] + head_parts[0, head:],
                head_parts[1, :head],
            ]
        ).reshape(-1, 128)
    ).reshape(-1)
    return (
        block_out,
        input_grad,
        gains[:d],
        qkv_grad[:nq].T,
        qkv_grad[nq : nq + nk].T,
        qkv_grad[nq + nk :].T,
        out_grad,
        gains[2 * d : 2 * d + head],
        gains[2 * d + head :],
        gains[d : 2 * d],
        ffn_grad[0].T,
        ffn_grad[1].T,
        ffn_grad[2],
    )


def solution(mesh):
    dp, tensor = mesh.shape["dp"], mesh.shape["tensor"]
    cut = Mesh(
        mesh.devices.reshape(dp // 4, 2, 2, tensor // 4, 2, 2), ("r", "y", "c", "zh", "zl", "x")
    )
    data, model = ("r", "y", "c"), TENSOR
    both = data + model
    rows, wide, tall = P(both, None), P(data, model), P(model, data)
    in_specs = (
        rows, P(data, None), rows, P(), wide, wide, wide, tall, P(), P(), P(), wide, wide, tall
    )
    out_specs = (
        rows, rows, P(), wide, wide, wide, tall, P(), P(), P(), wide, wide, tall
    )
    return jax.shard_map(
        per_device, mesh=cut, in_specs=in_specs, out_specs=out_specs, check_vma=False
    )
```

```python
import functools

import jax
import jax.numpy as jnp
from jax import lax
from jax.experimental import pallas as pl
from jax.experimental.pallas import tpu as pltpu
from jax.sharding import Mesh
from jax.sharding import PartitionSpec as P

EPSILON = 1e-05
ROPE_BASE = 1000000.0
BLOCK = 256
F32 = jnp.float32
BF16 = jnp.bfloat16
VMEM_LIMIT = 40 * 1024 * 1024
NO_COST = pl.CostEstimate(flops=0, bytes_accessed=0, transcendentals=0)

NEAR = ("zl", "x")
TENSOR = ("zh", "zl", "x")


def nn(a, b):
    return lax.dot_general(a, b, (((1,), (0,)), ((), ())), preferred_element_type=F32)


def nt(a, b):
    return lax.dot_general(a, b, (((1,), (1,)), ((), ())), preferred_element_type=F32)


def tn(a, b):
    return lax.dot_general(a, b, (((0,), (0,)), ((), ())), preferred_element_type=F32)


def params(**more):
    return pltpu.CompilerParams(vmem_limit_bytes=VMEM_LIMIT, **more)


def swap(v, axes, bit):
    size = lax.axis_size(axes)
    return lax.ppermute(v, axes, [(i, i ^ bit) for i in range(size)])


def quads(v):
    return jnp.split(v, 4, axis=-1)


def own_order(v, y, c):
    runs = lax.axis_size("r")
    if runs > 1:
        lead = v.shape[:-1]
        v = jnp.moveaxis(v.reshape(lead + (runs, 4, -1)), -3, -2).reshape(lead + (-1,))
    return exchange(v, y, c)


def exchange(v, y, c):
    a = quads(v)
    a = [jnp.where(c == 0, a[e], a[e ^ 1]) for e in range(4)]
    return jnp.concatenate([jnp.where(y == 0, a[e], a[e ^ 2]) for e in range(4)], axis=-1)


def arrays_order(v, y, c):
    v = exchange(v, y, c)
    runs = lax.axis_size("r")
    if runs > 1:
        lead = v.shape[:-1]
        v = jnp.moveaxis(v.reshape(lead + (4, runs, -1)), -2, -3).reshape(lead + (-1,))
    return v


def gather_runs(v):
    return lax.all_gather(v, "r", axis=v.ndim - 1, tiled=True) if lax.axis_size("r") > 1 else v


def scatter_runs(v):
    if lax.axis_size("r") == 1:
        return v
    return lax.psum_scatter(
        v.astype(BF16), "r", scatter_dimension=v.ndim - 1, tiled=True
    ).astype(F32)


def total_of(v):
    if lax.axis_size("r") > 1:
        v = lax.psum(v, "r")
    axes = ("y", "c") + TENSOR
    every = jnp.broadcast_to(v[None], (lax.axis_size(axes),) + v.shape)
    return jnp.sum(lax.all_to_all(every, axes, 0, 0, tiled=True), axis=0)


def after(later, *done):
    later, done = lax.optimization_barrier((later, done))
    return (later,) + tuple(done)


def add_swapped(keep, send, axes, bit):
    return keep.astype(F32) + swap(send, axes, bit).astype(F32)


def halves(v):
    return jnp.split(v, 2, axis=-1)


def lanes_of(shape):
    return lax.broadcasted_iota(jnp.int32, shape, len(shape) - 1)


def head_sums(v, head):
    width = v.shape[-1]
    row = lax.broadcasted_iota(jnp.int32, (width, width), 0) // head
    col = lax.broadcasted_iota(jnp.int32, (width, width), 1) // head
    ones = jnp.where(row == col, 1.0, 0.0).astype(BF16)
    high = v.astype(BF16)
    return nn(high, ones) + nn((v - high.astype(F32)).astype(BF16), ones)


def swap_halves(v, head):
    width, half = v.shape[-1], head // 2
    low = (lanes_of(v.shape) % head) < half
    return jnp.where(low, pltpu.roll(v, width - half, 1), pltpu.roll(v, half, 1))


def rope_prep(v, gain, cosine, sine, head):
    factor = lax.rsqrt(head_sums(v * v, head) * (1.0 / head) + EPSILON)
    n = v * factor * gain
    return n * cosine + swap_halves(n, head) * sine


def project_qkv(xa, w, slot, n):
    cols = w[0].shape[-1]
    return sum(nt(xa[:, e * cols : (e + 1) * cols], piece(w, slot, e)[:n]) for e in range(4))


def piece(w, slot, e):
    return w[e % 2][(e // 2) * 2 + slot]


def qkv_kernel(head, slot, *refs):
    xa, w = refs[:4], refs[4:6]
    cosine, sine, q_gain, k_gain, low = refs[6:]
    n = low.shape[-1]
    width = 2 * head
    for i in range(4):
        proj = project_qkv(xa[i], w, slot, n)
        q = rope_prep(proj[:, :width], q_gain[...], cosine[i], sine[i], head)
        kv = proj[:, width:]
        k = rope_prep(kv, k_gain[...], cosine[i], sine[i], head)
        low[i, :, :width] = q.astype(BF16)
        low[i, :, width:] = jnp.where(lanes_of(kv.shape) < head, k, kv).astype(BF16)


def qkv_call(xa, w, slot, cosine, sine, q_gain, k_gain, head):
    rows, n = xa[0].shape[0], w[1].shape[1]
    return pl.pallas_call(
        functools.partial(qkv_kernel, head, slot),
        out_shape=jax.ShapeDtypeStruct((4, rows, n), BF16),
        compiler_params=params(),
        cost_estimate=NO_COST,
        name="qkv",
    )(*xa, *w, cosine, sine, q_gain, k_gain)


def stack_heads(v, head, scale=None):
    out = jnp.concatenate([v[:, :head], v[:, head : 2 * head]], axis=0)
    return out if scale is None else (out.astype(F32) * scale).astype(BF16)


def unstack(v_t):
    rows = v_t.shape[1] // 2
    return jnp.concatenate([v_t[:, :rows], v_t[:, rows:]], axis=0).T


def attend_kernel(head, first, at, *refs):
    parts = refs[:2]
    start, context, log_total, qkv, turned = refs[2:]
    b = pl.program_id(0)
    width = 2 * head

    @pl.when(b == 0)
    def _():
        done = 0
        for part in parts:
            for i in range(part.shape[0]):
                place = pl.multiple_of(at[done] * BLOCK, BLOCK)
                qkv[pl.ds(place, BLOCK), :] = part[i]
                done += 1
        kv_t = qkv[:, width:].astype(F32).T
        row = lax.broadcasted_iota(jnp.int32, kv_t.shape, 0)
        turned[...] = jnp.where(row < head, 1.0, kv_t).astype(BF16)

    q2 = stack_heads(qkv[pl.ds(b * BLOCK, BLOCK), :width], head, head**-0.5)
    begin = start[0]
    key = lax.broadcasted_iota(jnp.int32, (BLOCK, 2 * BLOCK), 0)

    def block(j, acc, diagonal):
        s = nt(qkv[pl.ds(j * BLOCK, BLOCK), width : width + head], q2)
        allowed = key >= begin - j * BLOCK
        if diagonal:
            row = lanes_of((BLOCK, 2 * BLOCK)) % BLOCK
            allowed = allowed & (key <= row)
        p = jnp.where(allowed, jnp.exp(s), 0.0)
        return acc + nn(turned[:, pl.ds(j * BLOCK, BLOCK)], p.astype(BF16))

    acc = jnp.zeros((width, 2 * BLOCK), F32)
    acc = lax.fori_loop(first[b], b, lambda j, acc: block(j, acc, False), acc)
    acc = block(b, acc, True)
    total = acc[:1]
    context[...] = unstack(acc[head:] / total).astype(BF16)
    log_total[0] = jnp.log(total)


def attend_call(first, at, parts, start, head):
    n = parts[0].shape[-1]
    rows = sum(v.shape[0] for v in parts) * BLOCK
    blocks = rows // BLOCK
    whole = lambda shape: pl.BlockSpec(shape, lambda b, first, at: (0,) * len(shape))
    return pl.pallas_call(
        functools.partial(attend_kernel, head),
        grid_spec=pltpu.PrefetchScalarGridSpec(
            num_scalar_prefetch=2,
            grid=(blocks,),
            in_specs=[whole(v.shape) for v in parts]
            + [pl.BlockSpec((1, 1, 2 * BLOCK), lambda b, first, at: (b, 0, 0))],
            out_specs=[
                pl.BlockSpec((BLOCK, 2 * head), lambda b, first, at: (b, 0)),
                pl.BlockSpec((1, 1, 2 * BLOCK), lambda b, first, at: (b, 0, 0)),
                whole((rows, n)),
            ],
            scratch_shapes=[pltpu.VMEM((2 * head, rows), BF16)],
        ),
        out_shape=[
            jax.ShapeDtypeStruct((rows, 2 * head), BF16),
            jax.ShapeDtypeStruct((blocks, 1, 2 * BLOCK), F32),
            jax.ShapeDtypeStruct((rows, n), BF16),
        ],
        compiler_params=params(),
        cost_estimate=NO_COST,
        name="attend",
    )(first, at, *parts, start)


def attend_back_kernel(
    head, first, to, qkv, context, d_context, start, log_total, out, turned, d_key, d_value
):
    b = pl.program_id(0)
    width = 2 * head

    @pl.when(b == 0)
    def _():
        turned[...] = qkv[:, width:].astype(F32).T.astype(BF16)
        d_key[...] = jnp.zeros_like(d_key)
        d_value[...] = jnp.zeros_like(d_value)

    scale = head**-0.5
    q2 = stack_heads(qkv[pl.ds(b * BLOCK, BLOCK), :width], head, scale)
    g = d_context[...]
    g2 = stack_heads(g, head)
    begin = start[0]
    log_sum = log_total[0]
    picks = jnp.where(
        lanes_of((8, width)) // head == lax.broadcasted_iota(jnp.int32, (8, width), 0), 1.0, 0.0
    ).astype(F32)
    delta = lax.dot_general(
        picks,
        g.astype(F32) * context[...].astype(F32),
        (((1,), (1,)), ((), ())),
        preferred_element_type=F32,
        precision=lax.Precision.HIGHEST,
    )
    delta = jnp.concatenate([delta[0:1], delta[1:2]], axis=1)
    key = lax.broadcasted_iota(jnp.int32, (BLOCK, 2 * BLOCK), 0)

    def block(j, acc, diagonal):
        at = pl.ds(j * BLOCK, BLOCK)
        s = nt(qkv[at, width : width + head], q2)
        allowed = key >= begin - j * BLOCK
        if diagonal:
            row = lanes_of((BLOCK, 2 * BLOCK)) % BLOCK
            allowed = allowed & (key <= row)
        p = jnp.where(allowed, jnp.exp(s - log_sum), 0.0)
        d_p = nt(qkv[at, width + head :], g2)
        d_s = (p * (d_p - delta)).astype(BF16)
        d_value[at, :] += nn(p.astype(BF16), g2)
        d_key[at, :] += nn(d_s, q2)
        return acc + nn(turned[:, at], d_s)

    acc = jnp.zeros((width, 2 * BLOCK), F32)
    acc = lax.fori_loop(first[b], b, lambda j, acc: block(j, acc, False), acc)
    acc = block(b, acc, True)
    out[to[b], :, :width] = (unstack(acc[:head]) * scale).astype(BF16)

    @pl.when(b == pl.num_programs(0) - 1)
    def _():
        for j in range(out.shape[0]):
            at = pl.ds(j * BLOCK, BLOCK)
            out[to[j], :, width:] = jnp.concatenate([d_key[at, :], d_value[at, :]], axis=1).astype(
                BF16
            )


def attend_back_call(first, to, qkv, context, d_context, start, log_total, head):
    rows, n = qkv.shape
    blocks = rows // BLOCK
    per_block = pl.BlockSpec((BLOCK, 2 * head), lambda b, first, to: (b, 0))
    per_row = pl.BlockSpec((1, 1, 2 * BLOCK), lambda b, first, to: (b, 0, 0))
    return pl.pallas_call(
        functools.partial(attend_back_kernel, head),
        grid_spec=pltpu.PrefetchScalarGridSpec(
            num_scalar_prefetch=2,
            grid=(blocks,),
            in_specs=[
                pl.BlockSpec((rows, n), lambda b, first, to: (0, 0)),
                per_block,
                per_block,
                per_row,
                per_row,
            ],
            out_specs=pl.BlockSpec((blocks, BLOCK, n), lambda b, first, to: (0, 0, 0)),
            scratch_shapes=[
                pltpu.VMEM((2 * head, rows), BF16),
                pltpu.VMEM((rows, head), F32),
                pltpu.VMEM((rows, head), F32),
            ],
        ),
        out_shape=jax.ShapeDtypeStruct((blocks, BLOCK, n), BF16),
        compiler_params=params(),
        cost_estimate=NO_COST,
        name="attend_back",
    )(first, to, qkv, context, d_context, start, log_total)


def joined(context, at, q):
    return jnp.concatenate([context[at[q]], context[at[4 + q]]], axis=1)


def piece_of(w, q, e, cols):
    v = w[e % 2][2 * q : 2 * q + 2, :, (e // 2) * cols : (e // 2 + 1) * cols]
    return v.reshape(-1, cols)


def project_kernel(at, context, w_near, w_far, x, gain, hidden, normed):
    cols = w_near.shape[-1] // 2
    left = [joined(context, at, q) for q in range(4)]
    for e in range(4):
        to = slice(e * cols, (e + 1) * cols)
        hidden[:, to] = x[:, to] + sum(
            nn(left[q], piece_of((w_near, w_far), q, e, cols)) for q in range(4)
        )
    h = hidden[...]
    factor = lax.rsqrt(jnp.mean(h * h, axis=-1, keepdims=True) + EPSILON)
    normed[...] = (h * factor * gain[...]).astype(BF16)


def in_vmem(count):
    return [pl.BlockSpec(memory_space=pltpu.VMEM)] * count


def project_call(at, context, w, x, gain):
    rows, d = x.shape
    return pl.pallas_call(
        project_kernel,
        in_specs=[pl.BlockSpec(memory_space=pltpu.SMEM)] + in_vmem(5),
        out_shape=[jax.ShapeDtypeStruct((rows, d), F32), jax.ShapeDtypeStruct((rows, d), BF16)],
        compiler_params=params(),
        cost_estimate=NO_COST,
        name="project",
    )(at, context, w[0], w[1], x, gain)


def project_back_kernel(
    at, context, w_near, w_far, hidden, gain, dy, p0, p1, p2, p3, d_context, keep, send, d_hidden, part
):
    cols = w_near.shape[-1] // 2
    n = context.shape[-1]
    h = hidden[...]
    g = (p0[...].astype(F32) + p1[...].astype(F32)) + (p2[...].astype(F32) + p3[...].astype(F32))
    factor = lax.rsqrt(jnp.mean(h * h, axis=-1, keepdims=True) + EPSILON)
    part[...] = jnp.sum(g * h * factor, axis=0, keepdims=True)
    u = gain[...] * g
    mean = jnp.mean(u * h, axis=-1, keepdims=True)
    out = dy[...].astype(F32) + (factor * u - h * (factor * factor * factor * mean))
    d_hidden[...] = out
    low = out.astype(BF16)
    for q in range(4):
        both = sum(
            nt(low[:, e * cols : (e + 1) * cols], piece_of((w_near, w_far), q, e, cols))
            for e in range(4)
        ).astype(BF16)
        d_context[at[q]] = both[:, :n]
        d_context[at[4 + q]] = both[:, n:]
    for q in range(4):
        grad = tn(joined(context, at, q), low).astype(BF16)
        for s in (0, 1):
            rows = slice(s * n, (s + 1) * n)
            keep[2 * q + s, :, :cols] = grad[rows, :cols]
            send[2 * q + s, :, :cols] = grad[rows, cols : 2 * cols]
            keep[2 * q + s, :, cols:] = grad[rows, 2 * cols : 3 * cols]
            send[2 * q + s, :, cols:] = grad[rows, 3 * cols :]


def project_back_call(at, context, w, hidden, gain, dy, parts):
    rows, d = hidden.shape
    grad = jax.ShapeDtypeStruct(w[0].shape, BF16)
    return pl.pallas_call(
        project_back_kernel,
        in_specs=[pl.BlockSpec(memory_space=pltpu.SMEM)] + in_vmem(10),
        out_shape=[
            jax.ShapeDtypeStruct(context.shape, BF16),
            grad,
            grad,
            jax.ShapeDtypeStruct((rows, d), F32),
            jax.ShapeDtypeStruct((1, d), F32),
        ],
        compiler_params=params(),
        cost_estimate=NO_COST,
        name="project_back",
    )(at, context, w[0], w[1], hidden, gain, dy, *parts)


def qkv_back_kernel(head, *refs):
    grads, xa, w = refs[:2], refs[2:6], refs[6:8]
    cosine, sine, q_gain, k_gain, a_gain = refs[8:13]
    d_xa, (keep, send, parts, a_part) = refs[13:17], refs[17:]
    n = keep.shape[1]
    width = 2 * head
    cols = w[0].shape[-1]

    def back(g, v, gain, i):
        e = g * cosine[i] - swap_halves(g, head) * sine[i]
        m = lax.rsqrt(head_sums(v * v, head) * (1.0 / head) + EPSILON)
        u = gain * e
        mean = head_sums(u * v, head) * (1.0 / head)
        return m * u - v * (m * m * m * mean), jnp.sum(e * v * m, axis=0, keepdims=True)

    lows = []
    q_sum = k_sum = 0.0
    for slot in (0, 1):
        for i in range(4):
            v, g = project_qkv(xa[i], w, slot, n), grads[slot][i].astype(F32)
            d_q, part = back(g[:, :width], v[:, :width], q_gain[...], i)
            q_sum += part
            d_k, part = back(g[:, width:], v[:, width:], k_gain[...], i)
            k_sum += part
            d_kv = jnp.where(lanes_of(d_k.shape) < head, d_k, g[:, width:])
            lows.append(jnp.concatenate([d_q, d_kv], axis=1).astype(BF16))
    for e in range(4):
        at = slice(e * cols, (e + 1) * cols)
        to = slice((e // 2) * cols, (e // 2 + 1) * cols)
        total = 0.0
        for i in range(4):
            here = nn(lows[i], piece(w, 0, e)[:n]) + nn(lows[4 + i], piece(w, 1, e)[:n])
            d_xa[i][:, at] = here.astype(BF16)
            total += jnp.sum(here * xa[i][:, at].astype(F32), axis=0, keepdims=True)
        a_part[:, at] = total / a_gain[:, at]
        for slot in (0, 1):
            here = sum(tn(lows[slot * 4 + i], xa[i][:, at]) for i in range(4))
            (keep, send)[e % 2][slot, :, to] = here.astype(BF16)
    parts[0:1] = q_sum
    parts[1:2] = k_sum


def qkv_back_call(grads, xa, w, cosine, sine, gains, head):
    rows, d = xa[0].shape
    n = w[1].shape[1]
    half = jax.ShapeDtypeStruct((2, n, d // 2), BF16)
    return pl.pallas_call(
        functools.partial(qkv_back_kernel, head),
        out_shape=[jax.ShapeDtypeStruct((rows, d), BF16)] * 4
        + [half, half]
        + [jax.ShapeDtypeStruct((2, 2 * head), F32), jax.ShapeDtypeStruct((1, d), F32)],
        compiler_params=params(),
        cost_estimate=NO_COST,
        name="qkv_back",
    )(*grads, *xa, *w, cosine, sine, *gains)


def ffn_kernel(count, *refs):
    xf, dy, w = refs[:count], refs[count : 2 * count], refs[2 * count : 2 * count + 16]
    refs = refs[2 * count + 16 :]
    cols = w[0].shape[-1]

    def piece(slot, e, which):
        return w[e][which] if slot == 0 else w[4 + 4 * which + e][...]

    def wide(v, slot, which):
        return sum(nt(v[:, e * cols : (e + 1) * cols], piece(slot, e, which)) for e in range(4))

    for i in range(count):
        acts, out, d_xf = refs[3 * i : 3 * i + 3]
        for slot in (0, 1):
            gate, up = wide(xf[i], slot, 0), wide(xf[i], slot, 1)
            d_act = wide(dy[i], slot, 2).astype(BF16).astype(F32)
            sig = 1.0 / (1.0 + jnp.exp(-gate))
            silu = gate * sig
            acts[2, slot] = (silu * up).astype(BF16)
            acts[0, slot] = (d_act * up * (sig * (1.0 + gate * (1.0 - sig)))).astype(BF16)
            acts[1, slot] = (d_act * silu).astype(BF16)
        for e in range(4):
            at = slice(e * cols, (e + 1) * cols)
            d_xf[:, at] = sum(
                nn(acts[k, slot], piece(slot, e, k)) for slot in (0, 1) for k in (0, 1)
            ).astype(BF16)
        for e in range(4):
            at = slice(e * cols, (e + 1) * cols)
            out[:, at] = sum(nn(acts[2, slot], piece(slot, e, 2)) for slot in (0, 1)).astype(BF16)


def ffn_call(xf, dy, w):
    count, (rows, d) = len(xf), xf[0].shape
    units = w[0].shape[1]
    tokens = jax.ShapeDtypeStruct((rows, d), BF16)
    return pl.pallas_call(
        functools.partial(ffn_kernel, count),
        out_shape=[jax.ShapeDtypeStruct((3, 2, rows, units), BF16), tokens, tokens] * count,
        compiler_params=params(),
        cost_estimate=NO_COST,
        name="ffn",
    )(*xf, *dy, *w)


def ffn_grad_kernel(*refs):
    acts, xf, dy = refs[:4], refs[4:8], refs[8:12]
    keep, send = refs[12:]
    cols = keep.shape[-1] // 2

    def write(right):
        for e in range(4):
            at = slice(e * cols, (e + 1) * cols)
            here = sum(tn(acts[b][0, 0], right[b][:, at]) for b in range(4)).astype(BF16)
            to = slice((e // 2) * cols, (e // 2 + 1) * cols)
            (keep, send)[e % 2][0, :, to] = here

    pl.when(pl.program_id(0) < 2)(lambda: write(xf))
    pl.when(pl.program_id(0) == 2)(lambda: write(dy))


def ffn_grad_call(acts, xf, dy, slot):
    three, _, rows, units = acts[0].shape
    d = xf[0].shape[1]
    by_kind = pl.BlockSpec((1, 1, rows, units), lambda k: (k, slot, 0, 0))
    half = pl.BlockSpec((1, units, d // 2), lambda k: (k, 0, 0))
    out = jax.ShapeDtypeStruct((three, units, d // 2), BF16)
    return pl.pallas_call(
        ffn_grad_kernel,
        grid=(three,),
        in_specs=[by_kind] * 4 + [pl.BlockSpec((rows, d), lambda k: (0, 0))] * 8,
        out_specs=[half, half],
        out_shape=[out, out],
        compiler_params=params(),
        cost_estimate=NO_COST,
        name="ffn_grad",
    )(*acts, *xf, *dy)


def norm_factor(v):
    return lax.rsqrt(jnp.mean(v * v, axis=-1, keepdims=True) + EPSILON)


def norm_back(v, factor, gain, grad):
    u = gain * grad
    part = jnp.sum(grad * v * factor, axis=0)
    mean = jnp.mean(u * v, axis=-1, keepdims=True)
    return factor * u - v * (factor * factor * factor * mean), part


def per_device(
    tokens,
    segment_ids,
    cotangent,
    attn_gain,
    query_weight,
    key_weight,
    value_weight,
    output_weight,
    query_gain,
    key_gain,
    ffn_gain,
    gate_weight,
    up_weight,
    down_weight,
):
    y, c, zh = lax.axis_index("y"), lax.axis_index("c"), lax.axis_index("zh")
    near = lax.axis_index(NEAR)
    head = query_gain.shape[0]
    rows = tokens.shape[0]
    nq, nk = query_weight.shape[1], key_weight.shape[1]
    n = nq + 2 * nk

    x = own_order(tokens, y, c).astype(F32)
    gain_a = own_order(attn_gain[None], y, c)
    gain_f = own_order(ffn_gain[None], y, c)
    gain_q = jnp.concatenate([query_gain, query_gain])[None]
    gain_k = jnp.concatenate([key_gain, key_gain])[None]
    x_factor = norm_factor(x)
    xa = (x * x_factor * gain_a).astype(BF16)
    shard = gather_runs(
        jnp.concatenate([query_weight.T, key_weight.T, value_weight.T, output_weight], axis=0)
    )
    ffn_own = gather_runs(jnp.stack([gate_weight.T, up_weight.T, down_weight]))
    xa_near = [xa, swap(xa, NEAR, 1), swap(xa, NEAR, 2)]
    heads = [shard, swap(shard, "zh", 1), swap(shard, "y", 1), swap(shard, ("y", "zh"), 3)]
    gate_far = swap(ffn_own[0], "zh", 1)
    (xa_near, ffn_own), gate_far, *heads = after((xa_near, ffn_own), gate_far, *heads)
    xa_near.append(swap(xa_near[2], NEAR, 1))
    heads = jnp.stack(heads)
    qkv_w = (heads, swap(heads[:, :n], "c", 1))
    up_far = swap(ffn_own[1], "zh", 1)
    (ffn_own, xa_near, gate_far), qkv_w, up_far = after((ffn_own, xa_near, gate_far), qkv_w, up_far)

    segment = segment_ids[0]
    total_rows = segment.shape[0]
    index = jnp.arange(total_rows, dtype=jnp.int32)
    opens = jnp.concatenate([jnp.ones((1,), dtype=jnp.bool_), segment[1:] != segment[:-1]])
    begin = lax.cummax(jnp.where(opens, index, 0), axis=0)
    blocks = total_rows // BLOCK
    first = begin[::BLOCK] // BLOCK
    by_block = begin.reshape(blocks, 1, BLOCK)
    start = jnp.concatenate([by_block, by_block], axis=2)
    four = jnp.arange(4, dtype=jnp.int32) ^ near
    position = lax.dynamic_slice_in_dim(index - begin, zh * 4 * rows, 4 * rows).astype(F32)
    inverse = ROPE_BASE ** (-(jnp.arange(head // 2, dtype=F32) * 2.0) / head)
    angle = (position[:, None] * inverse[None, :]).reshape(4, rows, head // 2)[four]
    cos_half, sin_half = jnp.cos(angle), jnp.sin(angle)
    cosine = jnp.concatenate([cos_half] * 4, axis=2)
    sine = jnp.concatenate([-sin_half, sin_half] * 2, axis=2)
    eight = jnp.arange(8, dtype=jnp.int32)
    places = jnp.concatenate([zh * 4 + four, (1 - zh) * 4 + four]).astype(jnp.int32)

    other = qkv_call(xa_near, qkv_w, 1, cosine, sine, gain_q, gain_k, head)
    (cotangent, ffn_own, gate_far, up_far), other = after(
        (cotangent, ffn_own, gate_far, up_far), other
    )
    dy = own_order(cotangent, y, c)
    got = swap(other, "zh", 1)
    dy_near = [dy, swap(dy, NEAR, 1), swap(dy, NEAR, 2)]
    own_y = swap(ffn_own, "y", 1)
    own = qkv_call(xa_near, qkv_w, 0, cosine, sine, gain_q, gain_k, head)
    (dy_near, ffn_own, gate_far, up_far, heads), own, got, own_y = after(
        (dy_near, ffn_own, gate_far, up_far, qkv_w[0]), own, got, own_y
    )

    context, log_total, qkv = attend_call(first, places, (own, got), start, head)
    down_far = swap(ffn_own[2], "zh", 1)
    out_w = jnp.concatenate([heads[:2, n:], heads[2:, n:]], axis=-1)
    out_w = [out_w] + [swap(out_w, NEAR, bit) for bit in (1, 2, 3)]
    gate_y = swap(gate_far, "y", 1)
    (dy_near, ffn_own, own_y, gate_far, up_far), context, down_far, gate_y, out_w = after(
        (dy_near, ffn_own, own_y, gate_far, up_far), context, down_far, gate_y, out_w
    )

    def to_heads(v):
        return lax.all_to_all(v, TENSOR, 0, 0, tiled=True)

    context_rows = to_heads(context.reshape(-1, rows, nq))
    dy_near.append(swap(dy_near[2], NEAR, 1))
    up_y, down_y = swap(up_far, "y", 1), swap(down_far, "y", 1)
    out_w = jnp.stack(out_w)
    out_w = [v.reshape((8,) + v.shape[2:]) for v in (out_w, swap(out_w, "c", 1))]
    w = [ffn_own, own_y, gate_far, gate_y, up_far, up_y, down_far, down_y]
    own_c, own_yc = swap(ffn_own, "c", 1), swap(own_y, "c", 1)
    w, context_rows, dy_near, own_c, own_yc, out_w = after(
        w, context_rows, dy_near, own_c, own_yc, out_w
    )

    hidden, xf = project_call(places, context_rows, out_w, x, gain_f)
    ffn_w = [w[0], own_c, w[1], own_yc]
    for k in (0, 1, 2):
        far, far_y = w[2 + 2 * k : 4 + 2 * k]
        ffn_w += [far, swap(far, "c", 1), far_y, swap(far_y, "c", 1)]

    xf_near = [xf] + [swap(xf, NEAR, bit) for bit in (1, 2, 3)]
    acts_0, out_0, d_xf_0 = ffn_call(xf_near[:1], dy_near[:1], ffn_w)
    acts_1, out_1, d_xf_1, acts_2, out_2, d_xf_2 = ffn_call(xf_near[1:3], dy_near[1:3], ffn_w)
    acts_3, out_3, d_xf_3 = ffn_call(xf_near[3:], dy_near[3:], ffn_w)
    d_xf = [d_xf_0, swap(d_xf_1, NEAR, 1), swap(d_xf_2, NEAR, 2), swap(d_xf_3, NEAR, 3)]
    acts = [acts_0, acts_1, acts_2, acts_3]
    keep_1, send_1 = ffn_grad_call(acts, xf_near, dy_near, 1)
    keep_0, send_0 = ffn_grad_call(acts, xf_near, dy_near, 0)
    (out_0, out_1, out_2, out_3), d_xf, keep_1, send_1, keep_0, send_0 = after(
        (out_0, out_1, out_2, out_3), d_xf, keep_1, send_1, keep_0, send_0
    )

    d_context_rows, out_keep, out_send, d_hidden, ffn_gain_part = project_back_call(
        places, context_rows, out_w, hidden, gain_f, dy, d_xf
    )
    d_context = to_heads(d_context_rows).reshape(total_rows, nq)
    ffn_1 = add_swapped(keep_1, send_1, "c", 1).astype(BF16)
    gate_1 = add_swapped(*halves(ffn_1[0]), "y", 1).astype(BF16)
    out_grad = add_swapped(out_keep, out_send, "c", 1).astype(BF16)
    (out_1, out_2, out_3, keep_0, ffn_1), d_context, gate_1, out_grad = after(
        (out_1, out_2, out_3, keep_0, ffn_1), d_context, gate_1, out_grad
    )

    place = jnp.where(eight // 4 == zh, 4, 0) + ((eight % 4) ^ near)
    d_qkv = attend_back_call(
        first, place.astype(jnp.int32), qkv, context, d_context, start, log_total, head
    )
    ffn_0 = add_swapped(keep_0, send_0, "c", 1).astype(BF16)
    up_1 = add_swapped(*halves(ffn_1[1]), "y", 1).astype(BF16)
    gate_part = swap(gate_1, "zh", 1)
    ffn_out = [out_0, swap(out_1, NEAR, 1), swap(out_2, NEAR, 2)]
    (ffn_1, out_3, out_grad), d_qkv, ffn_0, up_1, gate_part, *ffn_out = after(
        (ffn_1, out_3, out_grad), d_qkv, ffn_0, up_1, gate_part, *ffn_out
    )

    got = swap(d_qkv[:4], "zh", 1)
    ffn_0 = add_swapped(*halves(ffn_0), "y", 1)
    out_grad = out_grad.reshape((4, 2) + out_grad.shape[1:])
    out_grad = out_grad[0].astype(F32) + sum(
        swap(out_grad[bit], NEAR, bit).astype(F32) for bit in (1, 2, 3)
    )
    (ffn_1, up_1, out_3, d_qkv), got, ffn_0, out_grad = after(
        (ffn_1, up_1, out_3, d_qkv), got, ffn_0, out_grad.astype(BF16)
    )

    gains = (gain_q, gain_k, gain_a)
    xa = [xa_near[b] for b in (3, 1)]
    *d_xa, qkv_keep, qkv_send, head_parts, attn_gain_part = qkv_back_call(
        (d_qkv[4:], got), xa_near, qkv_w, cosine, sine, gains, head
    )
    down_1 = add_swapped(*halves(ffn_1[2]), "y", 1).astype(BF16)
    out_grad = add_swapped(*halves(out_grad), "y", 1)
    up_down = jnp.stack([up_1, down_1])
    (up_down, out_3), d_xa, qkv_send, out_grad, attn_gain_part = after(
        (up_down, out_3), d_xa, qkv_send, out_grad, attn_gain_part
    )

    d_xa = [d_xa[0]] + [swap(d_xa[bit], NEAR, bit) for bit in (1, 2, 3)]
    qkv_grad = add_swapped(qkv_keep, qkv_send, "c", 1).astype(BF16)
    up_down = swap(up_down, "zh", 1)
    (qkv_grad, out_grad, out_3, attn_gain_part), d_xa, up_down = after(
        (qkv_grad, out_grad, out_3, attn_gain_part), d_xa, up_down
    )

    ffn_out.append(swap(out_3, NEAR, 3))
    d = x.shape[1]
    gains = total_of(
        jnp.concatenate(
            [
                arrays_order(attn_gain_part, y, c)[0],
                arrays_order(ffn_gain_part, y, c)[0],
                head_parts[0, :head] + head_parts[0, head:],
                head_parts[1, :head],
            ]
        ).reshape(-1, 128)
    ).reshape(-1)
    own, far = halves(qkv_grad)
    qkv_grad = own[0].astype(F32) + swap(far[0], "y", 1).astype(F32)
    qkv_grad = qkv_grad + swap(own[1], "zh", 1).astype(F32)
    qkv_grad = qkv_grad + swap(far[1], ("y", "zh"), 3).astype(F32)
    out_grad = add_swapped(out_grad[0], out_grad[1].astype(BF16), "zh", 1)
    d_xa = sum(v.astype(F32) for v in d_xa)
    x_back, _ = norm_back(x, x_factor, gain_a, d_xa)
    input_grad = arrays_order((d_hidden + x_back).astype(BF16), y, c)
    block_out = arrays_order((hidden + sum(v.astype(F32) for v in ffn_out)).astype(BF16), y, c)
    qkv_grad = scatter_runs(qkv_grad)
    out_grad = scatter_runs(out_grad)
    ffn_grad = [
        scatter_runs(ffn_0[k] + part.astype(F32))
        for k, part in enumerate((gate_part, up_down[0], up_down[1]))
    ]

    return (
        block_out,
        input_grad,
        gains[:d],
        qkv_grad[:nq].T,
        qkv_grad[nq : nq + nk].T,
        qkv_grad[nq + nk :].T,
        out_grad,
        gains[2 * d : 2 * d + head],
        gains[2 * d + head :],
        gains[d : 2 * d],
        ffn_grad[0].T,
        ffn_grad[1].T,
        ffn_grad[2],
    )


def solution(mesh):
    dp, tensor = mesh.shape["dp"], mesh.shape["tensor"]
    cut = Mesh(
        mesh.devices.reshape(dp // 4, 2, 2, tensor // 4, 2, 2), ("r", "y", "c", "zh", "zl", "x")
    )
    data, model = ("r", "y", "c"), TENSOR
    both = data + model
    rows, wide, tall = P(both, None), P(data, model), P(model, data)
    in_specs = (
        rows, P(data, None), rows, P(), wide, wide, wide, tall, P(), P(), P(), wide, wide, tall
    )
    out_specs = (
        rows, rows, P(), wide, wide, wide, tall, P(), P(), P(), wide, wide, tall
    )
    return jax.shard_map(
        per_device, mesh=cut, in_specs=in_specs, out_specs=out_specs, check_vma=False
    )
```

```python
import functools

import jax
import jax.numpy as jnp
from jax import lax
from jax.experimental import pallas as pl
from jax.experimental.pallas import tpu as pltpu
from jax.sharding import Mesh
from jax.sharding import PartitionSpec as P

EPSILON = 1e-05
ROPE_BASE = 1000000.0
BLOCK = 256
F32 = jnp.float32
BF16 = jnp.bfloat16
VMEM_LIMIT = 40 * 1024 * 1024
NO_COST = pl.CostEstimate(flops=0, bytes_accessed=0, transcendentals=0)

NEAR = ("zl", "x")
TENSOR = ("zh", "zl", "x")


def nn(a, b):
    return lax.dot_general(a, b, (((1,), (0,)), ((), ())), preferred_element_type=F32)


def nt(a, b):
    return lax.dot_general(a, b, (((1,), (1,)), ((), ())), preferred_element_type=F32)


def tn(a, b):
    return lax.dot_general(a, b, (((0,), (0,)), ((), ())), preferred_element_type=F32)


def params(**more):
    return pltpu.CompilerParams(vmem_limit_bytes=VMEM_LIMIT, **more)


def swap(v, axes, bit):
    size = lax.axis_size(axes)
    return lax.ppermute(v, axes, [(i, i ^ bit) for i in range(size)])


def quads(v):
    return jnp.split(v, 4, axis=-1)


def own_order(v, y, c):
    runs = lax.axis_size("r")
    if runs > 1:
        lead = v.shape[:-1]
        v = jnp.moveaxis(v.reshape(lead + (runs, 4, -1)), -3, -2).reshape(lead + (-1,))
    return exchange(v, y, c)


def exchange(v, y, c):
    a = quads(v)
    a = [jnp.where(c == 0, a[e], a[e ^ 1]) for e in range(4)]
    return jnp.concatenate([jnp.where(y == 0, a[e], a[e ^ 2]) for e in range(4)], axis=-1)


def arrays_order(v, y, c):
    v = exchange(v, y, c)
    runs = lax.axis_size("r")
    if runs > 1:
        lead = v.shape[:-1]
        v = jnp.moveaxis(v.reshape(lead + (4, runs, -1)), -2, -3).reshape(lead + (-1,))
    return v


def gather_runs(v):
    return lax.all_gather(v, "r", axis=v.ndim - 1, tiled=True) if lax.axis_size("r") > 1 else v


def scatter_runs(v):
    if lax.axis_size("r") == 1:
        return v
    return lax.psum_scatter(
        v.astype(BF16), "r", scatter_dimension=v.ndim - 1, tiled=True
    ).astype(F32)


def total_of(v):
    if lax.axis_size("r") > 1:
        v = lax.psum(v, "r")
    axes = ("y", "c") + TENSOR
    every = jnp.broadcast_to(v[None], (lax.axis_size(axes),) + v.shape)
    return jnp.sum(lax.all_to_all(every, axes, 0, 0, tiled=True), axis=0)


def after(later, *done):
    later, done = lax.optimization_barrier((later, done))
    return (later,) + tuple(done)


def add_swapped(keep, send, axes, bit):
    return keep.astype(F32) + swap(send, axes, bit).astype(F32)


def halves(v):
    return jnp.split(v, 2, axis=-1)


def lanes_of(shape):
    return lax.broadcasted_iota(jnp.int32, shape, len(shape) - 1)


def head_sums(v, head):
    width = v.shape[-1]
    row = lax.broadcasted_iota(jnp.int32, (width, width), 0) // head
    col = lax.broadcasted_iota(jnp.int32, (width, width), 1) // head
    ones = jnp.where(row == col, 1.0, 0.0).astype(BF16)
    high = v.astype(BF16)
    return nn(high, ones) + nn((v - high.astype(F32)).astype(BF16), ones)


def swap_halves(v, head):
    width, half = v.shape[-1], head // 2
    low = (lanes_of(v.shape) % head) < half
    return jnp.where(low, pltpu.roll(v, width - half, 1), pltpu.roll(v, half, 1))


def rope_prep(v, gain, cosine, sine, head):
    factor = lax.rsqrt(head_sums(v * v, head) * (1.0 / head) + EPSILON)
    n = v * factor * gain
    return n * cosine + swap_halves(n, head) * sine


def project_qkv(xa, w, slot, n):
    cols = w[0].shape[-1]
    return sum(nt(xa[:, e * cols : (e + 1) * cols], piece(w, slot, e)[:n]) for e in range(4))


def piece(w, slot, e):
    return w[e % 2][(e // 2) * 2 + slot]


def qkv_kernel(head, slot, *refs):
    xa, w = refs[:4], refs[4:6]
    cosine, sine, q_gain, k_gain, low = refs[6:]
    n = low.shape[-1]
    width = 2 * head
    for i in range(4):
        proj = project_qkv(xa[i], w, slot, n)
        q = rope_prep(proj[:, :width], q_gain[...], cosine[i], sine[i], head)
        kv = proj[:, width:]
        k = rope_prep(kv, k_gain[...], cosine[i], sine[i], head)
        low[i, :, :width] = q.astype(BF16)
        low[i, :, width:] = jnp.where(lanes_of(kv.shape) < head, k, kv).astype(BF16)


def qkv_call(xa, w, slot, cosine, sine, q_gain, k_gain, head):
    rows, n = xa[0].shape[0], w[1].shape[1]
    return pl.pallas_call(
        functools.partial(qkv_kernel, head, slot),
        out_shape=jax.ShapeDtypeStruct((4, rows, n), BF16),
        compiler_params=params(),
        cost_estimate=NO_COST,
        name="qkv",
    )(*xa, *w, cosine, sine, q_gain, k_gain)


def stack_heads(v, head, scale=None):
    out = jnp.concatenate([v[:, :head], v[:, head : 2 * head]], axis=0)
    return out if scale is None else (out.astype(F32) * scale).astype(BF16)


def unstack(v_t):
    rows = v_t.shape[1] // 2
    return jnp.concatenate([v_t[:, :rows], v_t[:, rows:]], axis=0).T


def attend_kernel(head, first, at, *refs):
    parts = refs[:2]
    start, context, log_total, qkv, turned = refs[2:]
    b = pl.program_id(0)
    width = 2 * head

    @pl.when(b == 0)
    def _():
        done = 0
        for part in parts:
            for i in range(part.shape[0]):
                place = pl.multiple_of(at[done] * BLOCK, BLOCK)
                qkv[pl.ds(place, BLOCK), :] = part[i]
                done += 1
        kv_t = qkv[:, width:].astype(F32).T
        row = lax.broadcasted_iota(jnp.int32, kv_t.shape, 0)
        turned[...] = jnp.where(row < head, 1.0, kv_t).astype(BF16)

    q2 = stack_heads(qkv[pl.ds(b * BLOCK, BLOCK), :width], head, head**-0.5)
    begin = start[0]
    key = lax.broadcasted_iota(jnp.int32, (BLOCK, 2 * BLOCK), 0)

    def block(j, acc, diagonal):
        s = nt(qkv[pl.ds(j * BLOCK, BLOCK), width : width + head], q2)
        allowed = key >= begin - j * BLOCK
        if diagonal:
            row = lanes_of((BLOCK, 2 * BLOCK)) % BLOCK
            allowed = allowed & (key <= row)
        p = jnp.where(allowed, jnp.exp(s), 0.0)
        return acc + nn(turned[:, pl.ds(j * BLOCK, BLOCK)], p.astype(BF16))

    acc = jnp.zeros((width, 2 * BLOCK), F32)
    acc = lax.fori_loop(first[b], b, lambda j, acc: block(j, acc, False), acc)
    acc = block(b, acc, True)
    total = acc[:1]
    context[...] = unstack(acc[head:] / total).astype(BF16)
    log_total[0] = jnp.log(total)


def attend_call(first, at, parts, start, head):
    n = parts[0].shape[-1]
    rows = sum(v.shape[0] for v in parts) * BLOCK
    blocks = rows // BLOCK
    whole = lambda shape: pl.BlockSpec(shape, lambda b, first, at: (0,) * len(shape))
    return pl.pallas_call(
        functools.partial(attend_kernel, head),
        grid_spec=pltpu.PrefetchScalarGridSpec(
            num_scalar_prefetch=2,
            grid=(blocks,),
            in_specs=[whole(v.shape) for v in parts]
            + [pl.BlockSpec((1, 1, 2 * BLOCK), lambda b, first, at: (b, 0, 0))],
            out_specs=[
                pl.BlockSpec((BLOCK, 2 * head), lambda b, first, at: (b, 0)),
                pl.BlockSpec((1, 1, 2 * BLOCK), lambda b, first, at: (b, 0, 0)),
                whole((rows, n)),
            ],
            scratch_shapes=[pltpu.VMEM((2 * head, rows), BF16)],
        ),
        out_shape=[
            jax.ShapeDtypeStruct((rows, 2 * head), BF16),
            jax.ShapeDtypeStruct((blocks, 1, 2 * BLOCK), F32),
            jax.ShapeDtypeStruct((rows, n), BF16),
        ],
        compiler_params=params(),
        cost_estimate=NO_COST,
        name="attend",
    )(first, at, *parts, start)


def attend_back_kernel(
    head, first, to, qkv, context, d_context, start, log_total, out, turned, d_key, d_value
):
    b = pl.program_id(0)
    width = 2 * head

    @pl.when(b == 0)
    def _():
        turned[...] = qkv[:, width:].astype(F32).T.astype(BF16)
        d_key[...] = jnp.zeros_like(d_key)
        d_value[...] = jnp.zeros_like(d_value)

    scale = head**-0.5
    q2 = stack_heads(qkv[pl.ds(b * BLOCK, BLOCK), :width], head, scale)
    g = d_context[...]
    g2 = stack_heads(g, head)
    begin = start[0]
    log_sum = log_total[0]
    picks = jnp.where(
        lanes_of((8, width)) // head == lax.broadcasted_iota(jnp.int32, (8, width), 0), 1.0, 0.0
    ).astype(F32)
    delta = lax.dot_general(
        picks,
        g.astype(F32) * context[...].astype(F32),
        (((1,), (1,)), ((), ())),
        preferred_element_type=F32,
        precision=lax.Precision.HIGHEST,
    )
    delta = jnp.concatenate([delta[0:1], delta[1:2]], axis=1)
    key = lax.broadcasted_iota(jnp.int32, (BLOCK, 2 * BLOCK), 0)

    def block(j, acc, diagonal):
        at = pl.ds(j * BLOCK, BLOCK)
        s = nt(qkv[at, width : width + head], q2)
        allowed = key >= begin - j * BLOCK
        if diagonal:
            row = lanes_of((BLOCK, 2 * BLOCK)) % BLOCK
            allowed = allowed & (key <= row)
        p = jnp.where(allowed, jnp.exp(s - log_sum), 0.0)
        d_p = nt(qkv[at, width + head :], g2)
        d_s = (p * (d_p - delta)).astype(BF16)
        d_value[at, :] += nn(p.astype(BF16), g2)
        d_key[at, :] += nn(d_s, q2)
        return acc + nn(turned[:, at], d_s)

    acc = jnp.zeros((width, 2 * BLOCK), F32)
    acc = lax.fori_loop(first[b], b, lambda j, acc: block(j, acc, False), acc)
    acc = block(b, acc, True)
    out[to[b], :, :width] = (unstack(acc[:head]) * scale).astype(BF16)

    @pl.when(b == pl.num_programs(0) - 1)
    def _():
        for j in range(out.shape[0]):
            at = pl.ds(j * BLOCK, BLOCK)
            out[to[j], :, width:] = jnp.concatenate([d_key[at, :], d_value[at, :]], axis=1).astype(
                BF16
            )


def attend_back_call(first, to, qkv, context, d_context, start, log_total, head):
    rows, n = qkv.shape
    blocks = rows // BLOCK
    per_block = pl.BlockSpec((BLOCK, 2 * head), lambda b, first, to: (b, 0))
    per_row = pl.BlockSpec((1, 1, 2 * BLOCK), lambda b, first, to: (b, 0, 0))
    return pl.pallas_call(
        functools.partial(attend_back_kernel, head),
        grid_spec=pltpu.PrefetchScalarGridSpec(
            num_scalar_prefetch=2,
            grid=(blocks,),
            in_specs=[
                pl.BlockSpec((rows, n), lambda b, first, to: (0, 0)),
                per_block,
                per_block,
                per_row,
                per_row,
            ],
            out_specs=pl.BlockSpec((blocks, BLOCK, n), lambda b, first, to: (0, 0, 0)),
            scratch_shapes=[
                pltpu.VMEM((2 * head, rows), BF16),
                pltpu.VMEM((rows, head), F32),
                pltpu.VMEM((rows, head), F32),
            ],
        ),
        out_shape=jax.ShapeDtypeStruct((blocks, BLOCK, n), BF16),
        compiler_params=params(),
        cost_estimate=NO_COST,
        name="attend_back",
    )(first, to, qkv, context, d_context, start, log_total)


def joined(context, at, q):
    return jnp.concatenate([context[at[q]], context[at[4 + q]]], axis=1)


def piece_of(w, q, e, cols):
    v = w[e % 2][2 * q : 2 * q + 2, :, (e // 2) * cols : (e // 2 + 1) * cols]
    return v.reshape(-1, cols)


def project_kernel(at, context, w_near, w_far, x, gain, hidden, normed):
    cols = w_near.shape[-1] // 2
    left = [joined(context, at, q) for q in range(4)]
    for e in range(4):
        to = slice(e * cols, (e + 1) * cols)
        hidden[:, to] = x[:, to] + sum(
            nn(left[q], piece_of((w_near, w_far), q, e, cols)) for q in range(4)
        )
    h = hidden[...]
    factor = lax.rsqrt(jnp.mean(h * h, axis=-1, keepdims=True) + EPSILON)
    normed[...] = (h * factor * gain[...]).astype(BF16)


def in_vmem(count):
    return [pl.BlockSpec(memory_space=pltpu.VMEM)] * count


def project_call(at, context, w, x, gain):
    rows, d = x.shape
    return pl.pallas_call(
        project_kernel,
        in_specs=[pl.BlockSpec(memory_space=pltpu.SMEM)] + in_vmem(5),
        out_shape=[jax.ShapeDtypeStruct((rows, d), F32), jax.ShapeDtypeStruct((rows, d), BF16)],
        compiler_params=params(),
        cost_estimate=NO_COST,
        name="project",
    )(at, context, w[0], w[1], x, gain)


def project_back_kernel(
    at, context, w_near, w_far, hidden, gain, dy, p0, p1, p2, p3, d_context, keep, send, d_hidden, part
):
    cols = w_near.shape[-1] // 2
    n = context.shape[-1]
    h = hidden[...]
    g = (p0[...].astype(F32) + p1[...].astype(F32)) + (p2[...].astype(F32) + p3[...].astype(F32))
    factor = lax.rsqrt(jnp.mean(h * h, axis=-1, keepdims=True) + EPSILON)
    part[...] = jnp.sum(g * h * factor, axis=0, keepdims=True)
    u = gain[...] * g
    mean = jnp.mean(u * h, axis=-1, keepdims=True)
    out = dy[...].astype(F32) + (factor * u - h * (factor * factor * factor * mean))
    d_hidden[...] = out
    low = out.astype(BF16)
    for q in range(4):
        both = sum(
            nt(low[:, e * cols : (e + 1) * cols], piece_of((w_near, w_far), q, e, cols))
            for e in range(4)
        ).astype(BF16)
        d_context[at[q]] = both[:, :n]
        d_context[at[4 + q]] = both[:, n:]
    for q in range(4):
        grad = tn(joined(context, at, q), low).astype(BF16)
        for s in (0, 1):
            rows = slice(s * n, (s + 1) * n)
            keep[2 * q + s, :, :cols] = grad[rows, :cols]
            send[2 * q + s, :, :cols] = grad[rows, cols : 2 * cols]
            keep[2 * q + s, :, cols:] = grad[rows, 2 * cols : 3 * cols]
            send[2 * q + s, :, cols:] = grad[rows, 3 * cols :]


def project_back_call(at, context, w, hidden, gain, dy, parts):
    rows, d = hidden.shape
    grad = jax.ShapeDtypeStruct(w[0].shape, BF16)
    return pl.pallas_call(
        project_back_kernel,
        in_specs=[pl.BlockSpec(memory_space=pltpu.SMEM)] + in_vmem(10),
        out_shape=[
            jax.ShapeDtypeStruct(context.shape, BF16),
            grad,
            grad,
            jax.ShapeDtypeStruct((rows, d), F32),
            jax.ShapeDtypeStruct((1, d), F32),
        ],
        compiler_params=params(),
        cost_estimate=NO_COST,
        name="project_back",
    )(at, context, w[0], w[1], hidden, gain, dy, *parts)


def qkv_back_kernel(head, *refs):
    grads, xa, w = refs[:2], refs[2:6], refs[6:8]
    cosine, sine, q_gain, k_gain, a_gain = refs[8:13]
    d_xa, (keep, send, parts, a_part) = refs[13:17], refs[17:]
    n = keep.shape[1]
    width = 2 * head
    cols = w[0].shape[-1]

    def back(g, v, gain, i):
        e = g * cosine[i] - swap_halves(g, head) * sine[i]
        m = lax.rsqrt(head_sums(v * v, head) * (1.0 / head) + EPSILON)
        u = gain * e
        mean = head_sums(u * v, head) * (1.0 / head)
        return m * u - v * (m * m * m * mean), jnp.sum(e * v * m, axis=0, keepdims=True)

    lows = []
    q_sum = k_sum = 0.0
    for slot in (0, 1):
        for i in range(4):
            v, g = project_qkv(xa[i], w, slot, n), grads[slot][i].astype(F32)
            d_q, part = back(g[:, :width], v[:, :width], q_gain[...], i)
            q_sum += part
            d_k, part = back(g[:, width:], v[:, width:], k_gain[...], i)
            k_sum += part
            d_kv = jnp.where(lanes_of(d_k.shape) < head, d_k, g[:, width:])
            lows.append(jnp.concatenate([d_q, d_kv], axis=1).astype(BF16))
    for e in range(4):
        at = slice(e * cols, (e + 1) * cols)
        to = slice((e // 2) * cols, (e // 2 + 1) * cols)
        total = 0.0
        for i in range(4):
            here = nn(lows[i], piece(w, 0, e)[:n]) + nn(lows[4 + i], piece(w, 1, e)[:n])
            d_xa[i][:, at] = here.astype(BF16)
            total += jnp.sum(here * xa[i][:, at].astype(F32), axis=0, keepdims=True)
        a_part[:, at] = total / a_gain[:, at]
        for slot in (0, 1):
            here = sum(tn(lows[slot * 4 + i], xa[i][:, at]) for i in range(4))
            (keep, send)[e % 2][slot, :, to] = here.astype(BF16)
    parts[0:1] = q_sum
    parts[1:2] = k_sum


def qkv_back_call(grads, xa, w, cosine, sine, gains, head):
    rows, d = xa[0].shape
    n = w[1].shape[1]
    half = jax.ShapeDtypeStruct((2, n, d // 2), BF16)
    return pl.pallas_call(
        functools.partial(qkv_back_kernel, head),
        out_shape=[jax.ShapeDtypeStruct((rows, d), BF16)] * 4
        + [half, half]
        + [jax.ShapeDtypeStruct((2, 2 * head), F32), jax.ShapeDtypeStruct((1, d), F32)],
        compiler_params=params(),
        cost_estimate=NO_COST,
        name="qkv_back",
    )(*grads, *xa, *w, cosine, sine, *gains)


def ffn_kernel(count, *refs):
    xf, dy, w = refs[:count], refs[count : 2 * count], refs[2 * count : 2 * count + 16]
    refs = refs[2 * count + 16 :]
    cols = w[0].shape[-1]

    def piece(slot, e, which):
        return w[e][which] if slot == 0 else w[4 + 4 * which + e][...]

    def wide(v, slot, which):
        return sum(nt(v[:, e * cols : (e + 1) * cols], piece(slot, e, which)) for e in range(4))

    for i in range(count):
        acts, out, d_xf = refs[3 * i : 3 * i + 3]
        for slot in (0, 1):
            gate, up = wide(xf[i], slot, 0), wide(xf[i], slot, 1)
            d_act = wide(dy[i], slot, 2).astype(BF16).astype(F32)
            sig = 1.0 / (1.0 + jnp.exp(-gate))
            silu = gate * sig
            acts[2, slot] = (silu * up).astype(BF16)
            acts[0, slot] = (d_act * up * (sig * (1.0 + gate * (1.0 - sig)))).astype(BF16)
            acts[1, slot] = (d_act * silu).astype(BF16)
        for e in range(4):
            at = slice(e * cols, (e + 1) * cols)
            d_xf[:, at] = sum(
                nn(acts[k, slot], piece(slot, e, k)) for slot in (0, 1) for k in (0, 1)
            ).astype(BF16)
        for e in range(4):
            at = slice(e * cols, (e + 1) * cols)
            out[:, at] = sum(nn(acts[2, slot], piece(slot, e, 2)) for slot in (0, 1)).astype(BF16)


def ffn_call(xf, dy, w):
    count, (rows, d) = len(xf), xf[0].shape
    units = w[0].shape[1]
    tokens = jax.ShapeDtypeStruct((rows, d), BF16)
    return pl.pallas_call(
        functools.partial(ffn_kernel, count),
        out_shape=[jax.ShapeDtypeStruct((3, 2, rows, units), BF16), tokens, tokens] * count,
        compiler_params=params(),
        cost_estimate=NO_COST,
        name="ffn",
    )(*xf, *dy, *w)


def ffn_grad_kernel(*refs):
    acts, xf, dy = refs[:4], refs[4:8], refs[8:12]
    keep, send = refs[12:]
    cols = keep.shape[-1] // 2

    def write(right):
        for e in range(4):
            at = slice(e * cols, (e + 1) * cols)
            here = sum(tn(acts[b][0, 0], right[b][:, at]) for b in range(4)).astype(BF16)
            to = slice((e // 2) * cols, (e // 2 + 1) * cols)
            (keep, send)[e % 2][0, :, to] = here

    pl.when(pl.program_id(0) < 2)(lambda: write(xf))
    pl.when(pl.program_id(0) == 2)(lambda: write(dy))


def ffn_grad_call(acts, xf, dy, slot):
    three, _, rows, units = acts[0].shape
    d = xf[0].shape[1]
    by_kind = pl.BlockSpec((1, 1, rows, units), lambda k: (k, slot, 0, 0))
    half = pl.BlockSpec((1, units, d // 2), lambda k: (k, 0, 0))
    out = jax.ShapeDtypeStruct((three, units, d // 2), BF16)
    return pl.pallas_call(
        ffn_grad_kernel,
        grid=(three,),
        in_specs=[by_kind] * 4 + [pl.BlockSpec((rows, d), lambda k: (0, 0))] * 8,
        out_specs=[half, half],
        out_shape=[out, out],
        compiler_params=params(),
        cost_estimate=NO_COST,
        name="ffn_grad",
    )(*acts, *xf, *dy)


def norm_factor(v):
    return lax.rsqrt(jnp.mean(v * v, axis=-1, keepdims=True) + EPSILON)


def norm_back(v, factor, gain, grad):
    u = gain * grad
    part = jnp.sum(grad * v * factor, axis=0)
    mean = jnp.mean(u * v, axis=-1, keepdims=True)
    return factor * u - v * (factor * factor * factor * mean), part


def per_device(
    tokens,
    segment_ids,
    cotangent,
    attn_gain,
    query_weight,
    key_weight,
    value_weight,
    output_weight,
    query_gain,
    key_gain,
    ffn_gain,
    gate_weight,
    up_weight,
    down_weight,
):
    y, c, zh = lax.axis_index("y"), lax.axis_index("c"), lax.axis_index("zh")
    near = lax.axis_index(NEAR)
    head = query_gain.shape[0]
    rows = tokens.shape[0]
    nq, nk = query_weight.shape[1], key_weight.shape[1]
    n = nq + 2 * nk

    x = own_order(tokens, y, c).astype(F32)
    gain_a = own_order(attn_gain[None], y, c)
    gain_f = own_order(ffn_gain[None], y, c)
    gain_q = jnp.concatenate([query_gain, query_gain])[None]
    gain_k = jnp.concatenate([key_gain, key_gain])[None]
    x_factor = norm_factor(x)
    xa = (x * x_factor * gain_a).astype(BF16)
    shard = gather_runs(
        jnp.concatenate([query_weight.T, key_weight.T, value_weight.T, output_weight], axis=0)
    )
    ffn_own = gather_runs(jnp.stack([gate_weight.T, up_weight.T, down_weight]))
    xa_near = [xa, swap(xa, NEAR, 1), swap(xa, NEAR, 2)]
    shard_far = swap(shard, "zh", 1)
    heads = jnp.stack([shard, shard_far, swap(shard, "y", 1), swap(shard_far, "y", 1)])
    qkv_w = (heads, swap(heads[:, :n], "c", 1))
    gate_far = swap(ffn_own[0], "zh", 1)
    (xa_near, ffn_own), gate_far, qkv_w = after((xa_near, ffn_own), gate_far, qkv_w)
    xa_near.append(swap(xa_near[2], NEAR, 1))
    up_far = swap(ffn_own[1], "zh", 1)
    (ffn_own, xa_near, gate_far, qkv_w), up_far = after((ffn_own, xa_near, gate_far, qkv_w), up_far)

    segment = segment_ids[0]
    total_rows = segment.shape[0]
    index = jnp.arange(total_rows, dtype=jnp.int32)
    opens = jnp.concatenate([jnp.ones((1,), dtype=jnp.bool_), segment[1:] != segment[:-1]])
    begin = lax.cummax(jnp.where(opens, index, 0), axis=0)
    blocks = total_rows // BLOCK
    first = begin[::BLOCK] // BLOCK
    by_block = begin.reshape(blocks, 1, BLOCK)
    start = jnp.concatenate([by_block, by_block], axis=2)
    four = jnp.arange(4, dtype=jnp.int32) ^ near
    position = lax.dynamic_slice_in_dim(index - begin, zh * 4 * rows, 4 * rows).astype(F32)
    inverse = ROPE_BASE ** (-(jnp.arange(head // 2, dtype=F32) * 2.0) / head)
    angle = (position[:, None] * inverse[None, :]).reshape(4, rows, head // 2)[four]
    cos_half, sin_half = jnp.cos(angle), jnp.sin(angle)
    cosine = jnp.concatenate([cos_half] * 4, axis=2)
    sine = jnp.concatenate([-sin_half, sin_half] * 2, axis=2)
    eight = jnp.arange(8, dtype=jnp.int32)
    places = jnp.concatenate([zh * 4 + four, (1 - zh) * 4 + four]).astype(jnp.int32)

    other = qkv_call(xa_near, qkv_w, 1, cosine, sine, gain_q, gain_k, head)
    (cotangent, ffn_own, gate_far, up_far), other = after(
        (cotangent, ffn_own, gate_far, up_far), other
    )
    dy = own_order(cotangent, y, c)
    got = swap(other, "zh", 1)
    dy_near = [dy, swap(dy, NEAR, 1), swap(dy, NEAR, 2)]
    own_y = swap(ffn_own, "y", 1)
    own = qkv_call(xa_near, qkv_w, 0, cosine, sine, gain_q, gain_k, head)
    (dy_near, ffn_own, gate_far, up_far, heads), own, got, own_y = after(
        (dy_near, ffn_own, gate_far, up_far, qkv_w[0]), own, got, own_y
    )

    context, log_total, qkv = attend_call(first, places, (own, got), start, head)
    down_far = swap(ffn_own[2], "zh", 1)
    out_w = jnp.concatenate([heads[:2, n:], heads[2:, n:]], axis=-1)
    out_w = [out_w] + [swap(out_w, NEAR, bit) for bit in (1, 2, 3)]
    gate_y = swap(gate_far, "y", 1)
    (dy_near, ffn_own, own_y, gate_far, up_far), context, down_far, gate_y, out_w = after(
        (dy_near, ffn_own, own_y, gate_far, up_far), context, down_far, gate_y, out_w
    )

    def to_heads(v):
        return lax.all_to_all(v, TENSOR, 0, 0, tiled=True)

    context_rows = to_heads(context.reshape(-1, rows, nq))
    dy_near.append(swap(dy_near[2], NEAR, 1))
    up_y, down_y = swap(up_far, "y", 1), swap(down_far, "y", 1)
    out_w = jnp.stack(out_w)
    out_w = [v.reshape((8,) + v.shape[2:]) for v in (out_w, swap(out_w, "c", 1))]
    w = [ffn_own, own_y, gate_far, gate_y, up_far, up_y, down_far, down_y]
    own_c, own_yc = swap(ffn_own, "c", 1), swap(own_y, "c", 1)
    w, context_rows, dy_near, own_c, own_yc, out_w = after(
        w, context_rows, dy_near, own_c, own_yc, out_w
    )

    hidden, xf = project_call(places, context_rows, out_w, x, gain_f)
    ffn_w = [w[0], own_c, w[1], own_yc]
    for k in (0, 1, 2):
        far, far_y = w[2 + 2 * k : 4 + 2 * k]
        ffn_w += [far, swap(far, "c", 1), far_y, swap(far_y, "c", 1)]

    xf_near = [xf] + [swap(xf, NEAR, bit) for bit in (1, 2, 3)]
    acts_0, out_0, d_xf_0 = ffn_call(xf_near[:1], dy_near[:1], ffn_w)
    acts_1, out_1, d_xf_1, acts_2, out_2, d_xf_2 = ffn_call(xf_near[1:3], dy_near[1:3], ffn_w)
    acts_3, out_3, d_xf_3 = ffn_call(xf_near[3:], dy_near[3:], ffn_w)
    d_xf = [d_xf_0, swap(d_xf_1, NEAR, 1), swap(d_xf_2, NEAR, 2), swap(d_xf_3, NEAR, 3)]
    acts = [acts_0, acts_1, acts_2, acts_3]
    keep_1, send_1 = ffn_grad_call(acts, xf_near, dy_near, 1)
    keep_0, send_0 = ffn_grad_call(acts, xf_near, dy_near, 0)
    (out_0, out_1, out_2, out_3), d_xf, keep_1, send_1, keep_0, send_0 = after(
        (out_0, out_1, out_2, out_3), d_xf, keep_1, send_1, keep_0, send_0
    )

    d_context_rows, out_keep, out_send, d_hidden, ffn_gain_part = project_back_call(
        places, context_rows, out_w, hidden, gain_f, dy, d_xf
    )
    d_context = to_heads(d_context_rows).reshape(total_rows, nq)
    ffn_1 = add_swapped(keep_1, send_1, "c", 1).astype(BF16)
    gate_1 = add_swapped(*halves(ffn_1[0]), "y", 1).astype(BF16)
    out_grad = add_swapped(out_keep, out_send, "c", 1).astype(BF16)
    (out_1, out_2, out_3, keep_0, ffn_1), d_context, gate_1, out_grad = after(
        (out_1, out_2, out_3, keep_0, ffn_1), d_context, gate_1, out_grad
    )

    place = jnp.where(eight // 4 == zh, 4, 0) + ((eight % 4) ^ near)
    d_qkv = attend_back_call(
        first, place.astype(jnp.int32), qkv, context, d_context, start, log_total, head
    )
    up_1 = add_swapped(*halves(ffn_1[1]), "y", 1).astype(BF16)
    gate_part = swap(gate_1, "zh", 1)
    ffn_out = [out_0, swap(out_1, NEAR, 1), swap(out_2, NEAR, 2)]
    (ffn_1, out_3, out_grad, keep_0), d_qkv, up_1, gate_part, *ffn_out = after(
        (ffn_1, out_3, out_grad, keep_0), d_qkv, up_1, gate_part, *ffn_out
    )

    got = swap(d_qkv[:4], "zh", 1)
    ffn_0 = add_swapped(keep_0, send_0, "c", 1).astype(BF16)
    out_grad = out_grad.reshape((4, 2) + out_grad.shape[1:])
    out_grad = out_grad[0].astype(F32) + sum(
        swap(out_grad[bit], NEAR, bit).astype(F32) for bit in (1, 2, 3)
    )
    (ffn_1, up_1, out_3, d_qkv), got, ffn_0, out_grad = after(
        (ffn_1, up_1, out_3, d_qkv), got, ffn_0, out_grad.astype(BF16)
    )

    gains = (gain_q, gain_k, gain_a)
    xa = [xa_near[b] for b in (3, 1)]
    *d_xa, qkv_keep, qkv_send, head_parts, attn_gain_part = qkv_back_call(
        (d_qkv[4:], got), xa_near, qkv_w, cosine, sine, gains, head
    )
    out_grad = add_swapped(*halves(out_grad), "y", 1)
    down_1 = add_swapped(*halves(ffn_1[2]), "y", 1).astype(BF16)
    up_down = jnp.stack([up_1, down_1])
    (up_down, ffn_0, out_3), d_xa, qkv_send, out_grad, attn_gain_part = after(
        (up_down, ffn_0, out_3), d_xa, qkv_send, out_grad, attn_gain_part
    )

    d_xa = [d_xa[0]] + [swap(d_xa[bit], NEAR, bit) for bit in (1, 2, 3)]
    qkv_grad = add_swapped(qkv_keep, qkv_send, "c", 1).astype(BF16)
    qkv_grad = add_swapped(*halves(qkv_grad), "y", 1)
    up_down = swap(up_down, "zh", 1)
    ffn_0 = add_swapped(*halves(ffn_0), "y", 1)
    (out_grad, out_3, attn_gain_part), d_xa, up_down, qkv_grad, ffn_0 = after(
        (out_grad, out_3, attn_gain_part), d_xa, up_down, qkv_grad, ffn_0
    )

    heads_grad = jnp.concatenate([qkv_grad, out_grad], axis=1)
    heads_grad = add_swapped(heads_grad[0], heads_grad[1].astype(BF16), "zh", 1)
    qkv_grad, out_grad = heads_grad[:n], heads_grad[n:]
    ffn_out.append(swap(out_3, NEAR, 3))
    d = x.shape[1]
    gains = total_of(
        jnp.concatenate(
            [
                arrays_order(attn_gain_part, y, c)[0],
                arrays_order(ffn_gain_part, y, c)[0],
                head_parts[0, :head] + head_parts[0, head:],
                head_parts[1, :head],
            ]
        ).reshape(-1, 128)
    ).reshape(-1)
    d_xa = sum(v.astype(F32) for v in d_xa)
    x_back, _ = norm_back(x, x_factor, gain_a, d_xa)
    input_grad = arrays_order((d_hidden + x_back).astype(BF16), y, c)
    block_out = arrays_order((hidden + sum(v.astype(F32) for v in ffn_out)).astype(BF16), y, c)
    qkv_grad = scatter_runs(qkv_grad)
    out_grad = scatter_runs(out_grad)
    ffn_grad = [
        scatter_runs(ffn_0[k] + part.astype(F32))
        for k, part in enumerate((gate_part, up_down[0], up_down[1]))
    ]

    return (
        block_out,
        input_grad,
        gains[:d],
        qkv_grad[:nq].T,
        qkv_grad[nq : nq + nk].T,
        qkv_grad[nq + nk :].T,
        out_grad,
        gains[2 * d : 2 * d + head],
        gains[2 * d + head :],
        gains[d : 2 * d],
        ffn_grad[0].T,
        ffn_grad[1].T,
        ffn_grad[2],
    )


def solution(mesh):
    dp, tensor = mesh.shape["dp"], mesh.shape["tensor"]
    cut = Mesh(
        mesh.devices.reshape(dp // 4, 2, 2, tensor // 4, 2, 2), ("r", "y", "c", "zh", "zl", "x")
    )
    data, model = ("r", "y", "c"), TENSOR
    both = data + model
    rows, wide, tall = P(both, None), P(data, model), P(model, data)
    in_specs = (
        rows, P(data, None), rows, P(), wide, wide, wide, tall, P(), P(), P(), wide, wide, tall
    )
    out_specs = (
        rows, rows, P(), wide, wide, wide, tall, P(), P(), P(), wide, wide, tall
    )
    return jax.shard_map(
        per_device, mesh=cut, in_specs=in_specs, out_specs=out_specs, check_vma=False
    )
```

```python
import functools

import jax
import jax.numpy as jnp
from jax import lax
from jax.experimental import pallas as pl
from jax.experimental.pallas import tpu as pltpu
from jax.sharding import Mesh
from jax.sharding import PartitionSpec as P

EPSILON = 1e-05
ROPE_BASE = 1000000.0
BLOCK = 256
F32 = jnp.float32
BF16 = jnp.bfloat16
VMEM_LIMIT = 40 * 1024 * 1024
NO_COST = pl.CostEstimate(flops=0, bytes_accessed=0, transcendentals=0)

NEAR = ("zl", "x")
TENSOR = ("zh", "zl", "x")


def nn(a, b):
    return lax.dot_general(a, b, (((1,), (0,)), ((), ())), preferred_element_type=F32)


def nt(a, b):
    return lax.dot_general(a, b, (((1,), (1,)), ((), ())), preferred_element_type=F32)


def tn(a, b):
    return lax.dot_general(a, b, (((0,), (0,)), ((), ())), preferred_element_type=F32)


def params(**more):
    return pltpu.CompilerParams(vmem_limit_bytes=VMEM_LIMIT, **more)


def swap(v, axes, bit):
    size = lax.axis_size(axes)
    return lax.ppermute(v, axes, [(i, i ^ bit) for i in range(size)])


def quads(v):
    return jnp.split(v, 4, axis=-1)


def own_order(v, y, c):
    runs = lax.axis_size("r")
    if runs > 1:
        lead = v.shape[:-1]
        v = jnp.moveaxis(v.reshape(lead + (runs, 4, -1)), -3, -2).reshape(lead + (-1,))
    return exchange(v, y, c)


def exchange(v, y, c):
    a = quads(v)
    a = [jnp.where(c == 0, a[e], a[e ^ 1]) for e in range(4)]
    return jnp.concatenate([jnp.where(y == 0, a[e], a[e ^ 2]) for e in range(4)], axis=-1)


def arrays_order(v, y, c):
    v = exchange(v, y, c)
    runs = lax.axis_size("r")
    if runs > 1:
        lead = v.shape[:-1]
        v = jnp.moveaxis(v.reshape(lead + (4, runs, -1)), -2, -3).reshape(lead + (-1,))
    return v


def gather_runs(v):
    return lax.all_gather(v, "r", axis=v.ndim - 1, tiled=True) if lax.axis_size("r") > 1 else v


def scatter_runs(v):
    if lax.axis_size("r") == 1:
        return v
    return lax.psum_scatter(
        v.astype(BF16), "r", scatter_dimension=v.ndim - 1, tiled=True
    ).astype(F32)


def total_of(v):
    if lax.axis_size("r") > 1:
        v = lax.psum(v, "r")
    axes = ("y", "c") + TENSOR
    every = jnp.broadcast_to(v[None], (lax.axis_size(axes),) + v.shape)
    return jnp.sum(lax.all_to_all(every, axes, 0, 0, tiled=True), axis=0)


def after(later, *done):
    later, done = lax.optimization_barrier((later, done))
    return (later,) + tuple(done)


def add_swapped(keep, send, axes, bit):
    return keep.astype(F32) + swap(send, axes, bit).astype(F32)


def halves(v):
    return jnp.split(v, 2, axis=-1)


def lanes_of(shape):
    return lax.broadcasted_iota(jnp.int32, shape, len(shape) - 1)


def head_sums(v, head):
    width = v.shape[-1]
    row = lax.broadcasted_iota(jnp.int32, (width, width), 0) // head
    col = lax.broadcasted_iota(jnp.int32, (width, width), 1) // head
    ones = jnp.where(row == col, 1.0, 0.0).astype(BF16)
    high = v.astype(BF16)
    return nn(high, ones) + nn((v - high.astype(F32)).astype(BF16), ones)


def swap_halves(v, head):
    width, half = v.shape[-1], head // 2
    low = (lanes_of(v.shape) % head) < half
    return jnp.where(low, pltpu.roll(v, width - half, 1), pltpu.roll(v, half, 1))


def rope_prep(v, gain, cosine, sine, head):
    factor = lax.rsqrt(head_sums(v * v, head) * (1.0 / head) + EPSILON)
    n = v * factor * gain
    return n * cosine + swap_halves(n, head) * sine


def project_qkv(xa, w, slot, n):
    cols = w[0].shape[-1]
    return sum(nt(xa[:, e * cols : (e + 1) * cols], piece(w, slot, e)[:n]) for e in range(4))


def piece(w, slot, e):
    return w[e % 2][(e // 2) * 2 + slot]


def qkv_kernel(head, slot, *refs):
    xa, w = refs[:4], refs[4:6]
    cosine, sine, q_gain, k_gain, low = refs[6:]
    n = low.shape[-1]
    width = 2 * head
    for i in range(4):
        proj = project_qkv(xa[i], w, slot, n)
        q = rope_prep(proj[:, :width], q_gain[...], cosine[i], sine[i], head)
        kv = proj[:, width:]
        k = rope_prep(kv, k_gain[...], cosine[i], sine[i], head)
        low[i, :, :width] = q.astype(BF16)
        low[i, :, width:] = jnp.where(lanes_of(kv.shape) < head, k, kv).astype(BF16)


def qkv_call(xa, w, slot, cosine, sine, q_gain, k_gain, head):
    rows, n = xa[0].shape[0], w[1].shape[1]
    return pl.pallas_call(
        functools.partial(qkv_kernel, head, slot),
        out_shape=jax.ShapeDtypeStruct((4, rows, n), BF16),
        compiler_params=params(),
        cost_estimate=NO_COST,
        name="qkv",
    )(*xa, *w, cosine, sine, q_gain, k_gain)


def stack_heads(v, head, scale=None):
    out = jnp.concatenate([v[:, :head], v[:, head : 2 * head]], axis=0)
    return out if scale is None else (out.astype(F32) * scale).astype(BF16)


def unstack(v_t):
    rows = v_t.shape[1] // 2
    return jnp.concatenate([v_t[:, :rows], v_t[:, rows:]], axis=0).T


def attend_kernel(head, first, at, *refs):
    parts = refs[:2]
    start, context, log_total, qkv, turned = refs[2:]
    b = pl.program_id(0)
    width = 2 * head

    @pl.when(b == 0)
    def _():
        done = 0
        for part in parts:
            for i in range(part.shape[0]):
                place = pl.multiple_of(at[done] * BLOCK, BLOCK)
                qkv[pl.ds(place, BLOCK), :] = part[i]
                done += 1
        kv_t = qkv[:, width:].astype(F32).T
        row = lax.broadcasted_iota(jnp.int32, kv_t.shape, 0)
        turned[...] = jnp.where(row < head, 1.0, kv_t).astype(BF16)

    q2 = stack_heads(qkv[pl.ds(b * BLOCK, BLOCK), :width], head, head**-0.5)
    begin = start[0]
    key = lax.broadcasted_iota(jnp.int32, (BLOCK, 2 * BLOCK), 0)

    def block(j, acc, diagonal):
        s = nt(qkv[pl.ds(j * BLOCK, BLOCK), width : width + head], q2)
        allowed = key >= begin - j * BLOCK
        if diagonal:
            row = lanes_of((BLOCK, 2 * BLOCK)) % BLOCK
            allowed = allowed & (key <= row)
        p = jnp.where(allowed, jnp.exp(s), 0.0)
        return acc + nn(turned[:, pl.ds(j * BLOCK, BLOCK)], p.astype(BF16))

    acc = jnp.zeros((width, 2 * BLOCK), F32)
    acc = lax.fori_loop(first[b], b, lambda j, acc: block(j, acc, False), acc)
    acc = block(b, acc, True)
    total = acc[:1]
    context[...] = unstack(acc[head:] / total).astype(BF16)
    log_total[0] = jnp.log(total)


def attend_call(first, at, parts, start, head):
    n = parts[0].shape[-1]
    rows = sum(v.shape[0] for v in parts) * BLOCK
    blocks = rows // BLOCK
    whole = lambda shape: pl.BlockSpec(shape, lambda b, first, at: (0,) * len(shape))
    return pl.pallas_call(
        functools.partial(attend_kernel, head),
        grid_spec=pltpu.PrefetchScalarGridSpec(
            num_scalar_prefetch=2,
            grid=(blocks,),
            in_specs=[whole(v.shape) for v in parts]
            + [pl.BlockSpec((1, 1, 2 * BLOCK), lambda b, first, at: (b, 0, 0))],
            out_specs=[
                pl.BlockSpec((BLOCK, 2 * head), lambda b, first, at: (b, 0)),
                pl.BlockSpec((1, 1, 2 * BLOCK), lambda b, first, at: (b, 0, 0)),
                whole((rows, n)),
            ],
            scratch_shapes=[pltpu.VMEM((2 * head, rows), BF16)],
        ),
        out_shape=[
            jax.ShapeDtypeStruct((rows, 2 * head), BF16),
            jax.ShapeDtypeStruct((blocks, 1, 2 * BLOCK), F32),
            jax.ShapeDtypeStruct((rows, n), BF16),
        ],
        compiler_params=params(),
        cost_estimate=NO_COST,
        name="attend",
    )(first, at, *parts, start)


def attend_back_kernel(
    head, first, to, qkv, context, d_context, start, log_total, out, turned, d_key, d_value
):
    b = pl.program_id(0)
    width = 2 * head

    @pl.when(b == 0)
    def _():
        turned[...] = qkv[:, width:].astype(F32).T.astype(BF16)
        d_key[...] = jnp.zeros_like(d_key)
        d_value[...] = jnp.zeros_like(d_value)

    scale = head**-0.5
    q2 = stack_heads(qkv[pl.ds(b * BLOCK, BLOCK), :width], head, scale)
    g = d_context[...]
    g2 = stack_heads(g, head)
    begin = start[0]
    log_sum = log_total[0]
    picks = jnp.where(
        lanes_of((8, width)) // head == lax.broadcasted_iota(jnp.int32, (8, width), 0), 1.0, 0.0
    ).astype(F32)
    delta = lax.dot_general(
        picks,
        g.astype(F32) * context[...].astype(F32),
        (((1,), (1,)), ((), ())),
        preferred_element_type=F32,
        precision=lax.Precision.HIGHEST,
    )
    delta = jnp.concatenate([delta[0:1], delta[1:2]], axis=1)
    key = lax.broadcasted_iota(jnp.int32, (BLOCK, 2 * BLOCK), 0)

    def block(j, acc, diagonal):
        at = pl.ds(j * BLOCK, BLOCK)
        s = nt(qkv[at, width : width + head], q2)
        allowed = key >= begin - j * BLOCK
        if diagonal:
            row = lanes_of((BLOCK, 2 * BLOCK)) % BLOCK
            allowed = allowed & (key <= row)
        p = jnp.where(allowed, jnp.exp(s - log_sum), 0.0)
        d_p = nt(qkv[at, width + head :], g2)
        d_s = (p * (d_p - delta)).astype(BF16)
        d_value[at, :] += nn(p.astype(BF16), g2)
        d_key[at, :] += nn(d_s, q2)
        return acc + nn(turned[:, at], d_s)

    acc = jnp.zeros((width, 2 * BLOCK), F32)
    acc = lax.fori_loop(first[b], b, lambda j, acc: block(j, acc, False), acc)
    acc = block(b, acc, True)
    out[to[b], :, :width] = (unstack(acc[:head]) * scale).astype(BF16)

    @pl.when(b == pl.num_programs(0) - 1)
    def _():
        for j in range(out.shape[0]):
            at = pl.ds(j * BLOCK, BLOCK)
            out[to[j], :, width:] = jnp.concatenate([d_key[at, :], d_value[at, :]], axis=1).astype(
                BF16
            )


def attend_back_call(first, to, qkv, context, d_context, start, log_total, head):
    rows, n = qkv.shape
    blocks = rows // BLOCK
    per_block = pl.BlockSpec((BLOCK, 2 * head), lambda b, first, to: (b, 0))
    per_row = pl.BlockSpec((1, 1, 2 * BLOCK), lambda b, first, to: (b, 0, 0))
    return pl.pallas_call(
        functools.partial(attend_back_kernel, head),
        grid_spec=pltpu.PrefetchScalarGridSpec(
            num_scalar_prefetch=2,
            grid=(blocks,),
            in_specs=[
                pl.BlockSpec((rows, n), lambda b, first, to: (0, 0)),
                per_block,
                per_block,
                per_row,
                per_row,
            ],
            out_specs=pl.BlockSpec((blocks, BLOCK, n), lambda b, first, to: (0, 0, 0)),
            scratch_shapes=[
                pltpu.VMEM((2 * head, rows), BF16),
                pltpu.VMEM((rows, head), F32),
                pltpu.VMEM((rows, head), F32),
            ],
        ),
        out_shape=jax.ShapeDtypeStruct((blocks, BLOCK, n), BF16),
        compiler_params=params(),
        cost_estimate=NO_COST,
        name="attend_back",
    )(first, to, qkv, context, d_context, start, log_total)


def joined(context, at, q):
    return jnp.concatenate([context[at[q]], context[at[4 + q]]], axis=1)


def piece_of(w, q, e, cols):
    v = w[e % 2][2 * q : 2 * q + 2, :, (e // 2) * cols : (e // 2 + 1) * cols]
    return v.reshape(-1, cols)


def project_kernel(at, context, w_near, w_far, x, gain, hidden, normed):
    cols = w_near.shape[-1] // 2
    left = [joined(context, at, q) for q in range(4)]
    for e in range(4):
        to = slice(e * cols, (e + 1) * cols)
        hidden[:, to] = x[:, to] + sum(
            nn(left[q], piece_of((w_near, w_far), q, e, cols)) for q in range(4)
        )
    h = hidden[...]
    factor = lax.rsqrt(jnp.mean(h * h, axis=-1, keepdims=True) + EPSILON)
    normed[...] = (h * factor * gain[...]).astype(BF16)


def in_vmem(count):
    return [pl.BlockSpec(memory_space=pltpu.VMEM)] * count


def project_call(at, context, w, x, gain):
    rows, d = x.shape
    return pl.pallas_call(
        project_kernel,
        in_specs=[pl.BlockSpec(memory_space=pltpu.SMEM)] + in_vmem(5),
        out_shape=[jax.ShapeDtypeStruct((rows, d), F32), jax.ShapeDtypeStruct((rows, d), BF16)],
        compiler_params=params(),
        cost_estimate=NO_COST,
        name="project",
    )(at, context, w[0], w[1], x, gain)


def project_back_kernel(
    at, context, w_near, w_far, hidden, gain, dy, p0, p1, p2, p3, d_context, keep, send, d_hidden, part
):
    cols = w_near.shape[-1] // 2
    n = context.shape[-1]
    h = hidden[...]
    g = (p0[...].astype(F32) + p1[...].astype(F32)) + (p2[...].astype(F32) + p3[...].astype(F32))
    factor = lax.rsqrt(jnp.mean(h * h, axis=-1, keepdims=True) + EPSILON)
    part[...] = jnp.sum(g * h * factor, axis=0, keepdims=True)
    u = gain[...] * g
    mean = jnp.mean(u * h, axis=-1, keepdims=True)
    out = dy[...].astype(F32) + (factor * u - h * (factor * factor * factor * mean))
    d_hidden[...] = out
    low = out.astype(BF16)
    for q in range(4):
        both = sum(
            nt(low[:, e * cols : (e + 1) * cols], piece_of((w_near, w_far), q, e, cols))
            for e in range(4)
        ).astype(BF16)
        d_context[at[q]] = both[:, :n]
        d_context[at[4 + q]] = both[:, n:]
    for q in range(4):
        grad = tn(joined(context, at, q), low).astype(BF16)
        for s in (0, 1):
            rows = slice(s * n, (s + 1) * n)
            keep[2 * q + s, :, :cols] = grad[rows, :cols]
            send[2 * q + s, :, :cols] = grad[rows, cols : 2 * cols]
            keep[2 * q + s, :, cols:] = grad[rows, 2 * cols : 3 * cols]
            send[2 * q + s, :, cols:] = grad[rows, 3 * cols :]


def project_back_call(at, context, w, hidden, gain, dy, parts):
    rows, d = hidden.shape
    grad = jax.ShapeDtypeStruct(w[0].shape, BF16)
    return pl.pallas_call(
        project_back_kernel,
        in_specs=[pl.BlockSpec(memory_space=pltpu.SMEM)] + in_vmem(10),
        out_shape=[
            jax.ShapeDtypeStruct(context.shape, BF16),
            grad,
            grad,
            jax.ShapeDtypeStruct((rows, d), F32),
            jax.ShapeDtypeStruct((1, d), F32),
        ],
        compiler_params=params(),
        cost_estimate=NO_COST,
        name="project_back",
    )(at, context, w[0], w[1], hidden, gain, dy, *parts)


def qkv_back_kernel(head, *refs):
    grads, xa, w = refs[:2], refs[2:6], refs[6:8]
    cosine, sine, q_gain, k_gain, a_gain = refs[8:13]
    d_xa, (keep, send, parts, a_part) = refs[13:17], refs[17:]
    n = keep.shape[1]
    width = 2 * head
    cols = w[0].shape[-1]

    def back(g, v, gain, i):
        e = g * cosine[i] - swap_halves(g, head) * sine[i]
        m = lax.rsqrt(head_sums(v * v, head) * (1.0 / head) + EPSILON)
        u = gain * e
        mean = head_sums(u * v, head) * (1.0 / head)
        return m * u - v * (m * m * m * mean), jnp.sum(e * v * m, axis=0, keepdims=True)

    lows = []
    q_sum = k_sum = 0.0
    for slot in (0, 1):
        for i in range(4):
            v, g = project_qkv(xa[i], w, slot, n), grads[slot][i].astype(F32)
            d_q, part = back(g[:, :width], v[:, :width], q_gain[...], i)
            q_sum += part
            d_k, part = back(g[:, width:], v[:, width:], k_gain[...], i)
            k_sum += part
            d_kv = jnp.where(lanes_of(d_k.shape) < head, d_k, g[:, width:])
            lows.append(jnp.concatenate([d_q, d_kv], axis=1).astype(BF16))
    for e in range(4):
        at = slice(e * cols, (e + 1) * cols)
        to = slice((e // 2) * cols, (e // 2 + 1) * cols)
        total = 0.0
        for i in range(4):
            here = nn(lows[i], piece(w, 0, e)[:n]) + nn(lows[4 + i], piece(w, 1, e)[:n])
            d_xa[i][:, at] = here.astype(BF16)
            total += jnp.sum(here * xa[i][:, at].astype(F32), axis=0, keepdims=True)
        a_part[:, at] = total / a_gain[:, at]
        for slot in (0, 1):
            here = sum(tn(lows[slot * 4 + i], xa[i][:, at]) for i in range(4))
            (keep, send)[e % 2][slot, :, to] = here.astype(BF16)
    parts[0:1] = q_sum
    parts[1:2] = k_sum


def qkv_back_call(grads, xa, w, cosine, sine, gains, head):
    rows, d = xa[0].shape
    n = w[1].shape[1]
    half = jax.ShapeDtypeStruct((2, n, d // 2), BF16)
    return pl.pallas_call(
        functools.partial(qkv_back_kernel, head),
        out_shape=[jax.ShapeDtypeStruct((rows, d), BF16)] * 4
        + [half, half]
        + [jax.ShapeDtypeStruct((2, 2 * head), F32), jax.ShapeDtypeStruct((1, d), F32)],
        compiler_params=params(),
        cost_estimate=NO_COST,
        name="qkv_back",
    )(*grads, *xa, *w, cosine, sine, *gains)


def ffn_kernel(count, *refs):
    xf, dy, w = refs[:count], refs[count : 2 * count], refs[2 * count : 2 * count + 16]
    refs = refs[2 * count + 16 :]
    cols = w[0].shape[-1]

    def piece(slot, e, which):
        return w[e][which] if slot == 0 else w[4 + 4 * which + e][...]

    def wide(v, slot, which):
        return sum(nt(v[:, e * cols : (e + 1) * cols], piece(slot, e, which)) for e in range(4))

    for i in range(count):
        acts, out, d_xf = refs[3 * i : 3 * i + 3]
        for slot in (0, 1):
            gate, up = wide(xf[i], slot, 0), wide(xf[i], slot, 1)
            d_act = wide(dy[i], slot, 2).astype(BF16).astype(F32)
            sig = 1.0 / (1.0 + jnp.exp(-gate))
            silu = gate * sig
            acts[2, slot] = (silu * up).astype(BF16)
            acts[0, slot] = (d_act * up * (sig * (1.0 + gate * (1.0 - sig)))).astype(BF16)
            acts[1, slot] = (d_act * silu).astype(BF16)
        for e in range(4):
            at = slice(e * cols, (e + 1) * cols)
            d_xf[:, at] = sum(
                nn(acts[k, slot], piece(slot, e, k)) for slot in (0, 1) for k in (0, 1)
            ).astype(BF16)
        for e in range(4):
            at = slice(e * cols, (e + 1) * cols)
            out[:, at] = sum(nn(acts[2, slot], piece(slot, e, 2)) for slot in (0, 1)).astype(BF16)


def ffn_call(xf, dy, w):
    count, (rows, d) = len(xf), xf[0].shape
    units = w[0].shape[1]
    tokens = jax.ShapeDtypeStruct((rows, d), BF16)
    return pl.pallas_call(
        functools.partial(ffn_kernel, count),
        out_shape=[jax.ShapeDtypeStruct((3, 2, rows, units), BF16), tokens, tokens] * count,
        compiler_params=params(),
        cost_estimate=NO_COST,
        name="ffn",
    )(*xf, *dy, *w)


def ffn_grad_kernel(*refs):
    acts, xf, dy = refs[:4], refs[4:8], refs[8:12]
    keep, send = refs[12:]
    cols = keep.shape[-1] // 2

    def write(right):
        for e in range(4):
            at = slice(e * cols, (e + 1) * cols)
            here = sum(tn(acts[b][0, 0], right[b][:, at]) for b in range(4)).astype(BF16)
            to = slice((e // 2) * cols, (e // 2 + 1) * cols)
            (keep, send)[e % 2][0, :, to] = here

    pl.when(pl.program_id(0) < 2)(lambda: write(xf))
    pl.when(pl.program_id(0) == 2)(lambda: write(dy))


def ffn_grad_call(acts, xf, dy, slot):
    three, _, rows, units = acts[0].shape
    d = xf[0].shape[1]
    by_kind = pl.BlockSpec((1, 1, rows, units), lambda k: (k, slot, 0, 0))
    half = pl.BlockSpec((1, units, d // 2), lambda k: (k, 0, 0))
    out = jax.ShapeDtypeStruct((three, units, d // 2), BF16)
    return pl.pallas_call(
        ffn_grad_kernel,
        grid=(three,),
        in_specs=[by_kind] * 4 + [pl.BlockSpec((rows, d), lambda k: (0, 0))] * 8,
        out_specs=[half, half],
        out_shape=[out, out],
        compiler_params=params(),
        cost_estimate=NO_COST,
        name="ffn_grad",
    )(*acts, *xf, *dy)


def norm_factor(v):
    return lax.rsqrt(jnp.mean(v * v, axis=-1, keepdims=True) + EPSILON)


def norm_back(v, factor, gain, grad):
    u = gain * grad
    part = jnp.sum(grad * v * factor, axis=0)
    mean = jnp.mean(u * v, axis=-1, keepdims=True)
    return factor * u - v * (factor * factor * factor * mean), part


def per_device(
    tokens,
    segment_ids,
    cotangent,
    attn_gain,
    query_weight,
    key_weight,
    value_weight,
    output_weight,
    query_gain,
    key_gain,
    ffn_gain,
    gate_weight,
    up_weight,
    down_weight,
):
    y, c, zh = lax.axis_index("y"), lax.axis_index("c"), lax.axis_index("zh")
    near = lax.axis_index(NEAR)
    head = query_gain.shape[0]
    rows = tokens.shape[0]
    nq, nk = query_weight.shape[1], key_weight.shape[1]
    n = nq + 2 * nk

    x = own_order(tokens, y, c).astype(F32)
    gain_a = own_order(attn_gain[None], y, c)
    gain_f = own_order(ffn_gain[None], y, c)
    gain_q = jnp.concatenate([query_gain, query_gain])[None]
    gain_k = jnp.concatenate([key_gain, key_gain])[None]
    x_factor = norm_factor(x)
    xa = (x * x_factor * gain_a).astype(BF16)
    shard = gather_runs(
        jnp.concatenate([query_weight.T, key_weight.T, value_weight.T, output_weight], axis=0)
    )
    ffn_own = gather_runs(jnp.stack([gate_weight.T, up_weight.T, down_weight]))
    xa_near = [xa, swap(xa, NEAR, 1), swap(xa, NEAR, 2)]
    shard_far = swap(shard, "zh", 1)
    heads = jnp.stack([shard, shard_far, swap(shard, "y", 1), swap(shard_far, "y", 1)])
    qkv_w = (heads, swap(heads[:, :n], "c", 1))
    gate_far = swap(ffn_own[0], "zh", 1)
    (xa_near, ffn_own), gate_far, qkv_w = after((xa_near, ffn_own), gate_far, qkv_w)
    xa_near.append(swap(xa_near[2], NEAR, 1))
    up_far = swap(ffn_own[1], "zh", 1)
    (ffn_own, xa_near, gate_far, qkv_w), up_far = after((ffn_own, xa_near, gate_far, qkv_w), up_far)

    segment = segment_ids[0]
    total_rows = segment.shape[0]
    index = jnp.arange(total_rows, dtype=jnp.int32)
    opens = jnp.concatenate([jnp.ones((1,), dtype=jnp.bool_), segment[1:] != segment[:-1]])
    begin = lax.cummax(jnp.where(opens, index, 0), axis=0)
    blocks = total_rows // BLOCK
    first = begin[::BLOCK] // BLOCK
    by_block = begin.reshape(blocks, 1, BLOCK)
    start = jnp.concatenate([by_block, by_block], axis=2)
    four = jnp.arange(4, dtype=jnp.int32) ^ near
    position = lax.dynamic_slice_in_dim(index - begin, zh * 4 * rows, 4 * rows).astype(F32)
    inverse = ROPE_BASE ** (-(jnp.arange(head // 2, dtype=F32) * 2.0) / head)
    angle = (position[:, None] * inverse[None, :]).reshape(4, rows, head // 2)[four]
    cos_half, sin_half = jnp.cos(angle), jnp.sin(angle)
    cosine = jnp.concatenate([cos_half] * 4, axis=2)
    sine = jnp.concatenate([-sin_half, sin_half] * 2, axis=2)
    eight = jnp.arange(8, dtype=jnp.int32)
    places = jnp.concatenate([zh * 4 + four, (1 - zh) * 4 + four]).astype(jnp.int32)

    other = qkv_call(xa_near, qkv_w, 1, cosine, sine, gain_q, gain_k, head)
    (cotangent, ffn_own, gate_far, up_far), other = after(
        (cotangent, ffn_own, gate_far, up_far), other
    )
    dy = own_order(cotangent, y, c)
    got = swap(other, "zh", 1)
    dy_near = [dy, swap(dy, NEAR, 1), swap(dy, NEAR, 2)]
    own_y = swap(ffn_own, "y", 1)
    own = qkv_call(xa_near, qkv_w, 0, cosine, sine, gain_q, gain_k, head)
    (dy_near, ffn_own, gate_far, up_far, heads), own, got, own_y = after(
        (dy_near, ffn_own, gate_far, up_far, qkv_w[0]), own, got, own_y
    )

    context, log_total, qkv = attend_call(first, places, (own, got), start, head)
    down_far = swap(ffn_own[2], "zh", 1)
    out_w = jnp.concatenate([heads[:2, n:], heads[2:, n:]], axis=-1)
    out_w = [out_w] + [swap(out_w, NEAR, bit) for bit in (1, 2, 3)]
    gate_y = swap(gate_far, "y", 1)
    (dy_near, ffn_own, own_y, gate_far, up_far), context, down_far, gate_y, out_w = after(
        (dy_near, ffn_own, own_y, gate_far, up_far), context, down_far, gate_y, out_w
    )

    def to_heads(v):
        return lax.all_to_all(v, TENSOR, 0, 0, tiled=True)

    context_rows = to_heads(context.reshape(-1, rows, nq))
    dy_near.append(swap(dy_near[2], NEAR, 1))
    up_y, down_y = swap(up_far, "y", 1), swap(down_far, "y", 1)
    out_w = jnp.stack(out_w)
    out_w = [v.reshape((8,) + v.shape[2:]) for v in (out_w, swap(out_w, "c", 1))]
    w = [ffn_own, own_y, gate_far, gate_y, up_far, up_y, down_far, down_y]
    own_c, own_yc = swap(ffn_own, "c", 1), swap(own_y, "c", 1)
    w, context_rows, dy_near, own_c, own_yc, out_w = after(
        w, context_rows, dy_near, own_c, own_yc, out_w
    )

    hidden, xf = project_call(places, context_rows, out_w, x, gain_f)
    ffn_w = [w[0], own_c, w[1], own_yc]
    for k in (0, 1, 2):
        far, far_y = w[2 + 2 * k : 4 + 2 * k]
        ffn_w += [far, swap(far, "c", 1), far_y, swap(far_y, "c", 1)]

    xf_near = [xf] + [swap(xf, NEAR, bit) for bit in (1, 2, 3)]
    acts_0, out_0, d_xf_0 = ffn_call(xf_near[:1], dy_near[:1], ffn_w)
    acts_1, out_1, d_xf_1, acts_2, out_2, d_xf_2 = ffn_call(xf_near[1:3], dy_near[1:3], ffn_w)
    acts_3, out_3, d_xf_3 = ffn_call(xf_near[3:], dy_near[3:], ffn_w)
    d_xf = [d_xf_0, swap(d_xf_1, NEAR, 1), swap(d_xf_2, NEAR, 2), swap(d_xf_3, NEAR, 3)]
    acts = [acts_0, acts_1, acts_2, acts_3]
    keep_1, send_1 = ffn_grad_call(acts, xf_near, dy_near, 1)
    keep_0, send_0 = ffn_grad_call(acts, xf_near, dy_near, 0)
    (out_0, out_1, out_2, out_3), d_xf, keep_1, send_1, keep_0, send_0 = after(
        (out_0, out_1, out_2, out_3), d_xf, keep_1, send_1, keep_0, send_0
    )

    d_context_rows, out_keep, out_send, d_hidden, ffn_gain_part = project_back_call(
        places, context_rows, out_w, hidden, gain_f, dy, d_xf
    )
    d_context = to_heads(d_context_rows).reshape(total_rows, nq)
    ffn_1 = add_swapped(keep_1, send_1, "c", 1).astype(BF16)
    gate_1 = add_swapped(*halves(ffn_1[0]), "y", 1).astype(BF16)
    out_grad = add_swapped(out_keep, out_send, "c", 1).astype(BF16)
    (out_1, out_2, out_3, keep_0, ffn_1), d_context, gate_1, out_grad = after(
        (out_1, out_2, out_3, keep_0, ffn_1), d_context, gate_1, out_grad
    )

    place = jnp.where(eight // 4 == zh, 4, 0) + ((eight % 4) ^ near)
    d_qkv = attend_back_call(
        first, place.astype(jnp.int32), qkv, context, d_context, start, log_total, head
    )
    up_1 = add_swapped(*halves(ffn_1[1]), "y", 1).astype(BF16)
    gate_part = swap(gate_1, "zh", 1)
    ffn_out = [out_0, swap(out_1, NEAR, 1), swap(out_2, NEAR, 2)]
    (ffn_1, out_3, out_grad, keep_0), d_qkv, up_1, gate_part, *ffn_out = after(
        (ffn_1, out_3, out_grad, keep_0), d_qkv, up_1, gate_part, *ffn_out
    )

    got = swap(d_qkv[:4], "zh", 1)
    ffn_0 = add_swapped(keep_0, send_0, "c", 1).astype(BF16)
    out_grad = out_grad.reshape((4, 2) + out_grad.shape[1:])
    out_grad = out_grad[0].astype(F32) + sum(
        swap(out_grad[bit], NEAR, bit).astype(F32) for bit in (1, 2, 3)
    )
    (ffn_1, up_1, out_3, d_qkv), got, ffn_0, out_grad = after(
        (ffn_1, up_1, out_3, d_qkv), got, ffn_0, out_grad.astype(BF16)
    )

    gains = (gain_q, gain_k, gain_a)
    xa = [xa_near[b] for b in (3, 1)]
    *d_xa, qkv_keep, qkv_send, head_parts, attn_gain_part = qkv_back_call(
        (d_qkv[4:], got), xa_near, qkv_w, cosine, sine, gains, head
    )
    out_grad = add_swapped(*halves(out_grad), "y", 1)
    down_1 = add_swapped(*halves(ffn_1[2]), "y", 1).astype(BF16)
    up_down = jnp.stack([up_1, down_1])
    (up_down, ffn_0, out_3), d_xa, qkv_send, out_grad, attn_gain_part = after(
        (up_down, ffn_0, out_3), d_xa, qkv_send, out_grad, attn_gain_part
    )

    d_xa = [d_xa[0]] + [swap(d_xa[bit], NEAR, bit) for bit in (1, 2, 3)]
    qkv_grad = add_swapped(qkv_keep, qkv_send, "c", 1).astype(BF16)
    qkv_grad = add_swapped(*halves(qkv_grad), "y", 1)
    ffn_0, qkv_grad = after(ffn_0, qkv_grad)
    up_down = swap(up_down, "zh", 1)
    ffn_0 = add_swapped(*halves(ffn_0), "y", 1)
    (out_grad, out_3, attn_gain_part), d_xa, up_down, qkv_grad, ffn_0 = after(
        (out_grad, out_3, attn_gain_part), d_xa, up_down, qkv_grad, ffn_0
    )

    heads_grad = jnp.concatenate([qkv_grad, out_grad], axis=1)
    heads_grad = add_swapped(heads_grad[0], heads_grad[1].astype(BF16), "zh", 1)
    qkv_grad, out_grad = heads_grad[:n], heads_grad[n:]
    ffn_out.append(swap(out_3, NEAR, 3))
    d = x.shape[1]
    gains = total_of(
        jnp.concatenate(
            [
                arrays_order(attn_gain_part, y, c)[0],
                arrays_order(ffn_gain_part, y, c)[0],
                head_parts[0, :head] + head_parts[0, head:],
                head_parts[1, :head],
            ]
        ).reshape(-1, 128)
    ).reshape(-1)
    d_xa = sum(v.astype(F32) for v in d_xa)
    x_back, _ = norm_back(x, x_factor, gain_a, d_xa)
    input_grad = arrays_order((d_hidden + x_back).astype(BF16), y, c)
    block_out = arrays_order((hidden + sum(v.astype(F32) for v in ffn_out)).astype(BF16), y, c)
    qkv_grad = scatter_runs(qkv_grad)
    out_grad = scatter_runs(out_grad)
    ffn_grad = [
        scatter_runs(ffn_0[k] + part.astype(F32))
        for k, part in enumerate((gate_part, up_down[0], up_down[1]))
    ]

    return (
        block_out,
        input_grad,
        gains[:d],
        qkv_grad[:nq].T,
        qkv_grad[nq : nq + nk].T,
        qkv_grad[nq + nk :].T,
        out_grad,
        gains[2 * d : 2 * d + head],
        gains[2 * d + head :],
        gains[d : 2 * d],
        ffn_grad[0].T,
        ffn_grad[1].T,
        ffn_grad[2],
    )


def solution(mesh):
    dp, tensor = mesh.shape["dp"], mesh.shape["tensor"]
    cut = Mesh(
        mesh.devices.reshape(dp // 4, 2, 2, tensor // 4, 2, 2), ("r", "y", "c", "zh", "zl", "x")
    )
    data, model = ("r", "y", "c"), TENSOR
    both = data + model
    rows, wide, tall = P(both, None), P(data, model), P(model, data)
    in_specs = (
        rows, P(data, None), rows, P(), wide, wide, wide, tall, P(), P(), P(), wide, wide, tall
    )
    out_specs = (
        rows, rows, P(), wide, wide, wide, tall, P(), P(), P(), wide, wide, tall
    )
    return jax.shard_map(
        per_device, mesh=cut, in_specs=in_specs, out_specs=out_specs, check_vma=False
    )
```
